32 devices in a mesh: dp: 8 (over z, x), section: 4 (over y, core).
Axes of the slice: x: 2, y: 2, z: 4, core: 2. Of those that a mesh axis runs over, the one named last changes fastest.
Arguments:
- inputs: bfloat16 [32, 248, 768], P('dp'), may hold values from -6 to 6
- out_grad: bfloat16 [32, 248, 768], P('dp'), may hold values from -6 to 6
- segment_ids: int32 [32, 248], P('dp'), may hold values from 0 to 3, never falling along the last dimension, each value on 1 to 124 neighbouring positions
- cls_index: int32 [32], P('dp'), may hold values from 0 to 247
- qkv_master: float32 [4, 768, 2304], P('section', 'dp'), may hold values from -0.21875 to 0.21875
- proj_master: float32 [4, 768, 768], P('section', 'dp'), may hold values from -0.875 to 0.875
- up_master: float32 [4, 768, 3072], P('section', 'dp'), may hold values from -0.21875 to 0.21875
- down_master: float32 [4, 3072, 768], P('section', 'dp'), may hold values from -0.109375 to 0.109375
- small_master: float32 [4, 9216], P('section', 'dp'), may hold values from -0.4 to 1.4, as said below
- qkv_first: float32 [4, 768, 2304], P('section', 'dp'), may hold values from -0.0012207031 to 0.0012207031
- proj_first: float32 [4, 768, 768], P('section', 'dp'), may hold values from -0.0012207031 to 0.0012207031
- up_first: float32 [4, 768, 3072], P('section', 'dp'), may hold values from -0.0012207031 to 0.0012207031
- down_first: float32 [4, 3072, 768], P('section', 'dp'), may hold values from -0.0012207031 to 0.0012207031
- small_first: float32 [4, 9216], P('section', 'dp'), may hold values from -0.0024414062 to 0.0024414062
- qkv_second: float32 [4, 768, 2304], P('section', 'dp'), may hold values from 3.5275338e-08 to 1.4110135e-07
- proj_second: float32 [4, 768, 768], P('section', 'dp'), may hold values from 3.5275338e-08 to 1.4110135e-07
- up_second: float32 [4, 768, 3072], P('section', 'dp'), may hold values from 3.5275338e-08 to 1.4110135e-07
- down_second: float32 [4, 3072, 768], P('section', 'dp'), may hold values from 3.5275338e-08 to 1.4110135e-07
- small_second: float32 [4, 9216], P('section', 'dp'), may hold values from 1.4110135e-07 to 5.644054e-07
Outputs:
- acts: bfloat16 [4, 32, 248, 768], P('section', 'dp')
- input_grads: bfloat16 [4, 32, 248, 768], P('section', 'dp')
- grad_norm: float32 [1], replicated
- qkv_grad: float32 [4, 768, 2304], P('section', 'dp')
- qkv_master_new: float32 [4, 768, 2304], P('section', 'dp')
- qkv_first_new: float32 [4, 768, 2304], P('section', 'dp')
- qkv_second_new: float32 [4, 768, 2304], P('section', 'dp')
- proj_grad: float32 [4, 768, 768], P('section', 'dp')
- proj_master_new: float32 [4, 768, 768], P('section', 'dp')
- proj_first_new: float32 [4, 768, 768], P('section', 'dp')
- proj_second_new: float32 [4, 768, 768], P('section', 'dp')
- up_grad: float32 [4, 768, 3072], P('section', 'dp')
- up_master_new: float32 [4, 768, 3072], P('section', 'dp')
- up_first_new: float32 [4, 768, 3072], P('section', 'dp')
- up_second_new: float32 [4, 768, 3072], P('section', 'dp')
- down_grad: float32 [4, 3072, 768], P('section', 'dp')
- down_master_new: float32 [4, 3072, 768], P('section', 'dp')
- down_first_new: float32 [4, 3072, 768], P('section', 'dp')
- down_second_new: float32 [4, 3072, 768], P('section', 'dp')
- small_grad: float32 [4, 9216], P('section', 'dp')
- small_master_new: float32 [4, 9216], P('section', 'dp')
- small_first_new: float32 [4, 9216], P('section', 'dp')
- small_second_new: float32 [4, 9216], P('section', 'dp')
The draws below stay inside these ranges and needn't reach their ends.
Inputs may be any that keep to these rules, and one draw needn't show every extreme that they name: `segment_ids`: clip numbers never fall along a sequence; each clip covers 1 to 124 patches, and one covers exactly 124. `small_master`: gains lie near one, biases near zero.
All inputs are finite; a program needn't handle non-finite values.
Results may differ from the reference program's by a relative error of at most 0.018.
Values may be sent and summed in bfloat16 or wider, within the bound.
A program may use at most 768 MiB of HBM per device.

```python
import math
import jax
import jax.numpy as jnp
import numpy as np
from jax import lax

D = 768
HEADS = 12
FF = 3072
SEQ_LEN = 248
CLIPS = 4
STEP = 3
SEG_MOST = 124
LAYERS = 4
SEQS = 32
SMALL = 9216
SLICES = 8


def draw_small_master(key, part):
    first_key, second_key, third_key = jax.random.split(jax.random.fold_in(key, 11), 3)
    gains = 1.0 + 0.1 * jnp.clip(jax.random.normal(first_key, (LAYERS, 2, D), jnp.float32), -4.0, 4.0)
    shifts = 0.1 * jnp.clip(jax.random.normal(second_key, (LAYERS, 6, D), jnp.float32), -4.0, 4.0)
    up_shift = 0.1 * jnp.clip(jax.random.normal(third_key, (LAYERS, FF), jnp.float32), -4.0, 4.0)
    ordered = jnp.stack([gains[:, 0], shifts[:, 0], shifts[:, 1], shifts[:, 2], shifts[:, 3], gains[:, 1], shifts[:, 4], shifts[:, 5]], axis=1)
    ordered = ordered.reshape(LAYERS, 8, SLICES, D // SLICES).transpose(0, 2, 1, 3).reshape(LAYERS, SLICES, 8 * (D // SLICES))
    up_sliced = up_shift.reshape(LAYERS, SLICES, FF // SLICES)
    return jnp.concatenate([ordered, up_sliced], axis=2).reshape(LAYERS, SMALL)


def place_ends(drawn, stream_key, least, top_value):
    dims = drawn.shape
    index_at = [jax.random.randint(jax.random.fold_in(stream_key, axis), (), 0, dims[axis]) for axis in range(len(dims))]
    drawn = drawn.at[tuple(index_at)].set(least)
    longest = dims.index(max(dims))
    index_at[longest] = (index_at[longest] + 1) % dims[longest]
    return drawn.at[tuple(index_at)].set(top_value)


def level_of(stream_key, shape, shards, least, largest):
    level = 1.0
    for position, shards_of in shards:
        draws = jax.random.uniform(jax.random.fold_in(jax.random.fold_in(stream_key, 6), position), (shards_of,), jnp.float32, least / len(shards), largest / len(shards))
        level = level * jnp.repeat(jnp.exp(draws), shape[position] // shards_of).reshape((-1,) + (1,) * (len(shape) - 1 - position))
    return level


def length_profile(count, total, limit, slope):
    portions = [(1 << 20) // math.isqrt(rank ** slope) + 1 for rank in range(2, count + 1)]
    spare, counts = total - limit - (count - 1), [1] * (count - 1)
    while spare > 0:
        free = [i for i in range(count - 1) if counts[i] < limit]
        pool, remaining = sum([portions[i] for i in free]), spare
        for i in free:
            more = min(limit - counts[i], max(1, remaining * portions[i] // pool), spare)
            counts[i] = counts[i] + more
            spare = spare - more
    return np.array([limit] + counts)


def ragged_sizes(stream_key, amount, total, limit, slope):
    if amount == 2:
        one = jax.random.randint(stream_key, (), max(1, total - limit), min(limit, total - 1) + 1)
        return jnp.stack([one, total - one])
    tallies = jnp.asarray(length_profile(amount, total, limit, slope), jnp.int32)
    couples = (amount - 1) // 2
    donor, sink = tallies[1:1 + 2 * couples:2], tallies[2:2 + 2 * couples:2]
    room = jnp.minimum(donor - 1, limit - sink)
    passed = jax.random.randint(jax.random.fold_in(stream_key, 1), (couples,), 0, 1 << 20) % (room + 1)
    tallies = tallies.at[1:1 + 2 * couples:2].set(donor - passed).at[2:2 + 2 * couples:2].set(sink + passed)
    return tallies[jax.random.permutation(jax.random.fold_in(stream_key, 2), amount)]


def gaussian(key, shape, deviation, reach, cuts=(), held_as=jnp.bfloat16):
    level = level_of(key, shape, cuts, -0.22, 0.18) if cuts else 1.0
    values = jax.random.normal(key, shape, jnp.float32) * deviation * level
    return jnp.minimum(jnp.maximum(values, -reach), reach).astype(held_as)


def setup_inputs(seed: int = 0) -> dict:
    arg_keys = jax.random.split(jax.random.key(seed), 20)
    inputs = gaussian(arg_keys[0], (SEQS, SEQ_LEN, D), 1.0, 6.0, ((0, 8),))
    out_grad = gaussian(arg_keys[1], (SEQS, SEQ_LEN, D), 1.0, 6.0, ((0, 8),))
    segment_ids = jax.vmap(lambda own: jnp.searchsorted(jnp.cumsum(ragged_sizes(own, CLIPS, SEQ_LEN, SEG_MOST, 0)), jnp.arange(SEQ_LEN), side="right"))(jax.random.split(arg_keys[2], SEQS)).reshape((SEQS, SEQ_LEN)).astype(jnp.int32)
    cls_index = place_ends(jax.random.randint(arg_keys[3], (SEQS,), 0, SEQ_LEN), jax.random.fold_in(arg_keys[3], 1), 0, SEQ_LEN - 1).astype(jnp.int32)
    qkv_master = gaussian(arg_keys[4], (LAYERS, D, 3 * D), D ** -0.5, 0.21875, ((0, 4), (1, 8)), jnp.float32)
    proj_master = gaussian(arg_keys[5], (LAYERS, D, D), (D // 16) ** -0.5, 0.875, ((0, 4), (1, 8)), jnp.float32)
    up_master = gaussian(arg_keys[6], (LAYERS, D, FF), D ** -0.5, 0.21875, ((0, 4), (1, 8)), jnp.float32)
    down_master = gaussian(arg_keys[7], (LAYERS, FF, D), FF ** -0.5, 0.109375, ((0, 4), (1, 8)), jnp.float32)
    small_master = draw_small_master(jax.random.fold_in(arg_keys[19], 71), 0)
    qkv_first = gaussian(arg_keys[9], (LAYERS, D, 3 * D), ((LAYERS * (4 * D * D + 2 * D * FF + SMALL)) ** -0.5), 0.0012207031, ((0, 4), (1, 8)), jnp.float32)
    proj_first = gaussian(arg_keys[10], (LAYERS, D, D), ((LAYERS * (4 * D * D + 2 * D * FF + SMALL)) ** -0.5), 0.0012207031, ((0, 4), (1, 8)), jnp.float32)
    up_first = gaussian(arg_keys[11], (LAYERS, D, FF), ((LAYERS * (4 * D * D + 2 * D * FF + SMALL)) ** -0.5), 0.0012207031, ((0, 4), (1, 8)), jnp.float32)
    down_first = gaussian(arg_keys[12], (LAYERS, FF, D), ((LAYERS * (4 * D * D + 2 * D * FF + SMALL)) ** -0.5), 0.0012207031, ((0, 4), (1, 8)), jnp.float32)
    small_first = gaussian(arg_keys[13], (LAYERS, SMALL), (2 * (LAYERS * (4 * D * D + 2 * D * FF + SMALL)) ** -0.5), 0.0024414062, ((0, 4), (1, 8)), jnp.float32)
    qkv_second = jnp.clip(jnp.exp(math.log(1.411013528240801e-07) - 1.3862944 * jax.random.uniform(arg_keys[14], (LAYERS, D, 3 * D), jnp.float32) ** level_of(arg_keys[14], (LAYERS, D, 3 * D), ((0, 4), (1, 8)), -0.2, 0.2)), 3.5275338206020024e-08, 1.411013528240801e-07)
    proj_second = jnp.clip(jnp.exp(math.log(1.411013528240801e-07) - 1.3862944 * jax.random.uniform(arg_keys[15], (LAYERS, D, D), jnp.float32) ** level_of(arg_keys[15], (LAYERS, D, D), ((0, 4), (1, 8)), -0.2, 0.2)), 3.5275338206020024e-08, 1.411013528240801e-07)
    up_second = jnp.clip(jnp.exp(math.log(1.411013528240801e-07) - 1.3862944 * jax.random.uniform(arg_keys[16], (LAYERS, D, FF), jnp.float32) ** level_of(arg_keys[16], (LAYERS, D, FF), ((0, 4), (1, 8)), -0.2, 0.2)), 3.5275338206020024e-08, 1.411013528240801e-07)
    down_second = jnp.clip(jnp.exp(math.log(1.411013528240801e-07) - 1.3862944 * jax.random.uniform(arg_keys[17], (LAYERS, FF, D), jnp.float32) ** level_of(arg_keys[17], (LAYERS, FF, D), ((0, 4), (1, 8)), -0.2, 0.2)), 3.5275338206020024e-08, 1.411013528240801e-07)
    small_second = jnp.clip(jnp.exp(math.log(5.644054112963204e-07) - 1.3862944 * jax.random.uniform(arg_keys[18], (LAYERS, SMALL), jnp.float32) ** level_of(arg_keys[18], (LAYERS, SMALL), ((0, 4), (1, 8)), -0.2, 0.2)), 1.411013528240801e-07, 5.644054112963204e-07)
    return {"inputs": inputs, "out_grad": out_grad, "segment_ids": segment_ids, "cls_index": cls_index, "qkv_master": qkv_master, "proj_master": proj_master, "up_master": up_master, "down_master": down_master, "small_master": small_master, "qkv_first": qkv_first, "proj_first": proj_first, "up_first": up_first, "down_first": down_first, "small_first": small_first, "qkv_second": qkv_second, "proj_second": proj_second, "up_second": up_second, "down_second": down_second, "small_second": small_second}


@jax.custom_vjp
def low(v):
    return lax.optimization_barrier(v.astype(jnp.bfloat16)).astype(jnp.float32)

@jax.custom_vjp
def low_back(v):
    return v

def low_keep(v):
    return (low(v), None)

def low_pass(kept, grad):
    return (grad,)

def back_keep(v):
    return (v, None)

def back_low(kept, grad):
    return (low(grad),)
low.defvjp(low_keep, low_pass)
low_back.defvjp(back_keep, back_low)
norm_eps = 1e-06
masked_score = -1e+30
learn_rate = 0.05
small_rate = 0.3
decay_rate = 0.05
adam_eps = 1e-08

def layer_norm(values):
    center = values - lax.optimization_barrier(jnp.mean(values, axis=-1, keepdims=True))
    spread = lax.optimization_barrier(jnp.mean(center * center, axis=-1, keepdims=True))
    return center * lax.rsqrt(spread + norm_eps)

def norm_affine(values, gain, shift):
    return layer_norm(values) * gain + shift

def split_small(small, width, hidden_width, slices):
    share = width // slices
    stacked = small.reshape(slices, small.shape[0] // slices)
    pieces = [stacked[:, place * share:(place + 1) * share].reshape(width) for place in range(8)]
    pieces.append(stacked[:, 8 * share:].reshape(hidden_width))
    return pieces

def allowed_pairs(segment_ids, cls_rows):
    length = segment_ids.shape[1]
    places = lax.broadcasted_iota(jnp.int32, (1, length), 1)
    is_cls = places == cls_rows[:, None]
    same = segment_ids[:, :, None] == segment_ids[:, None, :]
    allowed = same | is_cls[:, :, None] | is_cls[:, None, :]
    return allowed[:, None, :, :]

def block_forward(inputs, segment_ids, cls_rows, weights):
    w_qkv, w_proj, w_up, w_down, small = weights
    count, length, width = inputs.shape
    hidden_width = w_up.shape[1]
    head_size = width // HEADS
    parts = split_small(small, width, hidden_width, SLICES)
    highest = lax.Precision.HIGHEST
    normed = low(norm_affine(inputs, parts[0], parts[1]))
    mixed = jnp.einsum('nld,de->nle', normed, w_qkv, precision=highest)
    query = low_back(low(mixed[..., :width] + parts[2]))
    keys = low_back(low(mixed[..., width:2 * width]))
    values = low_back(low(mixed[..., 2 * width:] + parts[3]))
    shape_heads = (count, length, HEADS, head_size)
    scores = jnp.einsum('nqhd,nkhd->nhqk', query.reshape(shape_heads), keys.reshape(shape_heads), precision=highest)
    scores = low_back(scores * head_size ** (-0.5))
    scores = jnp.where(allowed_pairs(segment_ids, cls_rows), scores, masked_score)
    peak = lax.optimization_barrier(jnp.max(scores, axis=-1, keepdims=True))
    raised = jnp.exp(scores - peak)
    probs = low(raised / lax.optimization_barrier(jnp.sum(raised, axis=-1, keepdims=True)))
    attended = jnp.einsum('nhqk,nkhd->nqhd', probs, values.reshape(shape_heads), precision=highest)
    attended = low_back(low(attended.reshape(count, length, width)))
    branch = low_back(jnp.einsum('nld,de->nle', attended, w_proj, precision=highest) + parts[4])
    hidden = inputs + branch
    normed_two = low(norm_affine(hidden, parts[5], parts[6]))
    inner = low_back(jnp.einsum('nld,df->nlf', normed_two, w_up, precision=highest) + parts[8])
    active = low(jax.nn.gelu(inner, approximate=False))
    return hidden + low_back(jnp.einsum('nlf,fd->nld', active, w_down, precision=highest) + parts[7])

def reference(inputs, out_grad, segment_ids, cls_index, qkv_master, proj_master, up_master, down_master, small_master, qkv_first, proj_first, up_first, down_first, small_first, qkv_second, proj_second, up_second, down_second, small_second):
    masters = (qkv_master, proj_master, up_master, down_master, small_master)
    firsts = (qkv_first, proj_first, up_first, down_first, small_first)
    seconds = (qkv_second, proj_second, up_second, down_second, small_second)
    group = math.gcd(SEQS, max(1, 4096 // SEQ_LEN))
    start = inputs.astype(jnp.float32)
    offsets = tuple((jnp.zeros(start.shape, jnp.float32) for layer in range(LAYERS)))
    seg_groups = segment_ids.reshape(SEQS // group, group, SEQ_LEN)
    cls_groups = cls_index.reshape(SEQS // group, group)

    def forward(params, shifts):
        current = start
        outputs = []
        for layer in range(LAYERS):
            layer_in = low_back(current + shifts[layer])
            weights = tuple((low(param[layer]) for param in params))
            blocks = layer_in.reshape(SEQS // group, group, SEQ_LEN, D)

            def one(items, weights=weights):
                return block_forward(items[0], items[1], items[2], weights)
            result = lax.map(jax.checkpoint(one), (blocks, seg_groups, cls_groups))
            current = low(result.reshape(SEQS, SEQ_LEN, D))
            outputs.append(current)
        return (current, jnp.stack(outputs))
    top, vjp_fn, stacked = jax.vjp(forward, masters, offsets, has_aux=True)
    grads, offset_grads = vjp_fn(out_grad.astype(jnp.float32))
    total = jnp.sum(jnp.stack([jnp.sum(grad * grad) for grad in grads]))
    grad_norm = jnp.sqrt(total)
    factor = 1.0 / jnp.maximum(grad_norm, 1.0)
    first_fix = 1.0 - 0.5 ** STEP
    second_fix = 1.0 - 0.5 ** STEP
    results = []
    for kind in range(5):
        grad = grads[kind] * factor
        first = 0.5 * firsts[kind] + 0.5 * grad
        second = 0.5 * seconds[kind] + 0.5 * grad * grad
        update = first / first_fix / (jnp.sqrt(second / second_fix) + adam_eps)
        rate = small_rate
        if kind < 4:
            update = update + decay_rate * masters[kind]
            rate = learn_rate
        results += [grad, masters[kind] - rate * update, first, second]
    acts = stacked.astype(jnp.bfloat16)
    input_grads = jnp.stack(offset_grads).astype(jnp.bfloat16)
    return (acts, input_grads, grad_norm.reshape(1), results[0], results[1], results[2], results[3], results[4], results[5], results[6], results[7], results[8], results[9], results[10], results[11], results[12], results[13], results[14], results[15], results[16], results[17], results[18], results[19])
```

```python
import functools

import jax
import jax.numpy as jnp
from jax import lax
from jax.experimental import pallas as pl
from jax.experimental.pallas import tpu as pltpu
from jax.sharding import PartitionSpec as P

HEADS = 12
STEP = 3
F32 = jnp.float32
BF = jnp.bfloat16
MESH = pl.DeviceIdType.MESH
VMEM_CAP = 60 * 1024 * 1024

norm_eps = 1e-06
masked_score = -1e30
learn_rate = 0.05
small_rate = 0.3
decay_rate = 0.05
adam_eps = 1e-08

NT = (((1,), (1,)), ((), ()))


def mm(a, b):
    return jnp.dot(a, b, preferred_element_type=F32)


def mm_nt(a, b):
    return lax.dot_general(a, b, NT, preferred_element_type=F32)


def norm_parts(values):
    center = values - jnp.mean(values, axis=-1, keepdims=True)
    spread = jnp.mean(center * center, axis=-1, keepdims=True)
    inv = lax.rsqrt(spread + norm_eps)
    return center * inv, inv


def norm_back(y, normed, inv):
    pull = jnp.mean(y * normed, axis=-1, keepdims=True)
    return (y - jnp.mean(y, axis=-1, keepdims=True) - normed * pull) * inv


def column_sum(values):
    return jnp.sum(values, axis=0, keepdims=True)


def mask_bias(seg_row, seg_col, cls, length):
    size = seg_col.shape[0]
    key_at = lax.broadcasted_iota(jnp.int32, (size, size), 0)
    query_at = lax.broadcasted_iota(jnp.int32, (size, size), 1)
    allowed = (seg_row == seg_col) | (key_at == cls) | (query_at == cls)
    allowed = allowed & (key_at < length)
    return jnp.where(allowed, 0.0, masked_score).astype(F32)


def gelu_parts(z):
    density = jnp.exp(z * z * -0.5) * 0.3989422804014327
    below = 0.5 + 0.5 * lax.erf(z * 0.7071067811865476)
    return z * below, below + z * density


def layer_forward(x_ref, bias_ref, wqkv, wproj, wup, wdown, small, a_ref, qkv_ref, lse_ref, o_ref,
                  h_ref, a2_ref, gp_ref, u_ref, out_ref, ot_ref, before_up):
    rows, width = x_ref.shape
    hidden = wup.shape[1]
    normed, _ = norm_parts(x_ref[...].astype(F32))
    a_ref[...] = (normed * small[0:1, :] + small[1:2, :]).astype(BF)
    for part in range(3):
        cols = slice(part * width, (part + 1) * width)
        mixed = mm(a_ref[...], wqkv[:, cols])
        if part == 0:
            mixed = mixed + small[2:3, :]
        if part == 2:
            mixed = mixed + small[3:4, :]
        qkv_ref[:, cols] = mixed.astype(BF)
    lane = lax.broadcasted_iota(jnp.int32, (rows, 128), 1)
    for pair in range(HEADS // 2):
        q = qkv_ref[:, pair * 128 : pair * 128 + 128]
        k = qkv_ref[:, width + pair * 128 : width + pair * 128 + 128]
        vt = qkv_ref[:, 2 * width + pair * 128 : 2 * width + pair * 128 + 128].T
        for side in range(2):
            half = (lane < 64) if side == 0 else (lane >= 64)
            k_half = jnp.where(half, k, jnp.zeros_like(k))
            scores = mm_nt(k_half, q) * 0.125 + bias_ref[...]
            peak = jnp.max(scores, axis=0, keepdims=True)
            raised = jnp.exp(scores - peak)
            summed = jnp.sum(raised, axis=0, keepdims=True)
            mixed = mm(vt[side * 64 : side * 64 + 64, :], raised.astype(BF)) * (1.0 / summed)
            at = pair * 128 + side * 64
            ot_ref[at : at + 64, :] = mixed.astype(BF)
            head = 2 * pair + side
            lse_ref[head : head + 1, :] = peak + jnp.log(summed)
    o_ref[...] = ot_ref[...].T
    h = x_ref[...].astype(F32) + (mm(o_ref[...], wproj[...]) + small[4:5, :])
    h_ref[...] = h
    normed, _ = norm_parts(h)
    a2_ref[...] = (normed * small[5:6, :] + small[6:7, :]).astype(BF)
    before_up()
    for part in range(hidden // width):
        cols = slice(part * width, (part + 1) * width)
        z = mm(a2_ref[...], wup[:, cols]) + small[8 + part : 9 + part, :]
        u, slope = gelu_parts(z)
        u_ref[:, cols] = u.astype(BF)
        gp_ref[:, cols] = slope.astype(BF)
    out_ref[...] = (h_ref[...] + (mm(u_ref[...], wdown[...]) + small[7:8, :])).astype(BF)


def layer_backward(g_ref, x_ref, bias_ref, qkv_ref, lse_ref, h_ref, gp_ref, wqkv, wproj, wup, wdown,
                   small, dz_ref, f_ref, r_ref, gin_ref, sums_ref, do_ref, dh_ref, dqt_ref):
    rows, width = x_ref.shape
    hidden = wup.shape[1]
    carried = g_ref[...].astype(F32)
    sums_ref[7:8, :] += column_sum(carried)
    for part in range(hidden // width):
        cols = slice(part * width, (part + 1) * width)
        back = mm_nt(g_ref[...], wdown[cols, :])
        dz = (back * gp_ref[:, cols].astype(F32)).astype(BF)
        dz_ref[:, cols] = dz
        sums_ref[8 + part : 9 + part, :] += column_sum(dz.astype(F32))
    back = mm_nt(dz_ref[...], wup[...])
    normed, inv = norm_parts(h_ref[...])
    sums_ref[5:6, :] += column_sum(back * normed)
    sums_ref[6:7, :] += column_sum(back)
    dh = carried + norm_back(back * small[5:6, :], normed, inv)
    dh_ref[...] = dh
    f = dh.astype(BF)
    f_ref[...] = f
    sums_ref[4:5, :] += column_sum(f.astype(F32))
    do_ref[...] = mm_nt(f_ref[...], wproj[...]).astype(BF)
    lane = lax.broadcasted_iota(jnp.int32, (rows, 128), 1)
    for pair in range(HEADS // 2):
        q = qkv_ref[:, pair * 128 : pair * 128 + 128]
        k = qkv_ref[:, width + pair * 128 : width + pair * 128 + 128]
        v = qkv_ref[:, 2 * width + pair * 128 : 2 * width + pair * 128 + 128]
        do = do_ref[:, pair * 128 : pair * 128 + 128]
        kt = k.T
        dv_sides = []
        dk_sides = []
        for side in range(2):
            half = (lane < 64) if side == 0 else (lane >= 64)
            k_half = jnp.where(half, k, jnp.zeros_like(k))
            v_half = jnp.where(half, v, jnp.zeros_like(v))
            head = 2 * pair + side
            scores = mm_nt(k_half, q) * 0.125 + bias_ref[...]
            probs = jnp.exp(scores - lse_ref[head : head + 1, :])
            dv_sides.append(mm(probs.astype(BF), do))
            dp = mm_nt(v_half, do)
            inner = jnp.sum(probs * dp, axis=0, keepdims=True)
            ds = (probs * (dp - inner)).astype(BF)
            dk_sides.append(mm(ds, q))
            at = pair * 128 + side * 64
            dqt_ref[at : at + 64, :] = (mm(kt[side * 64 : side * 64 + 64, :], ds) * 0.125).astype(BF)
        at = width + pair * 128
        r_ref[:, at : at + 128] = (jnp.where(lane < 64, dk_sides[0], dk_sides[1]) * 0.125).astype(BF)
        at = 2 * width + pair * 128
        r_ref[:, at : at + 128] = jnp.where(lane < 64, dv_sides[0], dv_sides[1]).astype(BF)
    r_ref[:, 0:width] = dqt_ref[...].T
    sums_ref[2:3, :] += column_sum(r_ref[:, 0:width].astype(F32))
    sums_ref[3:4, :] += column_sum(r_ref[:, 2 * width :].astype(F32))
    back = mm_nt(r_ref[...], wqkv[...])
    normed, inv = norm_parts(x_ref[...].astype(F32))
    sums_ref[0:1, :] += column_sum(back * normed)
    sums_ref[1:2, :] += column_sum(back)
    gin_ref[...] = (dh_ref[...] + norm_back(back * small[0:1, :], normed, inv)).astype(BF)


class Line:
    def __init__(self, axis, count, stride):
        self.axis, self.count, self.stride = axis, count, stride

    def stage(self):
        return lax.axis_index(self.axis) // self.stride

    def beside(self, by):
        return {self.axis: lax.axis_index(self.axis) + by * self.stride}


def greet(line):
    stage = line.stage()
    barrier = pltpu.get_barrier_semaphore()

    @pl.when(stage > 0)
    def _():
        pl.semaphore_signal(barrier, inc=1, device_id=line.beside(-1), device_id_type=MESH)

    @pl.when(stage < line.count - 1)
    def _():
        pl.semaphore_signal(barrier, inc=1, device_id=line.beside(1), device_id_type=MESH)

    expected = jnp.where(stage > 0, 1, 0) + jnp.where(stage < line.count - 1, 1, 0)
    pl.semaphore_wait(barrier, expected)


def forward_kernel(line, length, x_in, segr, segc, cls, wqkv_h, wproj_h, wup_h, wdown_h, small,
                   x_o, a_o, qkv_o, lse_o, o_o, h_o, a2_o, gp_o, u_o, acts_o,
                   wqkv, wproj, wup, wdown, xs, outs, a, qkv, lse, o, h, a2, gp, u, bias, ot,
                   w_sem, in_sem, x_sem, save_sem, act_sem, send_sem, recv_sem):
    micro = xs.shape[0]
    stage = line.stage()
    loads = [
        pltpu.make_async_copy(src, dst, w_sem.at[i])
        for i, (src, dst) in enumerate(((wqkv_h, wqkv), (wproj_h, wproj), (wup_h, wup), (wdown_h, wdown)))
    ]
    for load in loads:
        load.start()

    def first_in(m):
        return pltpu.make_async_copy(x_in.at[m], xs.at[m], in_sem.at[m])

    @pl.when(stage == 0)
    def _():
        for m in range(micro):
            first_in(m).start()

    greet(line)

    saved = ((a, a_o), (qkv, qkv_o), (lse, lse_o), (o, o_o), (h, h_o), (a2, a2_o), (gp, gp_o), (u, u_o))

    def saves(m, slot):
        return [
            pltpu.make_async_copy(here.at[slot], there.at[m], save_sem.at[slot, i])
            for i, (here, there) in enumerate(saved)
        ]

    def hop(m):
        return pltpu.make_async_remote_copy(
            src_ref=outs.at[m], dst_ref=xs.at[m], send_sem=send_sem.at[m], recv_sem=recv_sem.at[m],
            device_id=line.beside(1), device_id_type=MESH)

    def step(m, carry):
        slot = lax.rem(m, 2)

        @pl.when(stage == 0)
        def _():
            first_in(m).wait()

        @pl.when(stage > 0)
        def _():
            hop(m).wait_recv()

        pltpu.make_async_copy(xs.at[m], x_o.at[m], x_sem.at[m]).start()

        @pl.when(m >= 2)
        def _():
            for save in saves(m - 2, slot):
                save.wait()

        @pl.when(m == 0)
        def _():
            loads[0].wait()
            loads[1].wait()

        bias[...] = mask_bias(segr[m], segc[m], cls[m], length)

        def before_up():
            @pl.when(m == 0)
            def _():
                loads[2].wait()
                loads[3].wait()

        layer_forward(xs.at[m], bias, wqkv, wproj, wup, wdown, small, a.at[slot], qkv.at[slot],
                      lse.at[slot], o.at[slot], h.at[slot], a2.at[slot], gp.at[slot], u.at[slot],
                      outs.at[m], ot, before_up)

        @pl.when(stage < line.count - 1)
        def _():
            hop(m).start()

        for save in saves(m, slot):
            save.start()
        pltpu.make_async_copy(outs.at[m], acts_o.at[m], act_sem.at[m]).start()
        return carry

    lax.fori_loop(0, micro, step, 0)

    for m in range(max(micro - 2, 0), micro):
        for save in saves(m, m % 2):
            save.wait()
    for m in range(micro):
        pltpu.make_async_copy(xs.at[m], x_o.at[m], x_sem.at[m]).wait()
        pltpu.make_async_copy(outs.at[m], acts_o.at[m], act_sem.at[m]).wait()

    @pl.when(stage < line.count - 1)
    def _():
        for m in range(micro):
            hop(m).wait_send()


def backward_kernel(line, length, g_in, x_h, qkv_h, lse_h, h_h, gp_h, segr, segc, cls,
                    wqkv_h, wproj_h, wup_h, wdown_h, small,
                    g_o, dz_o, f_o, r_o, gin_o, sums_o,
                    wqkv, wproj, wup, wdown, gs, gins, x, qkv, lse, h, gp, dz, f, r, bias, do, dh, dqt,
                    w_sem, in_sem, g_sem, load_sem, save_sem, act_sem, send_sem, recv_sem):
    micro = gs.shape[0]
    stage = line.stage()
    loads = [
        pltpu.make_async_copy(src, dst, w_sem.at[i])
        for i, (src, dst) in enumerate(((wdown_h, wdown), (wup_h, wup), (wproj_h, wproj), (wqkv_h, wqkv)))
    ]

    def last_in(m):
        return pltpu.make_async_copy(g_in.at[m], gs.at[m], in_sem.at[m])

    @pl.when(stage == line.count - 1)
    def _():
        for m in range(micro):
            last_in(m).start()

    kept = ((gp_h, gp), (h_h, h), (qkv_h, qkv), (lse_h, lse), (x_h, x))

    def fetches(m, slot):
        return [
            pltpu.make_async_copy(there.at[m], here.at[slot], load_sem.at[slot, i])
            for i, (there, here) in enumerate(kept)
        ]

    loads[0].start()
    for fetch in fetches(0, 0):
        fetch.start()
    for load in loads[1:]:
        load.start()
    sums_o[...] = jnp.zeros_like(sums_o)
    greet(line)

    saved = ((dz, dz_o), (f, f_o), (r, r_o))

    def saves(m, slot):
        return [
            pltpu.make_async_copy(here.at[slot], there.at[m], save_sem.at[slot, i])
            for i, (here, there) in enumerate(saved)
        ]

    def hop(m):
        return pltpu.make_async_remote_copy(
            src_ref=gins.at[m], dst_ref=gs.at[m], send_sem=send_sem.at[m], recv_sem=recv_sem.at[m],
            device_id=line.beside(-1), device_id_type=MESH)

    def step(m, carry):
        slot = lax.rem(m, 2)

        @pl.when(m + 1 < micro)
        def _():
            for fetch in fetches(m + 1, 1 - slot):
                fetch.start()

        @pl.when(m == 0)
        def _():
            for load in loads:
                load.wait()

        for fetch in fetches(m, slot):
            fetch.wait()
        bias[...] = mask_bias(segr[m], segc[m], cls[m], length)

        @pl.when(m >= 2)
        def _():
            for save in saves(m - 2, slot):
                save.wait()

        @pl.when(stage == line.count - 1)
        def _():
            last_in(m).wait()

        @pl.when(stage < line.count - 1)
        def _():
            hop(m).wait_recv()

        pltpu.make_async_copy(gs.at[m], g_o.at[m], g_sem.at[m]).start()
        layer_backward(gs.at[m], x.at[slot], bias, qkv.at[slot], lse.at[slot], h.at[slot], gp.at[slot],
                       wqkv, wproj, wup, wdown, small, dz.at[slot], f.at[slot], r.at[slot], gins.at[m],
                       sums_o, do, dh, dqt)

        @pl.when(stage > 0)
        def _():
            hop(m).start()

        for save in saves(m, slot):
            save.start()
        pltpu.make_async_copy(gins.at[m], gin_o.at[m], act_sem.at[m]).start()
        return carry

    lax.fori_loop(0, micro, step, 0)

    for m in range(max(micro - 2, 0), micro):
        for save in saves(m, m % 2):
            save.wait()
    for m in range(micro):
        pltpu.make_async_copy(gs.at[m], g_o.at[m], g_sem.at[m]).wait()
        pltpu.make_async_copy(gins.at[m], gin_o.at[m], act_sem.at[m]).wait()

    @pl.when(stage > 0)
    def _():
        for m in range(micro):
            hop(m).wait_send()


IN_VMEM = pl.BlockSpec(memory_space=pltpu.VMEM)
IN_SMEM = pl.BlockSpec(memory_space=pltpu.SMEM)
ANYWHERE = pl.BlockSpec(memory_space=pl.ANY)
DMA = pltpu.SemaphoreType.DMA


def run_forward(line, length, x_in, segr, segc, cls, weights, small):
    micro, rows, width = x_in.shape
    hidden = weights[2].shape[1]
    shape = jax.ShapeDtypeStruct
    saved = (
        ((rows, width), BF), ((rows, 3 * width), BF), ((16, rows), F32), ((rows, width), BF),
        ((rows, width), F32), ((rows, width), BF), ((rows, hidden), BF), ((rows, hidden), BF))
    many = shape((micro, rows, width), BF)
    return pl.pallas_call(
        functools.partial(forward_kernel, line, length),
        out_shape=[many] + [shape((micro,) + s, t) for s, t in saved] + [many],
        in_specs=[ANYWHERE, IN_VMEM, IN_VMEM, IN_SMEM] + [ANYWHERE] * 4 + [IN_VMEM],
        out_specs=[ANYWHERE] * 10,
        scratch_shapes=[pltpu.VMEM(w.shape, BF) for w in weights]
        + [pltpu.VMEM((micro, rows, width), BF)] * 2
        + [pltpu.VMEM((2,) + s, t) for s, t in saved]
        + [pltpu.VMEM((rows, rows), F32), pltpu.VMEM((width, rows), BF)]
        + [DMA((4,)), DMA((micro,)), DMA((micro,)), DMA((2, 8)), DMA((micro,)), DMA((micro,)), DMA((micro,))],
        compiler_params=pltpu.CompilerParams(
            collective_id=0, has_side_effects=True, vmem_limit_bytes=VMEM_CAP),
        name="forward_line",
    )(x_in, segr, segc, cls, *weights, small)


def run_backward(line, length, g_in, x, qkv, lse, h, gp, segr, segc, cls, weights, small):
    micro, rows, width = g_in.shape
    hidden = weights[2].shape[1]
    shape = jax.ShapeDtypeStruct
    many = shape((micro, rows, width), BF)
    wqkv, wproj, wup, wdown = weights
    return pl.pallas_call(
        functools.partial(backward_kernel, line, length),
        out_shape=[many, shape((micro, rows, hidden), BF), many, shape((micro, rows, 3 * width), BF), many,
                   shape((16, width), F32)],
        in_specs=[ANYWHERE] * 6 + [IN_VMEM, IN_VMEM, IN_SMEM] + [ANYWHERE] * 4 + [IN_VMEM],
        out_specs=[ANYWHERE] * 5 + [IN_VMEM],
        scratch_shapes=[pltpu.VMEM(w.shape, BF) for w in weights]
        + [pltpu.VMEM((micro, rows, width), BF)] * 2
        + [pltpu.VMEM((2, rows, width), BF), pltpu.VMEM((2, rows, 3 * width), BF), pltpu.VMEM((2, 16, rows), F32),
           pltpu.VMEM((2, rows, width), F32), pltpu.VMEM((2, rows, hidden), BF),
           pltpu.VMEM((2, rows, hidden), BF), pltpu.VMEM((2, rows, width), BF), pltpu.VMEM((2, rows, 3 * width), BF),
           pltpu.VMEM((rows, rows), F32), pltpu.VMEM((rows, width), BF), pltpu.VMEM((rows, width), F32),
           pltpu.VMEM((width, rows), BF)]
        + [DMA((4,)), DMA((micro,)), DMA((micro,)), DMA((2, 5)), DMA((2, 3)), DMA((micro,)), DMA((micro,)),
           DMA((micro,))],
        compiler_params=pltpu.CompilerParams(
            collective_id=1, has_side_effects=True, vmem_limit_bytes=VMEM_CAP),
        name="backward_line",
    )(g_in, x, qkv, lse, h, gp, segr, segc, cls, wqkv, wproj, wup, wdown, small)


def split_small(small, width, slices):
    share = width // slices
    stacked = small.reshape(slices, small.shape[0] // slices)
    eight = stacked[:, : 8 * share].reshape(slices, 8, share).transpose(1, 0, 2).reshape(8, width)
    up = stacked[:, 8 * share :].reshape(-1, width)
    return jnp.concatenate([eight, up, jnp.zeros((16 - 8 - up.shape[0], width), small.dtype)], axis=0)


def join_small(table, total, slices):
    width = table.shape[1]
    share = width // slices
    ups = total // width - 8
    eight = table[:8].reshape(8, slices, share).transpose(1, 0, 2).reshape(slices, 8 * share)
    up = table[8 : 8 + ups].reshape(slices, -1)
    return jnp.concatenate([eight, up], axis=1).reshape(-1)


def weight_grad(left, right):
    rows = left.shape[0] * left.shape[1]
    return lax.dot_general(left.reshape(rows, -1), right.reshape(rows, -1), (((0,), (0,)), ((), ())),
                           preferred_element_type=F32)


def per_device(inputs, out_grad, segment_ids, cls_index, *states):
    masters, firsts, seconds = states[0:5], states[5:10], states[10:15]
    slices = lax.axis_size("dp")
    line = Line("section", lax.axis_size("section"), 1)
    seq_dev, length, width = inputs.shape
    rows = -(-length // 128) * 128

    gathered = [lax.all_gather(m.astype(BF), "dp", axis=1, tiled=True)[0] for m in masters]
    weights = gathered[:4]
    total = gathered[4].shape[0]
    small = split_small(gathered[4].astype(F32), width, slices)

    extra = ((0, 0), (0, rows - length), (0, 0))
    x_in = jnp.pad(inputs, extra)
    g_in = jnp.pad(out_grad, extra)
    segs = jnp.pad(segment_ids, ((0, 0), (0, rows - length)), constant_values=-1)
    segr, segc = segs[:, None, :], segs[:, :, None]

    x, a, qkv, lse, o, h, a2, gp, u, acts = run_forward(line, length, x_in, segr, segc, cls_index, weights, small)
    g, dz, f, r, gin, sums = run_backward(line, length, g_in, x, qkv, lse, h, gp, segr, segc, cls_index, weights, small)
    totals = [weight_grad(a, r).astype(BF), weight_grad(o, f).astype(BF), weight_grad(a2, dz).astype(BF),
              weight_grad(u, g).astype(BF), join_small(sums, total, slices)]
    shards = [lax.psum_scatter(t[None], "dp", scatter_dimension=1, tiled=True).astype(F32) for t in totals]
    squares = jnp.sum(jnp.stack([jnp.sum(s * s) for s in shards]))
    grad_norm = jnp.sqrt(lax.psum(squares, ("dp", "section")))
    factor = 1.0 / jnp.maximum(grad_norm, 1.0)
    fix = 1.0 - 0.5**STEP
    results = []
    for kind in range(5):
        grad = shards[kind] * factor
        first = 0.5 * firsts[kind] + 0.5 * grad
        second = 0.5 * seconds[kind] + 0.5 * grad * grad
        update = first / fix / (jnp.sqrt(second / fix) + adam_eps)
        rate = small_rate
        if kind < 4:
            update = update + decay_rate * masters[kind]
            rate = learn_rate
        results += [grad, masters[kind] - rate * update, first, second]
    return (acts[:, :length][None], gin[:, :length][None], grad_norm.reshape(1)) + tuple(results)


def solution(mesh):
    matrix, vector = P("section", "dp", None), P("section", "dp")
    states = (matrix,) * 4 + (vector,)
    return jax.shard_map(
        per_device,
        mesh=mesh,
        in_specs=(P("dp", None, None), P("dp", None, None), P("dp", None), P("dp")) + states * 3,
        out_specs=(P("section", "dp", None, None), P("section", "dp", None, None), P())
        + (matrix,) * 16 + (vector,) * 4,
        check_vma=False,
    )
```

```python
import functools

import jax
import jax.numpy as jnp
from jax import lax
from jax.experimental import pallas as pl
from jax.experimental.pallas import tpu as pltpu
from jax.sharding import PartitionSpec as P

HEADS = 12
STEP = 3
F32 = jnp.float32
BF = jnp.bfloat16
MESH = pl.DeviceIdType.MESH
VMEM_CAP = 60 * 1024 * 1024

norm_eps = 1e-06
masked_score = -1e30
learn_rate = 0.05
small_rate = 0.3
decay_rate = 0.05
adam_eps = 1e-08

NT = (((1,), (1,)), ((), ()))


def mm(a, b):
    return jnp.dot(a, b, preferred_element_type=F32)


def mm_nt(a, b):
    return lax.dot_general(a, b, NT, preferred_element_type=F32)


def norm_parts(values):
    center = values - jnp.mean(values, axis=-1, keepdims=True)
    spread = jnp.mean(center * center, axis=-1, keepdims=True)
    inv = lax.rsqrt(spread + norm_eps)
    return center * inv, inv


def norm_back(y, normed, inv):
    pull = jnp.mean(y * normed, axis=-1, keepdims=True)
    return (y - jnp.mean(y, axis=-1, keepdims=True) - normed * pull) * inv


def column_sum(values):
    return jnp.sum(values, axis=0, keepdims=True)


def mask_bias(seg_row, seg_col, cls, length):
    size = seg_col.shape[0]
    key_at = lax.broadcasted_iota(jnp.int32, (size, size), 0)
    query_at = lax.broadcasted_iota(jnp.int32, (size, size), 1)
    allowed = (seg_row == seg_col) | (key_at == cls) | (query_at == cls)
    allowed = allowed & (key_at < length)
    return jnp.where(allowed, 0.0, masked_score).astype(F32)


def gelu_parts(z):
    density = jnp.exp(z * z * -0.5) * 0.3989422804014327
    below = 0.5 + 0.5 * lax.erf(z * 0.7071067811865476)
    return z * below, below + z * density


def layer_forward(x_ref, bias_ref, wqkv, wproj, wup, wdown, small, a_ref, qkv_ref, lse_ref, o_ref,
                  h_ref, a2_ref, gp_ref, u_ref, out_ref, ot_ref, before_up):
    rows, width = x_ref.shape
    hidden = wup.shape[1]
    normed, _ = norm_parts(x_ref[...].astype(F32))
    a_ref[...] = (normed * small[0:1, :] + small[1:2, :]).astype(BF)
    for part in range(3):
        cols = slice(part * width, (part + 1) * width)
        mixed = mm(a_ref[...], wqkv[:, cols])
        if part == 0:
            mixed = mixed + small[2:3, :]
        if part == 2:
            mixed = mixed + small[3:4, :]
        qkv_ref[:, cols] = mixed.astype(BF)
    lane = lax.broadcasted_iota(jnp.int32, (rows, 128), 1)
    for pair in range(HEADS // 2):
        q = qkv_ref[:, pair * 128 : pair * 128 + 128]
        k = qkv_ref[:, width + pair * 128 : width + pair * 128 + 128]
        vt = qkv_ref[:, 2 * width + pair * 128 : 2 * width + pair * 128 + 128].T
        for side in range(2):
            half = (lane < 64) if side == 0 else (lane >= 64)
            k_half = jnp.where(half, k, jnp.zeros_like(k))
            scores = mm_nt(k_half, q) * 0.125 + bias_ref[...]
            peak = jnp.max(scores, axis=0, keepdims=True)
            raised = jnp.exp(scores - peak)
            summed = jnp.sum(raised, axis=0, keepdims=True)
            mixed = mm(vt[side * 64 : side * 64 + 64, :], raised.astype(BF)) * (1.0 / summed)
            at = pair * 128 + side * 64
            ot_ref[at : at + 64, :] = mixed.astype(BF)
            head = 2 * pair + side
            lse_ref[head : head + 1, :] = peak + jnp.log(summed)
    o_ref[...] = ot_ref[...].T
    h = x_ref[...].astype(F32) + (mm(o_ref[...], wproj[...]) + small[4:5, :])
    h_ref[...] = h
    normed, _ = norm_parts(h)
    a2_ref[...] = (normed * small[5:6, :] + small[6:7, :]).astype(BF)
    before_up()
    for part in range(hidden // width):
        cols = slice(part * width, (part + 1) * width)
        z = mm(a2_ref[...], wup[:, cols]) + small[8 + part : 9 + part, :]
        u, slope = gelu_parts(z)
        u_ref[:, cols] = u.astype(BF)
        gp_ref[:, cols] = slope.astype(BF)
    out_ref[...] = (h_ref[...] + (mm(u_ref[...], wdown[...]) + small[7:8, :])).astype(BF)


def layer_backward(g_ref, x_ref, bias_ref, qkv_ref, lse_ref, h_ref, gp_ref, wqkv, wproj, wup, wdown,
                   small, dz_ref, f_ref, r_ref, gin_ref, sums_ref, do_ref, dh_ref, dqt_ref):
    rows, width = x_ref.shape
    hidden = wup.shape[1]
    carried = g_ref[...].astype(F32)
    sums_ref[7:8, :] += column_sum(carried)
    for part in range(hidden // width):
        cols = slice(part * width, (part + 1) * width)
        back = mm_nt(g_ref[...], wdown[cols, :])
        dz = (back * gp_ref[:, cols].astype(F32)).astype(BF)
        dz_ref[:, cols] = dz
        sums_ref[8 + part : 9 + part, :] += column_sum(dz.astype(F32))
    back = mm_nt(dz_ref[...], wup[...])
    normed, inv = norm_parts(h_ref[...])
    sums_ref[5:6, :] += column_sum(back * normed)
    sums_ref[6:7, :] += column_sum(back)
    dh = carried + norm_back(back * small[5:6, :], normed, inv)
    dh_ref[...] = dh
    f = dh.astype(BF)
    f_ref[...] = f
    sums_ref[4:5, :] += column_sum(f.astype(F32))
    do_ref[...] = mm_nt(f_ref[...], wproj[...]).astype(BF)
    lane = lax.broadcasted_iota(jnp.int32, (rows, 128), 1)
    for pair in range(HEADS // 2):
        q = qkv_ref[:, pair * 128 : pair * 128 + 128]
        k = qkv_ref[:, width + pair * 128 : width + pair * 128 + 128]
        v = qkv_ref[:, 2 * width + pair * 128 : 2 * width + pair * 128 + 128]
        do = do_ref[:, pair * 128 : pair * 128 + 128]
        kt = k.T
        dv_sides = []
        dk_sides = []
        for side in range(2):
            half = (lane < 64) if side == 0 else (lane >= 64)
            k_half = jnp.where(half, k, jnp.zeros_like(k))
            v_half = jnp.where(half, v, jnp.zeros_like(v))
            head = 2 * pair + side
            scores = mm_nt(k_half, q) * 0.125 + bias_ref[...]
            probs = jnp.exp(scores - lse_ref[head : head + 1, :])
            dv_sides.append(mm(probs.astype(BF), do))
            dp = mm_nt(v_half, do)
            inner = jnp.sum(probs * dp, axis=0, keepdims=True)
            ds = (probs * (dp - inner)).astype(BF)
            dk_sides.append(mm(ds, q))
            at = pair * 128 + side * 64
            dqt_ref[at : at + 64, :] = (mm(kt[side * 64 : side * 64 + 64, :], ds) * 0.125).astype(BF)
        at = width + pair * 128
        r_ref[:, at : at + 128] = (jnp.where(lane < 64, dk_sides[0], dk_sides[1]) * 0.125).astype(BF)
        at = 2 * width + pair * 128
        r_ref[:, at : at + 128] = jnp.where(lane < 64, dv_sides[0], dv_sides[1]).astype(BF)
    r_ref[:, 0:width] = dqt_ref[...].T
    sums_ref[2:3, :] += column_sum(r_ref[:, 0:width].astype(F32))
    sums_ref[3:4, :] += column_sum(r_ref[:, 2 * width :].astype(F32))
    back = mm_nt(r_ref[...], wqkv[...])
    normed, inv = norm_parts(x_ref[...].astype(F32))
    sums_ref[0:1, :] += column_sum(back * normed)
    sums_ref[1:2, :] += column_sum(back)
    gin_ref[...] = (dh_ref[...] + norm_back(back * small[0:1, :], normed, inv)).astype(BF)


class Line:
    def __init__(self, axis, count, stride):
        self.axis, self.count, self.stride = axis, count, stride

    def stage(self):
        return lax.axis_index(self.axis) // self.stride

    def beside(self, by):
        return {self.axis: lax.axis_index(self.axis) + by * self.stride}


class Spot:
    def __init__(self, x, y, z, c):
        self.x, self.y, self.z, self.c = x, y, z, c

    @staticmethod
    def here():
        dp, section = lax.axis_index("dp"), lax.axis_index("section")
        return Spot(dp % 2, section // 2, dp // 2, section % 2)

    def dp(self):
        return self.z * 2 + self.x

    def section(self):
        return self.y * 2 + self.c

    def id(self):
        return (self.dp(), self.section())

    def flip(self, x=0, y=0, c=0):
        return Spot(1 - self.x if x else self.x, 1 - self.y if y else self.y, self.z, 1 - self.c if c else self.c)

    def turned(self):
        return Spot(self.x, self.z // 2, self.section(), self.z % 2)

    def drop(self):
        return Spot(self.x, (self.y + self.z + self.c) % 2, self.section(), self.z // 2)

    def source(self):
        y, c = self.z // 2, self.z % 2
        return Spot(self.x, y, 2 * self.c + (self.y + y + c) % 2, c)

    def part(self):
        return self.source().dp()


def same(one, other):
    return (one.dp() == other.dp()) & (one.section() == other.section())


def hail(spot):
    pl.semaphore_signal(pltpu.get_barrier_semaphore(), inc=1, device_id=spot.id(), device_id_type=MESH)


def greet(line, turned):
    stage = line.stage()
    barrier = pltpu.get_barrier_semaphore()

    @pl.when(stage > 0)
    def _():
        pl.semaphore_signal(barrier, inc=1, device_id=line.beside(-1), device_id_type=MESH)

    @pl.when(stage < line.count - 1)
    def _():
        pl.semaphore_signal(barrier, inc=1, device_id=line.beside(1), device_id_type=MESH)

    expected = jnp.where(stage > 0, 1, 0) + jnp.where(stage < line.count - 1, 1, 0)
    if turned:
        me = Spot.here()
        alone = same(me, me.turned())

        @pl.when(jnp.logical_not(alone))
        def _():
            hail(me.turned())

        expected = expected + jnp.where(alone, 0, 1)
    pl.semaphore_wait(barrier, expected)


def forward_kernel(line, length, turned, x_first, x_in, segr, segc, cls, wqkv_h, wproj_h, wup_h, wdown_h, small,
                   x_o, a_o, qkv_o, lse_o, o_o, h_o, a2_o, gp_o, u_o, acts_o,
                   wqkv, wproj, wup, wdown, xs, outs, a, qkv, lse, o, h, a2, gp, u, bias, ot,
                   w_sem, in_sem, x_sem, save_sem, act_sem, send_sem, recv_sem):
    micro = xs.shape[0]
    stage = line.stage()
    loads = [
        pltpu.make_async_copy(src, dst, w_sem.at[i])
        for i, (src, dst) in enumerate(((wqkv_h, wqkv), (wproj_h, wproj), (wup_h, wup), (wdown_h, wdown)))
    ]
    for load in loads:
        load.start()

    def first_in(m):
        return pltpu.make_async_copy(x_in.at[m], xs.at[m], in_sem.at[m])

    greet(line, turned)
    if turned:
        me = Spot.here()
        partner = me.turned()
        alone = same(me, partner)

        def turn_in(m):
            return pltpu.make_async_remote_copy(
                src_ref=x_in.at[m], dst_ref=xs.at[m], send_sem=in_sem.at[m], recv_sem=recv_sem.at[m],
                device_id=partner.id(), device_id_type=MESH)

        feeds = jnp.logical_and(me.section() == 0, jnp.logical_not(alone))
        fed = jnp.logical_and(stage == 0, jnp.logical_not(alone))
        feeds_self = jnp.logical_and(stage == 0, alone)

        @pl.when(stage == 0)
        def _():
            pltpu.make_async_copy(x_first, xs.at[0], in_sem.at[0]).start()

        for m in range(1, micro):
            @pl.when(feeds)
            def _():
                turn_in(m).start()

            @pl.when(feeds_self)
            def _():
                first_in(m).start()
    else:
        @pl.when(stage == 0)
        def _():
            for m in range(micro):
                first_in(m).start()

    saved = ((a, a_o), (qkv, qkv_o), (lse, lse_o), (o, o_o), (h, h_o), (a2, a2_o), (gp, gp_o), (u, u_o))

    def saves(m, slot):
        return [
            pltpu.make_async_copy(here.at[slot], there.at[m], save_sem.at[slot, i])
            for i, (here, there) in enumerate(saved)
        ]

    def hop(m):
        return pltpu.make_async_remote_copy(
            src_ref=outs.at[m], dst_ref=xs.at[m], send_sem=send_sem.at[m], recv_sem=recv_sem.at[m],
            device_id=line.beside(1), device_id_type=MESH)

    def step(m, carry):
        slot = lax.rem(m, 2)

        if turned:
            here = jnp.logical_or(feeds_self, jnp.logical_and(stage == 0, m == 0))
        else:
            here = stage == 0

        @pl.when(here)
        def _():
            first_in(m).wait()

        @pl.when(jnp.logical_not(here))
        def _():
            hop(m).wait_recv()

        pltpu.make_async_copy(xs.at[m], x_o.at[m], x_sem.at[m]).start()

        @pl.when(m >= 2)
        def _():
            for save in saves(m - 2, slot):
                save.wait()

        @pl.when(m == 0)
        def _():
            loads[0].wait()
            loads[1].wait()

        bias[...] = mask_bias(segr[m], segc[m], cls[m], length)

        def before_up():
            @pl.when(m == 0)
            def _():
                loads[2].wait()
                loads[3].wait()

        layer_forward(xs.at[m], bias, wqkv, wproj, wup, wdown, small, a.at[slot], qkv.at[slot],
                      lse.at[slot], o.at[slot], h.at[slot], a2.at[slot], gp.at[slot], u.at[slot],
                      outs.at[m], ot, before_up)

        @pl.when(stage < line.count - 1)
        def _():
            hop(m).start()

        for save in saves(m, slot):
            save.start()
        pltpu.make_async_copy(outs.at[m], acts_o.at[m], act_sem.at[m]).start()
        return carry

    lax.fori_loop(0, micro, step, 0)

    for m in range(max(micro - 2, 0), micro):
        for save in saves(m, m % 2):
            save.wait()
    for m in range(micro):
        pltpu.make_async_copy(xs.at[m], x_o.at[m], x_sem.at[m]).wait()
        pltpu.make_async_copy(outs.at[m], acts_o.at[m], act_sem.at[m]).wait()

    @pl.when(stage < line.count - 1)
    def _():
        for m in range(micro):
            hop(m).wait_send()

    if turned:
        @pl.when(feeds)
        def _():
            for m in range(1, micro):
                turn_in(m).wait_send()


def backward_kernel(line, length, turned, acts_h, g_in, x_h, qkv_h, lse_h, h_h, gp_h, segr, segc, cls,
                    wqkv_h, wproj_h, wup_h, wdown_h, small,
                    acts_o, g_o, dz_o, f_o, r_o, gin_o, sums_o,
                    wqkv, wproj, wup, wdown, gs, gins, x, qkv, lse, h, gp, dz, f, r, bias, do, dh, dqt,
                    w_sem, in_sem, g_sem, load_sem, save_sem, act_sem, send_sem, recv_sem, home_sem):
    micro = gs.shape[0]
    stage = line.stage()
    loads = [
        pltpu.make_async_copy(src, dst, w_sem.at[i])
        for i, (src, dst) in enumerate(((wdown_h, wdown), (wup_h, wup), (wproj_h, wproj), (wqkv_h, wqkv)))
    ]

    def last_in(m):
        return pltpu.make_async_copy(g_in.at[m], gs.at[m], in_sem.at[m])

    @pl.when(stage == line.count - 1)
    def _():
        for m in range(micro):
            last_in(m).start()

    kept = ((gp_h, gp), (h_h, h), (qkv_h, qkv), (lse_h, lse), (x_h, x))

    def fetches(m, slot):
        return [
            pltpu.make_async_copy(there.at[m], here.at[slot], load_sem.at[slot, i])
            for i, (there, here) in enumerate(kept)
        ]

    loads[0].start()
    for fetch in fetches(0, 0):
        fetch.start()
    for load in loads[1:]:
        load.start()
    sums_o[...] = jnp.zeros_like(sums_o)
    greet(line, turned)
    if turned:
        me = Spot.here()
        partner = me.turned()
        alone = same(me, partner)

        def home(m):
            return pltpu.make_async_remote_copy(
                src_ref=acts_h.at[m], dst_ref=acts_o.at[m], send_sem=home_sem.at[0, m], recv_sem=home_sem.at[1, m],
                device_id=partner.id(), device_id_type=MESH)

        def stay(m):
            return pltpu.make_async_copy(acts_h.at[m], acts_o.at[m], home_sem.at[0, m])

        for m in range(micro):
            pl.when(alone)(lambda: stay(m).start())
            pl.when(jnp.logical_not(alone))(lambda: home(m).start())
    else:
        for m in range(micro):
            pltpu.make_async_copy(acts_h.at[m], acts_o.at[m], home_sem.at[0, m]).start()

    saved = ((dz, dz_o), (f, f_o), (r, r_o))

    def saves(m, slot):
        return [
            pltpu.make_async_copy(here.at[slot], there.at[m], save_sem.at[slot, i])
            for i, (here, there) in enumerate(saved)
        ]

    def hop(m):
        return pltpu.make_async_remote_copy(
            src_ref=gins.at[m], dst_ref=gs.at[m], send_sem=send_sem.at[m], recv_sem=recv_sem.at[m],
            device_id=line.beside(-1), device_id_type=MESH)

    def step(m, carry):
        slot = lax.rem(m, 2)

        @pl.when(m + 1 < micro)
        def _():
            for fetch in fetches(m + 1, 1 - slot):
                fetch.start()

        @pl.when(m == 0)
        def _():
            for load in loads:
                load.wait()

        for fetch in fetches(m, slot):
            fetch.wait()
        bias[...] = mask_bias(segr[m], segc[m], cls[m], length)

        @pl.when(m >= 2)
        def _():
            for save in saves(m - 2, slot):
                save.wait()

        @pl.when(stage == line.count - 1)
        def _():
            last_in(m).wait()

        @pl.when(stage < line.count - 1)
        def _():
            hop(m).wait_recv()

        pltpu.make_async_copy(gs.at[m], g_o.at[m], g_sem.at[m]).start()
        layer_backward(gs.at[m], x.at[slot], bias, qkv.at[slot], lse.at[slot], h.at[slot], gp.at[slot],
                       wqkv, wproj, wup, wdown, small, dz.at[slot], f.at[slot], r.at[slot], gins.at[m],
                       sums_o, do, dh, dqt)

        @pl.when(stage > 0)
        def _():
            hop(m).start()

        for save in saves(m, slot):
            save.start()
        pltpu.make_async_copy(gins.at[m], gin_o.at[m], act_sem.at[m]).start()
        return carry

    lax.fori_loop(0, micro, step, 0)

    for m in range(max(micro - 2, 0), micro):
        for save in saves(m, m % 2):
            save.wait()
    for m in range(micro):
        pltpu.make_async_copy(gs.at[m], g_o.at[m], g_sem.at[m]).wait()
        pltpu.make_async_copy(gins.at[m], gin_o.at[m], act_sem.at[m]).wait()

    @pl.when(stage > 0)
    def _():
        for m in range(micro):
            hop(m).wait_send()

    for m in range(micro):
        if turned:
            pl.when(alone)(lambda: stay(m).wait())
            pl.when(jnp.logical_not(alone))(lambda: home(m).wait())
        else:
            pltpu.make_async_copy(acts_h.at[m], acts_o.at[m], home_sem.at[0, m]).wait()


IN_VMEM = pl.BlockSpec(memory_space=pltpu.VMEM)
IN_SMEM = pl.BlockSpec(memory_space=pltpu.SMEM)
ANYWHERE = pl.BlockSpec(memory_space=pl.ANY)
DMA = pltpu.SemaphoreType.DMA


def run_forward(line, length, turned, x_first, x_in, segr, segc, cls, weights, small):
    micro, rows, width = x_in.shape
    hidden = weights[2].shape[1]
    shape = jax.ShapeDtypeStruct
    saved = (
        ((rows, width), BF), ((rows, 3 * width), BF), ((16, rows), F32), ((rows, width), BF),
        ((rows, width), F32), ((rows, width), BF), ((rows, hidden), BF), ((rows, hidden), BF))
    many = shape((micro, rows, width), BF)
    return pl.pallas_call(
        functools.partial(forward_kernel, line, length, turned),
        out_shape=[many] + [shape((micro,) + s, t) for s, t in saved] + [many],
        in_specs=[ANYWHERE, ANYWHERE, IN_VMEM, IN_VMEM, IN_SMEM] + [ANYWHERE] * 4 + [IN_VMEM],
        out_specs=[ANYWHERE] * 10,
        scratch_shapes=[pltpu.VMEM(w.shape, BF) for w in weights]
        + [pltpu.VMEM((micro, rows, width), BF)] * 2
        + [pltpu.VMEM((2,) + s, t) for s, t in saved]
        + [pltpu.VMEM((rows, rows), F32), pltpu.VMEM((width, rows), BF)]
        + [DMA((4,)), DMA((micro,)), DMA((micro,)), DMA((2, 8)), DMA((micro,)), DMA((micro,)), DMA((micro,))],
        compiler_params=pltpu.CompilerParams(
            collective_id=0, has_side_effects=True, vmem_limit_bytes=VMEM_CAP),
        name="forward_line",
    )(x_first, x_in, segr, segc, cls, *weights, small)


def run_backward(line, length, turned, acts, g_in, x, qkv, lse, h, gp, segr, segc, cls, weights, small):
    micro, rows, width = g_in.shape
    hidden = weights[2].shape[1]
    shape = jax.ShapeDtypeStruct
    many = shape((micro, rows, width), BF)
    wqkv, wproj, wup, wdown = weights
    return pl.pallas_call(
        functools.partial(backward_kernel, line, length, turned),
        out_shape=[many, many, shape((micro, rows, hidden), BF), many, shape((micro, rows, 3 * width), BF), many,
                   shape((16, width), F32)],
        in_specs=[ANYWHERE] * 7 + [IN_VMEM, IN_VMEM, IN_SMEM] + [ANYWHERE] * 4 + [IN_VMEM],
        out_specs=[ANYWHERE] * 6 + [IN_VMEM],
        scratch_shapes=[pltpu.VMEM(w.shape, BF) for w in weights]
        + [pltpu.VMEM((micro, rows, width), BF)] * 2
        + [pltpu.VMEM((2, rows, width), BF), pltpu.VMEM((2, rows, 3 * width), BF), pltpu.VMEM((2, 16, rows), F32),
           pltpu.VMEM((2, rows, width), F32), pltpu.VMEM((2, rows, hidden), BF),
           pltpu.VMEM((2, rows, hidden), BF), pltpu.VMEM((2, rows, width), BF), pltpu.VMEM((2, rows, 3 * width), BF),
           pltpu.VMEM((rows, rows), F32), pltpu.VMEM((rows, width), BF), pltpu.VMEM((rows, width), F32),
           pltpu.VMEM((width, rows), BF)]
        + [DMA((4,)), DMA((micro,)), DMA((micro,)), DMA((2, 5)), DMA((2, 3)), DMA((micro,)), DMA((micro,)),
           DMA((micro,)), DMA((2, micro))],
        compiler_params=pltpu.CompilerParams(
            collective_id=1, has_side_effects=True, vmem_limit_bytes=VMEM_CAP),
        name="backward_line",
    )(acts, g_in, x, qkv, lse, h, gp, segr, segc, cls, wqkv, wproj, wup, wdown, small)


GATHER_PIECES = ((0, 0, 96), (4, 0, 16), (1, 0, 96), (2, 0, 48), (2, 48, 48), (3, 0, 192), (3, 192, 192))
SCATTER_PIECES = ((3, 0, 192), (3, 192, 192), (2, 0, 48), (2, 48, 48), (0, 0, 96), (1, 0, 96), (4, 0, 16))


def gather_kernel(pieces, micro, *refs):
    count = 5
    shares, (x_in, g_in, seg_in) = refs[:count], refs[count : count + 3]
    wholes, (x_o, g_o, seg_o) = refs[count + 3 : 2 * count + 3], refs[2 * count + 3 : 2 * count + 6]
    send, recv, local, turn_send, turn_recv = refs[2 * count + 6 :]
    me = Spot.here()
    xn, yn, cn = me.flip(x=1), me.flip(y=1), me.flip(c=1)
    target, source, partner = me.drop(), me.source(), me.turned()
    stays, alone = same(me, target), same(me, partner)
    moves, pairs = jnp.logical_not(stays), jnp.logical_not(alone)
    for spot in (xn, yn, cn):
        hail(spot)

    @pl.when(moves)
    def _():
        hail(target)
        hail(source)

    @pl.when(pairs)
    def _():
        hail(partner)

    pl.semaphore_wait(pltpu.get_barrier_semaphore(), 3 + jnp.where(stays, 0, 2) + jnp.where(alone, 0, 1))

    def rows(k, part):
        array, first, size = pieces[k]
        share = shares[array].shape[0]
        return wholes[array].at[pl.ds(pl.multiple_of(part * share + first, 16), size)]

    def mine(k):
        array, first, size = pieces[k]
        return shares[array].at[pl.ds(first, size)]

    def remote(src, dst, kind, k, spot):
        return pltpu.make_async_remote_copy(
            src_ref=src, dst_ref=dst, send_sem=send.at[kind, k], recv_sem=recv.at[kind, k],
            device_id=spot.id(), device_id_type=MESH)

    def brought(k, part):
        return remote(mine(k), rows(k, part), 0, k, target)

    def kept(k):
        return pltpu.make_async_copy(mine(k), rows(k, me.dp()), local.at[k])

    def passed(kind, k, part, spot):
        return remote(rows(k, part), rows(k, part), kind, k, spot)

    def parts(spot):
        return [s.part() for s in (spot, spot.flip(x=1), spot.flip(y=1), spot.flip(x=1, y=1))]

    own, own_x, own_y, own_d = parts(me)
    beside = parts(cn)
    turns = [(x_in, x_o), (seg_in, seg_o)] + [(g_in.at[m], g_o.at[m]) for m in range(micro)]
    gives = [me.section() == 0, me.section() >= 0] + [me.section() == 3] * micro
    takes = [me.z == 0, me.z >= 0] + [me.z == 3] * micro

    def turn(i):
        return pltpu.make_async_remote_copy(
            src_ref=turns[i][0], dst_ref=turns[i][1], send_sem=turn_send.at[i], recv_sem=turn_recv.at[i],
            device_id=partner.id(), device_id_type=MESH)

    def turn_start(i):
        pl.when(gives[i] & alone)(lambda: pltpu.make_async_copy(*turns[i], turn_send.at[i]).start())
        pl.when(gives[i] & pairs)(lambda: turn(i).start())

    def turn_end(i):
        pl.when(gives[i] & alone)(lambda: pltpu.make_async_copy(*turns[i], turn_send.at[i]).wait())
        pl.when(gives[i] & pairs)(lambda: turn(i).wait_send())
        pl.when(takes[i] & pairs)(lambda: turn(i).wait_recv())

    for k in range(len(pieces)):
        pl.when(stays)(lambda: kept(k).start())
        pl.when(moves)(lambda: brought(k, me.dp()).start())
    turn_start(1)
    turn_start(0)
    for i in range(2, 2 + micro):
        turn_start(i)
    for k in range(len(pieces) + 2):
        if k < len(pieces):
            pl.when(stays)(lambda: kept(k).wait())
            pl.when(moves)(lambda: brought(k, own).wait_recv())
            passed(1, k, own, xn).start()
            passed(2, k, own, yn).start()
            passed(4, k, own, cn).start()
        if 0 <= k - 1 < len(pieces):
            passed(1, k - 1, own_x, xn).wait_recv()
            passed(5, k - 1, own_x, cn).start()
            pl.when(me.c == 0)(lambda: passed(3, k - 1, own_x, yn).start())
            passed(2, k - 1, own_y, yn).wait_recv()
            passed(6, k - 1, own_y, cn).start()
            pl.when(me.c == 1)(lambda: passed(3, k - 1, own_y, xn).start())
        if 0 <= k - 2 < len(pieces):
            passed(3, k - 2, own_d, yn).wait_recv()
            passed(7, k - 2, own_d, cn).start()
    for k in range(len(pieces)):
        for kind in range(4, 8):
            passed(kind, k, beside[kind - 4], cn).wait_recv()
        pl.when(moves)(lambda: brought(k, own).wait_send())
        for kind in range(1, 8):
            passed(kind, k, own, cn).wait_send()
    for i in range(len(turns)):
        turn_end(i)


def run_gather(shares, x_first, g, segs):
    pieces = GATHER_PIECES
    micro = g.shape[0]
    shape = jax.ShapeDtypeStruct
    outs = [shape((s.shape[0] * 8,) + s.shape[1:], s.dtype) for s in shares]
    outs += [shape(v.shape, v.dtype) for v in (x_first, g, segs)]
    return pl.pallas_call(
        functools.partial(gather_kernel, pieces, micro),
        out_shape=outs,
        in_specs=[ANYWHERE] * 8,
        out_specs=[ANYWHERE] * 8,
        scratch_shapes=[DMA((8, len(pieces))), DMA((8, len(pieces))), DMA((len(pieces),)), DMA((2 + micro,)),
                        DMA((2 + micro,))],
        compiler_params=pltpu.CompilerParams(collective_id=2, has_side_effects=True),
        name="gather_layers",
    )(*shares, x_first, g, segs)


def scatter_kernel(pieces, micro, *refs):
    count = 5
    totals, gin_in = refs[:count], refs[count]
    outs, gin_o, norm_o = refs[count + 1 : 2 * count + 1], refs[2 * count + 1], refs[2 * count + 2]
    at = 2 * count + 3
    held, beside, diag, from_x, from_y, done, home = (refs[at + i * count : at + (i + 1) * count] for i in range(7))
    sums, tallies, load, send, recv, local, turn_sem, note_send, note_recv, out_sem = refs[at + 7 * count :]
    me = Spot.here()
    xn, yn, cn = me.flip(x=1), me.flip(y=1), me.flip(c=1)
    target, partner = me.source(), me.turned()
    giver = me.drop()
    stays, alone = same(me, target), same(me, partner)
    moves, pairs = jnp.logical_not(stays), jnp.logical_not(alone)
    slab = [me.flip(x=i & 1, y=(i >> 1) & 1, c=i >> 2) for i in range(1, 8)]
    column = [Spot(me.x, me.y, (me.z + i) % 4, me.c) for i in range(1, 4)]
    for spot in slab + column:
        hail(spot)

    @pl.when(moves)
    def _():
        hail(target)
        hail(giver)

    @pl.when(pairs)
    def _():
        hail(partner)

    pl.semaphore_wait(pltpu.get_barrier_semaphore(), 10 + jnp.where(stays, 0, 2) + jnp.where(alone, 0, 1))

    def parts(spot):
        return [s.part() for s in (spot, spot.flip(x=1), spot.flip(y=1), spot.flip(x=1, y=1))]

    kept, given = parts(me), parts(cn)

    def whole(k, part):
        array, first, size = pieces[k]
        share = done[array].shape[0]
        return totals[array].at[pl.ds(pl.multiple_of(part * share + first, 16), size)]

    def span(k):
        return pl.ds(pieces[k][1], pieces[k][2])

    def remote(src, dst, kind, k, spot):
        return pltpu.make_async_remote_copy(
            src_ref=src, dst_ref=dst, send_sem=send.at[kind, k], recv_sem=recv.at[kind, k],
            device_id=spot.id(), device_id_type=MESH)

    def loaded(k, j):
        return pltpu.make_async_copy(whole(k, kept[j]), held[pieces[k][0]].at[j, span(k)], load.at[j, k])

    def crossed(k, j):
        return remote(whole(k, given[j]), beside[pieces[k][0]].at[j, span(k)], j, k, cn)

    def to_diag(k, spot):
        return remote(held[pieces[k][0]].at[3, span(k)], diag[pieces[k][0]].at[span(k)], 4, k, spot)

    def to_x(k):
        return remote(held[pieces[k][0]].at[1, span(k)], from_x[pieces[k][0]].at[span(k)], 5, k, xn)

    def to_y(k):
        return remote(held[pieces[k][0]].at[2, span(k)], from_y[pieces[k][0]].at[span(k)], 6, k, yn)

    def to_home(k):
        return remote(done[pieces[k][0]].at[span(k)], home[pieces[k][0]].at[span(k)], 7, k, target)

    def stay_home(k):
        return pltpu.make_async_copy(done[pieces[k][0]].at[span(k)], home[pieces[k][0]].at[span(k)], local.at[k])

    def add(k, j, extra):
        array = held[pieces[k][0]]
        array[j, span(k)] = (array[j, span(k)].astype(F32) + extra.astype(F32)).astype(array.dtype)

    def turn(m):
        return pltpu.make_async_remote_copy(
            src_ref=gin_in.at[m], dst_ref=gin_o.at[m], send_sem=turn_sem.at[0, m], recv_sem=turn_sem.at[1, m],
            device_id=partner.id(), device_id_type=MESH)

    def turn_stay(m):
        return pltpu.make_async_copy(gin_in.at[m], gin_o.at[m], turn_sem.at[0, m])

    for k in range(len(pieces)):
        for j in (3, 2, 1, 0):
            crossed(k, j).start()
            loaded(k, j).start()
    for m in range(micro):
        pl.when(alone)(lambda: turn_stay(m).start())
        pl.when(pairs)(lambda: turn(m).start())
    for k in range(len(pieces) + 2):
        if k < len(pieces):
            array = pieces[k][0]
            for j in (3, 2, 1, 0):
                loaded(k, j).wait()
                crossed(k, j).wait_recv()
                add(k, j, beside[array][j, span(k)])
                if j == 3:
                    pl.when(me.c == 0)(lambda: to_diag(k, yn).start())
                    pl.when(me.c == 1)(lambda: to_diag(k, xn).start())
                if j == 2:
                    pl.when(me.c == 0)(lambda: to_y(k).start())
                if j == 1:
                    pl.when(me.c == 1)(lambda: to_x(k).start())
        if 0 <= k - 1 < len(pieces):
            b = k - 1
            to_diag(b, yn).wait_recv()

            @pl.when(me.c == 0)
            def _():
                add(b, 1, diag[pieces[b][0]][span(b)])
                to_x(b).start()

            @pl.when(me.c == 1)
            def _():
                add(b, 2, diag[pieces[b][0]][span(b)])
                to_y(b).start()
        if 0 <= k - 2 < len(pieces):
            b = k - 2
            array = pieces[b][0]
            to_x(b).wait_recv()
            to_y(b).wait_recv()
            total = (held[array][0, span(b)].astype(F32) + from_x[array][span(b)].astype(F32)
                     + from_y[array][span(b)].astype(F32))
            done[array][span(b)] = total.astype(done[array].dtype)
            pl.when(stays)(lambda: stay_home(b).start())
            pl.when(moves)(lambda: to_home(b).start())
    tally = jnp.zeros((8, 128), F32)
    for k in range(len(pieces)):
        pl.when(stays)(lambda: stay_home(k).wait())
        pl.when(moves)(lambda: to_home(k).wait_recv())
        array = pieces[k][0]
        value = home[array][span(k)].astype(F32)
        value = value * value
        tally = tally + jnp.sum(value.reshape(-1, 8, value.shape[1] // 128, 128), axis=(0, 2))
    sums[0] = tally

    def note(i, src, slot, spot):
        return pltpu.make_async_remote_copy(
            src_ref=src, dst_ref=tallies.at[slot], send_sem=note_send.at[i], recv_sem=note_recv.at[slot],
            device_id=spot.id(), device_id_type=MESH)

    for i, spot in enumerate(column):
        note(i, sums.at[0], i, spot).start()
    for array in range(count):
        pltpu.make_async_copy(home[array], outs[array], out_sem.at[array]).start()
    for i, spot in enumerate(column):
        note(i, sums.at[0], i, spot).wait_recv()
        tally = tally + tallies[i]
    sums[1] = tally
    for i, spot in enumerate(slab):
        note(3 + i, sums.at[1], 3 + i, spot).start()
    for i, spot in enumerate(slab):
        note(3 + i, sums.at[1], 3 + i, spot).wait_recv()
        tally = tally + tallies[3 + i]
    norm_o[...] = tally
    for i, spot in enumerate(column):
        note(i, sums.at[0], i, spot).wait_send()
    for i, spot in enumerate(slab):
        note(3 + i, sums.at[1], 3 + i, spot).wait_send()
    for k in range(len(pieces)):
        for j in range(4):
            crossed(k, j).wait_send()
        to_diag(k, yn).wait_send()
        to_x(k).wait_send()
        to_y(k).wait_send()
        pl.when(moves)(lambda: to_home(k).wait_send())
    for m in range(micro):
        pl.when(alone)(lambda: turn_stay(m).wait())
        pl.when(pairs)(lambda: turn(m).wait())
    for array in range(count):
        pltpu.make_async_copy(home[array], outs[array], out_sem.at[array]).wait()


def run_scatter(totals, gin):
    pieces = SCATTER_PIECES
    micro = gin.shape[0]
    shape = jax.ShapeDtypeStruct
    shares = [((t.shape[0] // 8, t.shape[1]), t.dtype) for t in totals]
    four = [pltpu.VMEM((4,) + s, t) for s, t in shares]
    one = [pltpu.VMEM(s, t) for s, t in shares]
    return pl.pallas_call(
        functools.partial(scatter_kernel, pieces, micro),
        out_shape=[shape(s, t) for s, t in shares] + [shape(gin.shape, gin.dtype), shape((8, 128), F32)],
        in_specs=[ANYWHERE] * 6,
        out_specs=[ANYWHERE] * 6 + [IN_VMEM],
        scratch_shapes=four + four + one * 5
        + [pltpu.VMEM((2, 8, 128), F32), pltpu.VMEM((10, 8, 128), F32), DMA((4, len(pieces))), DMA((8, len(pieces))),
           DMA((8, len(pieces))), DMA((len(pieces),)), DMA((2, micro)), DMA((10,)), DMA((10,)), DMA((5,))],
        compiler_params=pltpu.CompilerParams(collective_id=3, has_side_effects=True, vmem_limit_bytes=VMEM_CAP),
        name="scatter_layers",
    )(*totals, gin)


def split_small(small, width, slices):
    share = width // slices
    stacked = small.reshape(slices, small.shape[0] // slices)
    eight = stacked[:, : 8 * share].reshape(slices, 8, share).transpose(1, 0, 2).reshape(8, width)
    up = stacked[:, 8 * share :].reshape(-1, width)
    return jnp.concatenate([eight, up, jnp.zeros((16 - 8 - up.shape[0], width), small.dtype)], axis=0)


def join_small(table, total, slices):
    width = table.shape[1]
    share = width // slices
    ups = total // width - 8
    eight = table[:8].reshape(8, slices, share).transpose(1, 0, 2).reshape(slices, 8 * share)
    up = table[8 : 8 + ups].reshape(slices, -1)
    return jnp.concatenate([eight, up], axis=1).reshape(-1)


def weight_grad(left, right):
    rows = left.shape[0] * left.shape[1]
    return lax.dot_general(left.reshape(rows, -1), right.reshape(rows, -1), (((0,), (0,)), ((), ())),
                           preferred_element_type=F32)


def per_device(inputs, out_grad, segment_ids, cls_index, *states):
    masters, firsts, seconds = states[0:5], states[5:10], states[10:15]
    slices = lax.axis_size("dp")
    stages = lax.axis_size("section")
    turned = slices == 8 and stages == 4
    seq_dev, length, width = inputs.shape
    rows = -(-length // 128) * 128
    total = masters[4].shape[1] * slices

    extra = ((0, 0), (0, rows - length), (0, 0))
    x_in = jnp.pad(inputs, extra)
    g_in = jnp.pad(out_grad, extra)
    segs = jnp.pad(segment_ids, ((0, 0), (0, rows - length)), constant_values=-1)
    shares = [m.astype(BF)[0] for m in masters]
    if turned:
        line = Line("dp", 4, 2)
        lanes = masters[4].shape[1] // 128
        shares[4] = jnp.pad(shares[4].astype(F32).reshape(lanes, 128), ((0, 16 - lanes), (0, 0)))
        words = jnp.concatenate([segs, jnp.broadcast_to(cls_index[:, None], (seq_dev, rows))], axis=0)
        *gathered, x_first, g_in, words = run_gather(shares, x_in[0], g_in, words)
        segs, classes = words[:seq_dev], words[seq_dev:, 0]
        flat = gathered[4].reshape(slices, 16, 128)[:, :lanes].reshape(-1)
    else:
        line = Line("section", stages, 1)
        gathered = [lax.all_gather(s, "dp", axis=0, tiled=True) for s in shares]
        flat, classes, x_first = gathered[4].astype(F32), cls_index, x_in[0]
    weights = gathered[:4]
    small = split_small(flat, width, slices)
    segr, segc = segs[:, None, :], segs[:, :, None]

    x, a, qkv, lse, o, h, a2, gp, u, acts = run_forward(
        line, length, turned, x_first, x_in, segr, segc, classes, weights, small)
    acts, g, dz, f, r, gin, sums = run_backward(
        line, length, turned, acts, g_in, x, qkv, lse, h, gp, segr, segc, classes, weights, small)
    totals = [weight_grad(a, r).astype(BF), weight_grad(o, f).astype(BF), weight_grad(a2, dz).astype(BF),
              weight_grad(u, g).astype(BF), join_small(sums, total, slices)]
    if turned:
        table = jnp.pad(totals[4].reshape(slices, lanes, 128), ((0, 0), (0, 16 - lanes), (0, 0)))
        *shards, gin, tally = run_scatter(totals[:4] + [table.reshape(slices * 16, 128)], gin)
        shards[4] = shards[4][:lanes].reshape(-1)
        shards = [s.astype(F32)[None] for s in shards]
        grad_norm = jnp.sqrt(jnp.sum(tally))
    else:
        shards = [lax.psum_scatter(t[None], "dp", scatter_dimension=1, tiled=True).astype(F32) for t in totals]
        squares = jnp.sum(jnp.stack([jnp.sum(s * s) for s in shards]))
        grad_norm = jnp.sqrt(lax.psum(squares, ("dp", "section")))
    factor = 1.0 / jnp.maximum(grad_norm, 1.0)
    fix = 1.0 - 0.5**STEP
    results = []
    for kind in range(5):
        grad = shards[kind] * factor
        first = 0.5 * firsts[kind] + 0.5 * grad
        second = 0.5 * seconds[kind] + 0.5 * grad * grad
        update = first / fix / (jnp.sqrt(second / fix) + adam_eps)
        rate = small_rate
        if kind < 4:
            update = update + decay_rate * masters[kind]
            rate = learn_rate
        results += [grad, masters[kind] - rate * update, first, second]
    return (acts[:, :length][None], gin[:, :length][None], grad_norm.reshape(1)) + tuple(results)


def solution(mesh):
    matrix, vector = P("section", "dp", None), P("section", "dp")
    states = (matrix,) * 4 + (vector,)
    return jax.shard_map(
        per_device,
        mesh=mesh,
        in_specs=(P("dp", None, None), P("dp", None, None), P("dp", None), P("dp")) + states * 3,
        out_specs=(P("section", "dp", None, None), P("section", "dp", None, None), P())
        + (matrix,) * 16 + (vector,) * 4,
        check_vma=False,
    )
```

```python
import functools

import jax
import jax.numpy as jnp
from jax import lax
from jax.experimental import pallas as pl
from jax.experimental.pallas import tpu as pltpu
from jax.sharding import PartitionSpec as P

HEADS = 12
STEP = 3
F32 = jnp.float32
BF = jnp.bfloat16
MESH = pl.DeviceIdType.MESH
VMEM_CAP = 60 * 1024 * 1024

norm_eps = 1e-06
masked_score = -1e30
learn_rate = 0.05
small_rate = 0.3
decay_rate = 0.05
adam_eps = 1e-08

NT = (((1,), (1,)), ((), ()))
TN = (((0,), (0,)), ((), ()))


def mm(a, b):
    return jnp.dot(a, b, preferred_element_type=F32)


def mm_nt(a, b):
    return lax.dot_general(a, b, NT, preferred_element_type=F32)


def norm_parts(values):
    center = values - jnp.mean(values, axis=-1, keepdims=True)
    spread = jnp.mean(center * center, axis=-1, keepdims=True)
    inv = lax.rsqrt(spread + norm_eps)
    return center * inv, inv


def norm_back(y, normed, inv):
    pull = jnp.mean(y * normed, axis=-1, keepdims=True)
    return (y - jnp.mean(y, axis=-1, keepdims=True) - normed * pull) * inv


def column_sum(values):
    return jnp.sum(values, axis=0, keepdims=True)


def mask_bias(seg_row, seg_col, cls, length):
    size = seg_col.shape[0]
    key_at = lax.broadcasted_iota(jnp.int32, (size, size), 0)
    query_at = lax.broadcasted_iota(jnp.int32, (size, size), 1)
    allowed = (seg_row == seg_col) | (key_at == cls) | (query_at == cls)
    allowed = allowed & (key_at < length)
    return jnp.where(allowed, 0.0, masked_score).astype(F32)


def gelu_parts(z):
    density = jnp.exp(z * z * -0.5) * 0.3989422804014327
    below = 0.5 + 0.5 * lax.erf(z * 0.7071067811865476)
    return z * below, below + z * density


def layer_forward(x_ref, bias_ref, wqkv, wproj, wup, wdown, small, a_ref, qkv_ref, lse_ref, o_ref,
                  h_ref, a2_ref, gp_ref, u_ref, out_ref, ot_ref, before_up):
    rows, width = x_ref.shape
    hidden = wup.shape[1]
    normed, _ = norm_parts(x_ref[...].astype(F32))
    a_ref[...] = (normed * small[0:1, :] + small[1:2, :]).astype(BF)
    for part in range(3):
        cols = slice(part * width, (part + 1) * width)
        mixed = mm(a_ref[...], wqkv[:, cols])
        if part == 0:
            mixed = mixed + small[2:3, :]
        if part == 2:
            mixed = mixed + small[3:4, :]
        qkv_ref[:, cols] = mixed.astype(BF)
    lane = lax.broadcasted_iota(jnp.int32, (rows, 128), 1)
    for pair in range(HEADS // 2):
        q = qkv_ref[:, pair * 128 : pair * 128 + 128]
        k = qkv_ref[:, width + pair * 128 : width + pair * 128 + 128]
        vt = qkv_ref[:, 2 * width + pair * 128 : 2 * width + pair * 128 + 128].T
        for side in range(2):
            half = (lane < 64) if side == 0 else (lane >= 64)
            k_half = jnp.where(half, k, jnp.zeros_like(k))
            scores = mm_nt(k_half, q) * 0.125 + bias_ref[...]
            peak = jnp.max(scores, axis=0, keepdims=True)
            raised = jnp.exp(scores - peak)
            summed = jnp.sum(raised, axis=0, keepdims=True)
            mixed = mm(vt[side * 64 : side * 64 + 64, :], raised.astype(BF)) * (1.0 / summed)
            at = pair * 128 + side * 64
            ot_ref[at : at + 64, :] = mixed.astype(BF)
            head = 2 * pair + side
            lse_ref[head : head + 1, :] = peak + jnp.log(summed)
    o_ref[...] = ot_ref[...].T
    h = x_ref[...].astype(F32) + (mm(o_ref[...], wproj[...]) + small[4:5, :])
    h_ref[...] = h
    normed, _ = norm_parts(h)
    a2_ref[...] = (normed * small[5:6, :] + small[6:7, :]).astype(BF)
    before_up()
    for part in range(hidden // width):
        cols = slice(part * width, (part + 1) * width)
        z = mm(a2_ref[...], wup[:, cols]) + small[8 + part : 9 + part, :]
        u, slope = gelu_parts(z)
        u_ref[:, cols] = u.astype(BF)
        gp_ref[:, cols] = slope.astype(BF)
    out_ref[...] = (h_ref[...] + (mm(u_ref[...], wdown[...]) + small[7:8, :])).astype(BF)


def layer_backward(g_ref, x_ref, bias_ref, qkv_ref, lse_ref, h_ref, gp_ref, wqkv, wproj, wup, wdown,
                   small, dz_ref, f_ref, r_ref, gin_ref, sums_ref, do_ref, dh_ref, dqt_ref):
    rows, width = x_ref.shape
    hidden = wup.shape[1]
    carried = g_ref[...].astype(F32)
    sums_ref[7:8, :] += column_sum(carried)
    for part in range(hidden // width):
        cols = slice(part * width, (part + 1) * width)
        back = mm_nt(g_ref[...], wdown[cols, :])
        dz = (back * gp_ref[:, cols].astype(F32)).astype(BF)
        dz_ref[:, cols] = dz
        sums_ref[8 + part : 9 + part, :] += column_sum(dz.astype(F32))
    back = mm_nt(dz_ref[...], wup[...])
    normed, inv = norm_parts(h_ref[...])
    sums_ref[5:6, :] += column_sum(back * normed)
    sums_ref[6:7, :] += column_sum(back)
    dh = carried + norm_back(back * small[5:6, :], normed, inv)
    dh_ref[...] = dh
    f = dh.astype(BF)
    f_ref[...] = f
    sums_ref[4:5, :] += column_sum(f.astype(F32))
    do_ref[...] = mm_nt(f_ref[...], wproj[...]).astype(BF)
    lane = lax.broadcasted_iota(jnp.int32, (rows, 128), 1)
    for pair in range(HEADS // 2):
        q = qkv_ref[:, pair * 128 : pair * 128 + 128]
        k = qkv_ref[:, width + pair * 128 : width + pair * 128 + 128]
        v = qkv_ref[:, 2 * width + pair * 128 : 2 * width + pair * 128 + 128]
        do = do_ref[:, pair * 128 : pair * 128 + 128]
        kt = k.T
        dv_sides = []
        dk_sides = []
        for side in range(2):
            half = (lane < 64) if side == 0 else (lane >= 64)
            k_half = jnp.where(half, k, jnp.zeros_like(k))
            v_half = jnp.where(half, v, jnp.zeros_like(v))
            head = 2 * pair + side
            scores = mm_nt(k_half, q) * 0.125 + bias_ref[...]
            probs = jnp.exp(scores - lse_ref[head : head + 1, :])
            dv_sides.append(mm(probs.astype(BF), do))
            dp = mm_nt(v_half, do)
            inner = jnp.sum(probs * dp, axis=0, keepdims=True)
            ds = (probs * (dp - inner)).astype(BF)
            dk_sides.append(mm(ds, q))
            at = pair * 128 + side * 64
            dqt_ref[at : at + 64, :] = (mm(kt[side * 64 : side * 64 + 64, :], ds) * 0.125).astype(BF)
        at = width + pair * 128
        r_ref[:, at : at + 128] = (jnp.where(lane < 64, dk_sides[0], dk_sides[1]) * 0.125).astype(BF)
        at = 2 * width + pair * 128
        r_ref[:, at : at + 128] = jnp.where(lane < 64, dv_sides[0], dv_sides[1]).astype(BF)
    r_ref[:, 0:width] = dqt_ref[...].T
    sums_ref[2:3, :] += column_sum(r_ref[:, 0:width].astype(F32))
    sums_ref[3:4, :] += column_sum(r_ref[:, 2 * width :].astype(F32))
    back = mm_nt(r_ref[...], wqkv[...])
    normed, inv = norm_parts(x_ref[...].astype(F32))
    sums_ref[0:1, :] += column_sum(back * normed)
    sums_ref[1:2, :] += column_sum(back)
    gin_ref[...] = (dh_ref[...] + norm_back(back * small[0:1, :], normed, inv)).astype(BF)


class Line:
    def __init__(self, axis, count, stride):
        self.axis, self.count, self.stride = axis, count, stride

    def stage(self):
        return lax.axis_index(self.axis) // self.stride

    def beside(self, by):
        return {self.axis: lax.axis_index(self.axis) + by * self.stride}


class Spot:
    def __init__(self, x, y, z, c):
        self.x, self.y, self.z, self.c = x, y, z, c

    @staticmethod
    def here():
        dp, section = lax.axis_index("dp"), lax.axis_index("section")
        return Spot(dp % 2, section // 2, dp // 2, section % 2)

    def dp(self):
        return self.z * 2 + self.x

    def section(self):
        return self.y * 2 + self.c

    def id(self):
        return (self.dp(), self.section())

    def flip(self, x=0, y=0, c=0):
        return Spot(1 - self.x if x else self.x, 1 - self.y if y else self.y, self.z, 1 - self.c if c else self.c)

    def ahead(self):
        return Spot(self.x, self.z % 2, self.section(), self.z // 2)

    def back(self):
        return Spot(self.x, self.z // 2, 2 * self.c + self.y, self.z % 2)

    def crosses(self):
        return (self.z + self.c) % 2 == 1

    def drop(self):
        return Spot(self.x, self.y, 2 * ((self.y + self.z + self.c) % 2) + self.c, self.z // 2)

    def source(self):
        c = self.z % 2
        return Spot(self.x, self.y, 2 * self.c + (self.y + self.z // 2 + c) % 2, c)

    def part(self):
        return self.source().dp()


def same(one, other):
    return (one.dp() == other.dp()) & (one.section() == other.section())


def hail(spot):
    pl.semaphore_signal(pltpu.get_barrier_semaphore(), inc=1, device_id=spot.id(), device_id_type=MESH)


def greet(line, turned):
    stage = line.stage()
    barrier = pltpu.get_barrier_semaphore()

    @pl.when(stage > 0)
    def _():
        pl.semaphore_signal(barrier, inc=1, device_id=line.beside(-1), device_id_type=MESH)

    @pl.when(stage < line.count - 1)
    def _():
        pl.semaphore_signal(barrier, inc=1, device_id=line.beside(1), device_id_type=MESH)

    expected = jnp.where(stage > 0, 1, 0) + jnp.where(stage < line.count - 1, 1, 0)
    if turned:
        me = Spot.here()
        alone = same(me, me.back())

        @pl.when(jnp.logical_not(alone))
        def _():
            hail(me.back())
            hail(me.ahead())

        expected = expected + jnp.where(alone, 0, 2)
    pl.semaphore_wait(barrier, expected)


def forward_kernel(line, length, turned, x_first, x_in, segr, segc, cls, wqkv_h, wproj_h, wup_h, wdown_h, small,
                   x_o, a_o, qkv_o, lse_o, o_o, h_o, a2_o, gp_o, u_o, acts_o, home_o,
                   wqkv, wproj, wup, wdown, xs, outs, a, qkv, lse, o, h, a2, gp, u, bias, ot,
                   w_sem, in_sem, x_sem, save_sem, act_sem, send_sem, recv_sem, home_sem):
    micro = xs.shape[0]
    stage = line.stage()
    loads = [
        pltpu.make_async_copy(src, dst, w_sem.at[i])
        for i, (src, dst) in enumerate(((wqkv_h, wqkv), (wproj_h, wproj), (wup_h, wup), (wdown_h, wdown)))
    ]
    for load in loads:
        load.start()

    def first_in(m):
        return pltpu.make_async_copy(x_in.at[m], xs.at[m], in_sem.at[m])

    greet(line, turned)
    if turned:
        me = Spot.here()
        ahead, back = me.ahead(), me.back()
        alone = same(me, back)

        def turn_in(m):
            return pltpu.make_async_remote_copy(
                src_ref=x_in.at[m], dst_ref=xs.at[m], send_sem=in_sem.at[m], recv_sem=recv_sem.at[m],
                device_id=ahead.id(), device_id_type=MESH)

        feeds = jnp.logical_and(me.section() == 0, jnp.logical_not(alone))
        fed = jnp.logical_and(stage == 0, jnp.logical_not(alone))
        feeds_self = jnp.logical_and(stage == 0, alone)
        homing = jnp.logical_and(stage >= 2, jnp.logical_not(alone))
        homed = jnp.logical_and(me.section() >= 2, jnp.logical_not(alone))
        settled = jnp.logical_and(stage >= 2, alone)

        def home(m):
            return pltpu.make_async_remote_copy(
                src_ref=outs.at[m], dst_ref=home_o.at[m], send_sem=home_sem.at[0, m], recv_sem=home_sem.at[1, m],
                device_id=back.id(), device_id_type=MESH)

        def settle(m):
            return pltpu.make_async_copy(outs.at[m], home_o.at[m], home_sem.at[0, m])

        @pl.when(stage == 0)
        def _():
            pltpu.make_async_copy(x_first, xs.at[0], in_sem.at[0]).start()

        for m in range(1, micro):
            @pl.when(feeds)
            def _():
                turn_in(m).start()

            @pl.when(feeds_self)
            def _():
                first_in(m).start()
    else:
        @pl.when(stage == 0)
        def _():
            for m in range(micro):
                first_in(m).start()

    saved = ((a, a_o), (qkv, qkv_o), (lse, lse_o), (o, o_o), (h, h_o), (a2, a2_o), (gp, gp_o), (u, u_o))

    def saves(m, slot):
        return [
            pltpu.make_async_copy(here.at[slot], there.at[m], save_sem.at[slot, i])
            for i, (here, there) in enumerate(saved)
        ]

    def hop(m):
        return pltpu.make_async_remote_copy(
            src_ref=outs.at[m], dst_ref=xs.at[m], send_sem=send_sem.at[m], recv_sem=recv_sem.at[m],
            device_id=line.beside(1), device_id_type=MESH)

    def step(m, carry):
        slot = lax.rem(m, 2)

        if turned:
            here = jnp.logical_or(feeds_self, jnp.logical_and(stage == 0, m == 0))
        else:
            here = stage == 0

        @pl.when(here)
        def _():
            first_in(m).wait()

        @pl.when(jnp.logical_not(here))
        def _():
            hop(m).wait_recv()

        pltpu.make_async_copy(xs.at[m], x_o.at[m], x_sem.at[m]).start()

        @pl.when(m >= 2)
        def _():
            for save in saves(m - 2, slot):
                save.wait()

        @pl.when(m == 0)
        def _():
            loads[0].wait()
            loads[1].wait()

        bias[...] = mask_bias(segr[m], segc[m], cls[m], length)

        def before_up():
            @pl.when(m == 0)
            def _():
                loads[2].wait()
                loads[3].wait()

        layer_forward(xs.at[m], bias, wqkv, wproj, wup, wdown, small, a.at[slot], qkv.at[slot],
                      lse.at[slot], o.at[slot], h.at[slot], a2.at[slot], gp.at[slot], u.at[slot],
                      outs.at[m], ot, before_up)

        @pl.when(stage < line.count - 1)
        def _():
            hop(m).start()

        for save in saves(m, slot):
            save.start()
        pltpu.make_async_copy(outs.at[m], acts_o.at[m], act_sem.at[m]).start()
        if turned:
            pl.when(homing & (m < micro - 1))(lambda: home(m).start())
            pl.when(settled & (m < micro - 1))(lambda: settle(m).start())
        return carry

    lax.fori_loop(0, micro, step, 0)

    for m in range(max(micro - 2, 0), micro):
        for save in saves(m, m % 2):
            save.wait()
    for m in range(micro):
        pltpu.make_async_copy(xs.at[m], x_o.at[m], x_sem.at[m]).wait()
        pltpu.make_async_copy(outs.at[m], acts_o.at[m], act_sem.at[m]).wait()

    @pl.when(stage < line.count - 1)
    def _():
        for m in range(micro):
            hop(m).wait_send()

    if turned:
        @pl.when(feeds)
        def _():
            for m in range(1, micro):
                turn_in(m).wait_send()

        for m in range(micro - 1):
            pl.when(homing)(lambda: home(m).wait_send())
            pl.when(homed)(lambda: home(m).wait_recv())
            pl.when(settled)(lambda: settle(m).wait())


def backward_kernel(line, length, turned, acts_h, g_in, x_h, qkv_h, lse_h, h_h, gp_h, segr, segc, cls,
                    wqkv_h, wproj_h, wup_h, wdown_h, small,
                    acts_o, home_o, g_o, dz_o, f_o, r_o, gin_o, sums_o,
                    wqkv, wproj, wup, wdown, gs, gins, x, qkv, lse, h, gp, dz, f, r, bias, do, dh, dqt,
                    w_sem, in_sem, g_sem, load_sem, save_sem, act_sem, send_sem, recv_sem, home_sem, back_sem):
    micro = gs.shape[0]
    stage = line.stage()
    loads = [
        pltpu.make_async_copy(src, dst, w_sem.at[i])
        for i, (src, dst) in enumerate(((wdown_h, wdown), (wup_h, wup), (wproj_h, wproj), (wqkv_h, wqkv)))
    ]

    def last_in(m):
        return pltpu.make_async_copy(g_in.at[m], gs.at[m], in_sem.at[m])

    @pl.when(stage == line.count - 1)
    def _():
        for m in range(micro):
            last_in(m).start()

    kept = ((gp_h, gp), (h_h, h), (qkv_h, qkv), (lse_h, lse), (x_h, x))

    def fetches(m, slot):
        return [
            pltpu.make_async_copy(there.at[m], here.at[slot], load_sem.at[slot, i])
            for i, (there, here) in enumerate(kept)
        ]

    loads[0].start()
    for fetch in fetches(0, 0):
        fetch.start()
    for load in loads[1:]:
        load.start()
    sums_o[...] = jnp.zeros_like(sums_o)
    greet(line, turned)
    if turned:
        me = Spot.here()
        back = me.back()
        alone = same(me, back)

        def home(m):
            return pltpu.make_async_remote_copy(
                src_ref=acts_h.at[m], dst_ref=acts_o.at[m], send_sem=home_sem.at[0, m], recv_sem=home_sem.at[1, m],
                device_id=back.id(), device_id_type=MESH)

        def stay(m):
            return pltpu.make_async_copy(acts_h.at[m], acts_o.at[m], home_sem.at[0, m])

        pairs = jnp.logical_not(alone)
        low, low_home = stage < 2, me.section() < 2

        def home_back(m):
            return pltpu.make_async_remote_copy(
                src_ref=gins.at[m], dst_ref=home_o.at[m], send_sem=back_sem.at[0, m], recv_sem=back_sem.at[1, m],
                device_id=back.id(), device_id_type=MESH)

        def settle_back(m):
            return pltpu.make_async_copy(gins.at[m], home_o.at[m], back_sem.at[0, m])

        for m in range(micro):
            now = low | (m == micro - 1)
            pl.when(alone & now)(lambda: stay(m).start())
            pl.when(pairs & now)(lambda: home(m).start())
    else:
        for m in range(micro):
            pltpu.make_async_copy(acts_h.at[m], acts_o.at[m], home_sem.at[0, m]).start()

    saved = ((dz, dz_o), (f, f_o), (r, r_o))

    def saves(m, slot):
        return [
            pltpu.make_async_copy(here.at[slot], there.at[m], save_sem.at[slot, i])
            for i, (here, there) in enumerate(saved)
        ]

    def hop(m):
        return pltpu.make_async_remote_copy(
            src_ref=gins.at[m], dst_ref=gs.at[m], send_sem=send_sem.at[m], recv_sem=recv_sem.at[m],
            device_id=line.beside(-1), device_id_type=MESH)

    def step(m, carry):
        slot = lax.rem(m, 2)

        @pl.when(m + 1 < micro)
        def _():
            for fetch in fetches(m + 1, 1 - slot):
                fetch.start()

        @pl.when(m == 0)
        def _():
            for load in loads:
                load.wait()

        for fetch in fetches(m, slot):
            fetch.wait()
        bias[...] = mask_bias(segr[m], segc[m], cls[m], length)

        @pl.when(m >= 2)
        def _():
            for save in saves(m - 2, slot):
                save.wait()

        @pl.when(stage == line.count - 1)
        def _():
            last_in(m).wait()

        @pl.when(stage < line.count - 1)
        def _():
            hop(m).wait_recv()

        pltpu.make_async_copy(gs.at[m], g_o.at[m], g_sem.at[m]).start()
        layer_backward(gs.at[m], x.at[slot], bias, qkv.at[slot], lse.at[slot], h.at[slot], gp.at[slot],
                       wqkv, wproj, wup, wdown, small, dz.at[slot], f.at[slot], r.at[slot], gins.at[m],
                       sums_o, do, dh, dqt)

        @pl.when(stage > 0)
        def _():
            hop(m).start()

        for save in saves(m, slot):
            save.start()
        pltpu.make_async_copy(gins.at[m], gin_o.at[m], act_sem.at[m]).start()
        if turned:
            pl.when(pairs & low & (m < micro - 1))(lambda: home_back(m).start())
            pl.when(alone & low & (m < micro - 1))(lambda: settle_back(m).start())
        return carry

    lax.fori_loop(0, micro, step, 0)

    for m in range(max(micro - 2, 0), micro):
        for save in saves(m, m % 2):
            save.wait()
    for m in range(micro):
        pltpu.make_async_copy(gs.at[m], g_o.at[m], g_sem.at[m]).wait()
        pltpu.make_async_copy(gins.at[m], gin_o.at[m], act_sem.at[m]).wait()

    @pl.when(stage > 0)
    def _():
        for m in range(micro):
            hop(m).wait_send()

    for m in range(micro):
        if turned:
            now, then = low | (m == micro - 1), low_home | (m == micro - 1)
            pl.when(alone & now)(lambda: stay(m).wait())
            pl.when(pairs & now)(lambda: home(m).wait_send())
            pl.when(pairs & then)(lambda: home(m).wait_recv())
            if m < micro - 1:
                pl.when(pairs & low)(lambda: home_back(m).wait_send())
                pl.when(pairs & low_home)(lambda: home_back(m).wait_recv())
                pl.when(alone & low)(lambda: settle_back(m).wait())
        else:
            pltpu.make_async_copy(acts_h.at[m], acts_o.at[m], home_sem.at[0, m]).wait()


IN_VMEM = pl.BlockSpec(memory_space=pltpu.VMEM)
IN_SMEM = pl.BlockSpec(memory_space=pltpu.SMEM)
ANYWHERE = pl.BlockSpec(memory_space=pl.ANY)
DMA = pltpu.SemaphoreType.DMA


def run_forward(line, length, turned, x_first, x_in, segr, segc, cls, weights, small):
    micro, rows, width = x_in.shape
    hidden = weights[2].shape[1]
    shape = jax.ShapeDtypeStruct
    saved = (
        ((rows, width), BF), ((rows, 3 * width), BF), ((16, rows), F32), ((rows, width), BF),
        ((rows, width), F32), ((rows, width), BF), ((rows, hidden), BF), ((rows, hidden), BF))
    many = shape((micro, rows, width), BF)
    return pl.pallas_call(
        functools.partial(forward_kernel, line, length, turned),
        out_shape=[many] + [shape((micro,) + s, t) for s, t in saved] + [many, many],
        in_specs=[ANYWHERE, ANYWHERE, IN_VMEM, IN_VMEM, IN_SMEM] + [ANYWHERE] * 4 + [IN_VMEM],
        out_specs=[ANYWHERE] * 11,
        scratch_shapes=[pltpu.VMEM(w.shape, BF) for w in weights]
        + [pltpu.VMEM((micro, rows, width), BF)] * 2
        + [pltpu.VMEM((2,) + s, t) for s, t in saved]
        + [pltpu.VMEM((rows, rows), F32), pltpu.VMEM((width, rows), BF)]
        + [DMA((4,)), DMA((micro,)), DMA((micro,)), DMA((2, 8)), DMA((micro,)), DMA((micro,)), DMA((micro,)),
           DMA((2, micro))],
        compiler_params=pltpu.CompilerParams(
            collective_id=0, has_side_effects=True, vmem_limit_bytes=VMEM_CAP),
        name="forward_line",
    )(x_first, x_in, segr, segc, cls, *weights, small)


def run_backward(line, length, turned, acts, g_in, x, qkv, lse, h, gp, segr, segc, cls, weights, small):
    micro, rows, width = g_in.shape
    hidden = weights[2].shape[1]
    shape = jax.ShapeDtypeStruct
    many = shape((micro, rows, width), BF)
    wqkv, wproj, wup, wdown = weights
    return pl.pallas_call(
        functools.partial(backward_kernel, line, length, turned),
        out_shape=[many, many, many, shape((micro, rows, hidden), BF), many, shape((micro, rows, 3 * width), BF), many,
                   shape((16, width), F32)],
        in_specs=[ANYWHERE] * 7 + [IN_VMEM, IN_VMEM, IN_SMEM] + [ANYWHERE] * 4 + [IN_VMEM],
        out_specs=[ANYWHERE] * 7 + [IN_VMEM],
        scratch_shapes=[pltpu.VMEM(w.shape, BF) for w in weights]
        + [pltpu.VMEM((micro, rows, width), BF)] * 2
        + [pltpu.VMEM((2, rows, width), BF), pltpu.VMEM((2, rows, 3 * width), BF), pltpu.VMEM((2, 16, rows), F32),
           pltpu.VMEM((2, rows, width), F32), pltpu.VMEM((2, rows, hidden), BF),
           pltpu.VMEM((2, rows, hidden), BF), pltpu.VMEM((2, rows, width), BF), pltpu.VMEM((2, rows, 3 * width), BF),
           pltpu.VMEM((rows, rows), F32), pltpu.VMEM((rows, width), BF), pltpu.VMEM((rows, width), F32),
           pltpu.VMEM((width, rows), BF)]
        + [DMA((4,)), DMA((micro,)), DMA((micro,)), DMA((2, 5)), DMA((2, 3)), DMA((micro,)), DMA((micro,)),
           DMA((micro,)), DMA((2, micro)), DMA((2, micro))],
        compiler_params=pltpu.CompilerParams(
            collective_id=1, has_side_effects=True, vmem_limit_bytes=VMEM_CAP),
        name="backward_line",
    )(acts, g_in, x, qkv, lse, h, gp, segr, segc, cls, wqkv, wproj, wup, wdown, small)


GATHER_PIECES = ((0, 0, 48, "c"), (0, 48, 48, "x"), (4, 0, 16, "x"), (1, 0, 96, "c"), (2, 0, 48, "x"), (2, 48, 48, "c"),
                 (3, 0, 192, "x"), (3, 192, 192, "c"))


def gather_kernel(pieces, micro, *refs):
    count = 5
    shares, (x_in, g_in, seg_in) = refs[:count], refs[count : count + 3]
    wholes, (x_o, g_o, seg_o) = refs[count + 3 : 2 * count + 3], refs[2 * count + 3 : 2 * count + 6]
    swap, (send, recv, local, turn_send, turn_recv) = refs[2 * count + 6 : 3 * count + 6], refs[3 * count + 6 :]
    me = Spot.here()
    xn, yn, cn = me.flip(x=1), me.flip(y=1), me.flip(c=1)
    target, source, ahead, back = me.drop(), me.source(), me.ahead(), me.back()
    stays, alone = same(me, target), same(me, back)
    moves, pairs = jnp.logical_not(stays), jnp.logical_not(alone)
    crosses = me.crosses()
    direct = jnp.logical_and(moves, jnp.logical_not(crosses))
    for spot in (xn, yn, cn):
        hail(spot)

    @pl.when(moves)
    def _():
        hail(target)
        hail(source)

    @pl.when(pairs)
    def _():
        hail(ahead)
        hail(back)

    pl.semaphore_wait(pltpu.get_barrier_semaphore(), 3 + jnp.where(stays, 0, 2) + jnp.where(alone, 0, 2))

    def rows(k, part):
        array, first, size, _ = pieces[k]
        share = shares[array].shape[0]
        return wholes[array].at[pl.ds(pl.multiple_of(part * share + first, 16), size)]

    def mine(k):
        array, first, size, _ = pieces[k]
        return shares[array].at[pl.ds(first, size)]

    def swapped(k):
        array, first, size, _ = pieces[k]
        return swap[array].at[pl.ds(first, size)]

    def remote(src, dst, kind, k, spot):
        return pltpu.make_async_remote_copy(
            src_ref=src, dst_ref=dst, send_sem=send.at[kind, k], recv_sem=recv.at[kind, k],
            device_id=spot.id(), device_id_type=MESH)

    def crossed(k):
        return remote(mine(k), swapped(k), 8, k, yn)

    def brought(k, part):
        return remote(mine(k), rows(k, part), 0, k, target)

    def brought_on(k, part):
        return remote(swapped(k), rows(k, part), 0, k, target)

    def kept(k):
        return pltpu.make_async_copy(mine(k), rows(k, me.dp()), local.at[k])

    def passed(kind, k, part, spot):
        return remote(rows(k, part), rows(k, part), kind, k, spot)

    def parts(spot):
        return [s.part() for s in (spot, spot.flip(x=1), spot.flip(y=1), spot.flip(x=1, y=1))]

    own, own_x, own_y, own_d = parts(me)
    beside = parts(cn)
    turns = [(x_in, x_o), (seg_in, seg_o)] + [(g_in.at[m], g_o.at[m]) for m in range(micro)]
    gives = [me.section() == 0, me.section() >= 0] + [me.section() == 3] * micro
    takes = [me.z == 0, me.z >= 0] + [me.z == 3] * micro

    def turn(i):
        return pltpu.make_async_remote_copy(
            src_ref=turns[i][0], dst_ref=turns[i][1], send_sem=turn_send.at[i], recv_sem=turn_recv.at[i],
            device_id=ahead.id(), device_id_type=MESH)

    def turn_start(i):
        pl.when(gives[i] & alone)(lambda: pltpu.make_async_copy(*turns[i], turn_send.at[i]).start())
        pl.when(gives[i] & pairs)(lambda: turn(i).start())

    def turn_end(i):
        pl.when(gives[i] & alone)(lambda: pltpu.make_async_copy(*turns[i], turn_send.at[i]).wait())
        pl.when(gives[i] & pairs)(lambda: turn(i).wait_send())
        pl.when(takes[i] & pairs)(lambda: turn(i).wait_recv())

    for k in range(len(pieces)):
        pl.when(stays)(lambda: kept(k).start())
        pl.when(direct)(lambda: brought(k, me.dp()).start())
        pl.when(crosses)(lambda: crossed(k).start())
    turn_start(1)
    turn_start(0)
    for k in range(len(pieces) + 3):
        if k < len(pieces):
            @pl.when(crosses)
            def _():
                crossed(k).wait_recv()
                brought_on(k, me.dp()).start()

        if k == len(pieces) - 1:
            for i in range(2, 2 + micro):
                turn_start(i)
        b = k - 1
        if 0 <= b < len(pieces):
            pl.when(stays)(lambda: kept(b).wait())
            pl.when(moves)(lambda: brought(b, own).wait_recv())
            passed(1, b, own, xn).start()
            passed(2, b, own, yn).start()
            passed(4, b, own, cn).start()
        b = k - 2
        if 0 <= b < len(pieces):
            turn_x = (me.c == 0) if pieces[b][3] == "c" else (me.c < 0)
            passed(1, b, own_x, xn).wait_recv()
            pl.when(turn_x)(lambda: passed(3, b, own_x, yn).start())
            passed(5, b, own_x, cn).start()
            passed(2, b, own_y, yn).wait_recv()
            pl.when(jnp.logical_not(turn_x))(lambda: passed(3, b, own_y, xn).start())
            passed(6, b, own_y, cn).start()
        b = k - 3
        if 0 <= b < len(pieces):
            passed(3, b, own_d, yn).wait_recv()
            passed(7, b, own_d, cn).start()
    for k in range(len(pieces)):
        for kind in range(4, 8):
            passed(kind, k, beside[kind - 4], cn).wait_recv()
        pl.when(moves)(lambda: brought(k, own).wait_send())
        pl.when(crosses)(lambda: crossed(k).wait_send())
        for kind in range(1, 8):
            passed(kind, k, own, cn).wait_send()
    for i in range(len(turns)):
        turn_end(i)


def run_gather(shares, x_first, g, segs):
    pieces = GATHER_PIECES
    micro = g.shape[0]
    shape = jax.ShapeDtypeStruct
    outs = [shape((s.shape[0] * 8,) + s.shape[1:], s.dtype) for s in shares]
    outs += [shape(v.shape, v.dtype) for v in (x_first, g, segs)]
    return pl.pallas_call(
        functools.partial(gather_kernel, pieces, micro),
        out_shape=outs,
        in_specs=[ANYWHERE] * 8,
        out_specs=[ANYWHERE] * 8,
        scratch_shapes=[pltpu.VMEM(s.shape, s.dtype) for s in shares]
        + [DMA((9, len(pieces))), DMA((9, len(pieces))), DMA((len(pieces),)), DMA((2 + micro,)), DMA((2 + micro,))],
        compiler_params=pltpu.CompilerParams(collective_id=2, has_side_effects=True, vmem_limit_bytes=VMEM_CAP),
        name="gather_layers",
    )(*shares, x_first, g, segs)


SCATTER_PIECES = ((3, 0, 128, 0, 768, "x"), (3, 128, 128, 0, 768, "x"), (3, 256, 128, 0, 768, "x"),
                  (2, 0, 96, 0, 1024, "x"), (2, 0, 96, 1024, 1024, "x"), (2, 0, 96, 2048, 1024, "x"),
                  (0, 0, 96, 0, 768, "x"), (0, 0, 96, 768, 768, "x"), (0, 0, 96, 1536, 768, "x"),
                  (1, 0, 96, 0, 768, "x"), (4, 0, 16, 0, 128, "x"))


def scatter_kernel(pieces, micro, *refs):
    count = 5
    a_h, r_h, o_h, f_h, a2_h, dz_h, u_h, g_h, small_h, gin_in = refs[:10]
    outs, gin_o, norm_o = refs[10:15], refs[15], refs[16]
    at = 17
    totals, beside, diag, from_x, from_y, done, swap, home = (refs[at + i * count : at + (i + 1) * count] for i in range(8))
    (stream, fixed, flipped, sums, tallies, stream_sem, fixed_sem, send, recv, local, turn_sem, note_send, note_recv,
     out_sem) = refs[at + 8 * count :]
    me = Spot.here()
    xn, yn, cn = me.flip(x=1), me.flip(y=1), me.flip(c=1)
    target, giver, back, ahead = me.source(), me.drop(), me.back(), me.ahead()
    stays, alone = same(me, target), same(me, back)
    moves, pairs = jnp.logical_not(stays), jnp.logical_not(alone)
    crosses, target_crosses = me.crosses(), target.crosses()
    slab = [me.flip(x=i & 1, y=(i >> 1) & 1, c=i >> 2) for i in range(1, 8)]
    column = [Spot(me.x, me.y, (me.z + i) % 4, me.c) for i in range(1, 4)]
    left_right = {0: (a_h, r_h), 1: (o_h, f_h), 2: (a2_h, dz_h), 3: (u_h, g_h)}
    resting = (g_h, a2_h, a_h, o_h)
    rest_at = {3: 0, 2: 1, 0: 2, 1: 3}

    def streamed(k):
        array, first, size, column_at, columns, _ = pieces[k]
        slot = k % 2
        if array == 3:
            share = totals[3].shape[0] // 8
            return [pltpu.make_async_copy(u_h.at[:, pl.ds(p * share + first, size)],
                                          stream.at[slot, :, pl.ds(p * size, size)], stream_sem.at[slot, p])
                    for p in range(8)]
        if array == 4:
            return [pltpu.make_async_copy(small_h, totals[4], stream_sem.at[slot, 0])]
        return [pltpu.make_async_copy(left_right[array][1].at[:, pl.ds(column_at, columns)],
                                      stream.at[slot, :, pl.ds(0, columns)], stream_sem.at[slot, 0])]

    def rested(i):
        return pltpu.make_async_copy(resting[i], fixed.at[i], fixed_sem.at[i])

    for copy in streamed(0):
        copy.start()
    rested(0).start()
    for copy in streamed(1):
        copy.start()
    for i in range(1, 4):
        rested(i).start()
    for spot in slab + column:
        hail(spot)

    @pl.when(moves)
    def _():
        hail(target)
        hail(giver)

    @pl.when(pairs)
    def _():
        hail(back)
        hail(ahead)

    def work(k):
        array, first, size, column_at, columns, _ = pieces[k]
        slot = k % 2
        for copy in streamed(k):
            copy.wait()
        if array == 4:
            return
        if array == 3:
            if first == 0:
                rested(rest_at[3]).wait()
            share = totals[3].shape[0] // 8
            for p in range(0, 8, 2):
                both = lax.dot_general(stream[slot, :, p * size : (p + 2) * size], fixed[rest_at[3]], TN,
                                       preferred_element_type=F32).astype(BF)
                for i in range(2):
                    totals[3][(p + i) * share + first : (p + i) * share + first + size, :] = both[i * size : (i + 1) * size]
        else:
            if column_at == 0:
                rested(rest_at[array]).wait()
                flipped[...] = fixed[rest_at[array]].T
            for c in range(0, columns, 256):
                totals[array][:, column_at + c : column_at + c + 256] = mm(flipped[...], stream[slot, :, c : c + 256]).astype(BF)
        if k + 2 < len(pieces):
            for copy in streamed(k + 2):
                copy.start()

    def parts(spot):
        return [s.part() for s in (spot, spot.flip(x=1), spot.flip(y=1), spot.flip(x=1, y=1))]

    kept, given = parts(me), parts(cn)

    def box(k):
        _, first, size, column_at, columns, _ = pieces[k]
        return pl.ds(first, size), pl.ds(column_at, columns)

    def whole(k, part):
        array, first, size, column_at, columns, _ = pieces[k]
        share = done[array].shape[0]
        return totals[array].at[pl.ds(pl.multiple_of(part * share + first, 16), size), pl.ds(column_at, columns)]

    def remote(src, dst, kind, k, spot):
        return pltpu.make_async_remote_copy(
            src_ref=src, dst_ref=dst, send_sem=send.at[kind, k], recv_sem=recv.at[kind, k],
            device_id=spot.id(), device_id_type=MESH)

    def of(refs_, k):
        return refs_[pieces[k][0]].at[box(k)]

    def crossed(k, j):
        return remote(whole(k, given[j]), beside[pieces[k][0]].at[(j,) + box(k)], j, k, cn)

    def to_diag(k, spot):
        return remote(whole(k, kept[3]), of(diag, k), 4, k, spot)

    def to_x(k):
        return remote(whole(k, kept[1]), of(from_x, k), 5, k, xn)

    def to_y(k):
        return remote(whole(k, kept[2]), of(from_y, k), 6, k, yn)

    def to_home(k):
        return remote(of(done, k), of(home, k), 7, k, target)

    def to_swap(k):
        return remote(of(done, k), of(swap, k), 7, k, target)

    def stay_home(k):
        return pltpu.make_async_copy(of(done, k), of(home, k), local.at[k])

    def over(k):
        return remote(of(swap, k), of(home, k), 8, k, yn)

    def add(k, j, extra):
        here = whole(k, kept[j])
        here[...] = (here[...].astype(F32) + extra.astype(F32)).astype(here.dtype)

    def turn(m):
        return pltpu.make_async_remote_copy(
            src_ref=gin_in.at[m], dst_ref=gin_o.at[m], send_sem=turn_sem.at[0, m], recv_sem=turn_sem.at[1, m],
            device_id=back.id(), device_id_type=MESH)

    def turn_stay(m):
        return pltpu.make_async_copy(gin_in.at[m], gin_o.at[m], turn_sem.at[0, m])

    work(0)
    pl.semaphore_wait(pltpu.get_barrier_semaphore(), 10 + jnp.where(stays, 0, 2) + jnp.where(alone, 0, 2))
    for m in range(micro):
        now = (me.z >= 2) | (m == micro - 1)
        pl.when(alone & now)(lambda: turn_stay(m).start())
        pl.when(pairs & now)(lambda: turn(m).start())
    for k in range(len(pieces) + 4):
        if k < len(pieces):
            if k > 0:
                work(k)
            for j in (3, 2, 1, 0):
                crossed(k, j).start()
        b = k - 1
        if 0 <= b < len(pieces):
            turn_x = (me.c == 0) if pieces[b][5] == "c" else (me.c < 0)
            for j in (3, 2, 1, 0):
                crossed(b, j).wait_recv()
                add(b, j, beside[pieces[b][0]][(j,) + box(b)])
                if j == 3:
                    pl.when(turn_x)(lambda: to_diag(b, yn).start())
                    pl.when(jnp.logical_not(turn_x))(lambda: to_diag(b, xn).start())
                if j == 2:
                    pl.when(turn_x)(lambda: to_y(b).start())
                if j == 1:
                    pl.when(jnp.logical_not(turn_x))(lambda: to_x(b).start())
        b = k - 2
        if 0 <= b < len(pieces):
            to_diag(b, yn).wait_recv()
            turn_x = (me.c == 0) if pieces[b][5] == "c" else (me.c < 0)

            @pl.when(turn_x)
            def _():
                add(b, 1, of(diag, b)[...])
                to_x(b).start()

            @pl.when(jnp.logical_not(turn_x))
            def _():
                add(b, 2, of(diag, b)[...])
                to_y(b).start()
        b = k - 3
        if 0 <= b < len(pieces):
            to_x(b).wait_recv()
            to_y(b).wait_recv()
            total = (whole(b, kept[0])[...].astype(F32) + of(from_x, b)[...].astype(F32) + of(from_y, b)[...].astype(F32))
            done[pieces[b][0]][box(b)] = total.astype(done[pieces[b][0]].dtype)
            pl.when(stays)(lambda: stay_home(b).start())
            pl.when(moves & jnp.logical_not(target_crosses))(lambda: to_home(b).start())
            pl.when(target_crosses)(lambda: to_swap(b).start())
        b = k - 4
        if 0 <= b < len(pieces):
            @pl.when(crosses)
            def _():
                to_swap(b).wait_recv()
                over(b).start()
    tally = jnp.zeros((8, 128), F32)
    for k in range(len(pieces)):
        pl.when(stays)(lambda: stay_home(k).wait())
        pl.when(moves & jnp.logical_not(crosses))(lambda: to_home(k).wait_recv())
        pl.when(crosses)(lambda: over(k).wait_recv())
        value = of(home, k)[...].astype(F32)
        value = value * value
        for c in range(0, value.shape[1], 128):
            tally = tally + jnp.sum(value[:, c : c + 128].reshape(-1, 8, 128), axis=0)
    sums[0] = tally

    def note(i, src, slot, spot):
        return pltpu.make_async_remote_copy(
            src_ref=src, dst_ref=tallies.at[slot], send_sem=note_send.at[i], recv_sem=note_recv.at[slot],
            device_id=spot.id(), device_id_type=MESH)

    for i, spot in enumerate(column):
        note(i, sums.at[0], i, spot).start()
    for array in range(count):
        pltpu.make_async_copy(home[array], outs[array], out_sem.at[array]).start()
    for i, spot in enumerate(column):
        note(i, sums.at[0], i, spot).wait_recv()
        tally = tally + tallies[i]
    sums[1] = tally
    for i, spot in enumerate(slab):
        note(3 + i, sums.at[1], 3 + i, spot).start()
    for i, spot in enumerate(slab):
        note(3 + i, sums.at[1], 3 + i, spot).wait_recv()
        tally = tally + tallies[3 + i]
    norm_o[...] = tally
    for i, spot in enumerate(column):
        note(i, sums.at[0], i, spot).wait_send()
    for i, spot in enumerate(slab):
        note(3 + i, sums.at[1], 3 + i, spot).wait_send()
    for k in range(len(pieces)):
        for j in range(4):
            crossed(k, j).wait_send()
        to_diag(k, yn).wait_send()
        to_x(k).wait_send()
        to_y(k).wait_send()
        pl.when(moves)(lambda: to_home(k).wait_send())
        pl.when(crosses)(lambda: over(k).wait_send())
    for m in range(micro):
        now, then = (me.z >= 2) | (m == micro - 1), (me.section() >= 2) | (m == micro - 1)
        pl.when(alone & now)(lambda: turn_stay(m).wait())
        pl.when(pairs & now)(lambda: turn(m).wait_send())
        pl.when(pairs & then)(lambda: turn(m).wait_recv())
    for array in range(count):
        pltpu.make_async_copy(home[array], outs[array], out_sem.at[array]).wait()


def run_scatter(operands, small, gin):
    pieces = SCATTER_PIECES
    micro = gin.shape[0]
    shape = jax.ShapeDtypeStruct
    a, r, o, f, a2, dz, u, g = operands = [v.reshape(-1, v.shape[-1]) for v in operands]
    rows = a.shape[0]
    sizes = [((left.shape[1], right.shape[1]), BF) for left, right in ((a, r), (o, f), (a2, dz), (u, g))]
    sizes.append((small.shape, F32))
    shares = [((s[0] // 8, s[1]), t) for s, t in sizes]
    one = [pltpu.VMEM(s, t) for s, t in shares]
    return pl.pallas_call(
        functools.partial(scatter_kernel, pieces, micro),
        out_shape=[shape(s, t) for s, t in shares] + [shape(gin.shape, gin.dtype), shape((8, 128), F32)],
        in_specs=[ANYWHERE] * 10,
        out_specs=[ANYWHERE] * 6 + [IN_VMEM],
        scratch_shapes=[pltpu.VMEM(s, t) for s, t in sizes] + [pltpu.VMEM((4,) + s, t) for s, t in shares] + one * 6
        + [pltpu.VMEM((2, rows, 1024), BF), pltpu.VMEM((4, rows, a.shape[1]), BF), pltpu.VMEM((a.shape[1], rows), BF),
           pltpu.VMEM((2, 8, 128), F32), pltpu.VMEM((10, 8, 128), F32), DMA((2, 8)), DMA((4,)),
           DMA((9, len(pieces))), DMA((9, len(pieces))), DMA((len(pieces),)), DMA((2, micro)), DMA((10,)), DMA((10,)),
           DMA((5,))],
        compiler_params=pltpu.CompilerParams(collective_id=3, has_side_effects=True, vmem_limit_bytes=VMEM_CAP),
        name="scatter_layers",
    )(*operands, small, gin)


def split_small(small, width, slices):
    share = width // slices
    stacked = small.reshape(slices, small.shape[0] // slices)
    eight = stacked[:, : 8 * share].reshape(slices, 8, share).transpose(1, 0, 2).reshape(8, width)
    up = stacked[:, 8 * share :].reshape(-1, width)
    return jnp.concatenate([eight, up, jnp.zeros((16 - 8 - up.shape[0], width), small.dtype)], axis=0)


def join_small(table, total, slices):
    width = table.shape[1]
    share = width // slices
    ups = total // width - 8
    eight = table[:8].reshape(8, slices, share).transpose(1, 0, 2).reshape(slices, 8 * share)
    up = table[8 : 8 + ups].reshape(slices, -1)
    return jnp.concatenate([eight, up], axis=1).reshape(-1)


def weight_grad(left, right):
    rows = left.shape[0] * left.shape[1]
    return lax.dot_general(left.reshape(rows, -1), right.reshape(rows, -1), (((0,), (0,)), ((), ())),
                           preferred_element_type=F32)


def per_device(inputs, out_grad, segment_ids, cls_index, *states):
    masters, firsts, seconds = states[0:5], states[5:10], states[10:15]
    slices = lax.axis_size("dp")
    stages = lax.axis_size("section")
    turned = slices == 8 and stages == 4
    seq_dev, length, width = inputs.shape
    rows = -(-length // 128) * 128
    total = masters[4].shape[1] * slices

    extra = ((0, 0), (0, rows - length), (0, 0))
    x_in = jnp.pad(inputs, extra)
    g_in = jnp.pad(out_grad, extra)
    segs = jnp.pad(segment_ids, ((0, 0), (0, rows - length)), constant_values=-1)
    shares = [m.astype(BF)[0] for m in masters]
    if turned:
        line = Line("dp", 4, 2)
        lanes = masters[4].shape[1] // 128
        shares[4] = jnp.pad(shares[4].astype(F32).reshape(lanes, 128), ((0, 16 - lanes), (0, 0)))
        words = jnp.concatenate([segs, jnp.broadcast_to(cls_index[:, None], (seq_dev, rows))], axis=0)
        *gathered, x_first, g_in, words = run_gather(shares, x_in[0], g_in, words)
        segs, classes = words[:seq_dev], words[seq_dev:, 0]
        flat = gathered[4].reshape(slices, 16, 128)[:, :lanes].reshape(-1)
    else:
        line = Line("section", stages, 1)
        gathered = [lax.all_gather(s, "dp", axis=0, tiled=True) for s in shares]
        flat, classes, x_first = gathered[4].astype(F32), cls_index, x_in[0]
    weights = gathered[:4]
    small = split_small(flat, width, slices)
    segr, segc = segs[:, None, :], segs[:, :, None]

    x, a, qkv, lse, o, h, a2, gp, u, acts, acts_early = run_forward(
        line, length, turned, x_first, x_in, segr, segc, classes, weights, small)
    acts, gin_early, g, dz, f, r, gin, sums = run_backward(
        line, length, turned, acts, g_in, x, qkv, lse, h, gp, segr, segc, classes, weights, small)
    small_total = join_small(sums, total, slices)
    if turned:
        table = jnp.pad(small_total.reshape(slices, lanes, 128), ((0, 0), (0, 16 - lanes), (0, 0)))
        *shards, gin, tally = run_scatter([a, r, o, f, a2, dz, u, g], table.reshape(slices * 16, 128), gin)
        shards[4] = shards[4][:lanes].reshape(-1)
        shards = [s.astype(F32)[None] for s in shards]
        grad_norm = jnp.sqrt(jnp.sum(tally))
        upper = lax.axis_index("section") >= 2
        early = lax.broadcasted_iota(jnp.int32, (seq_dev, 1, 1), 0) < seq_dev - 1
        acts = jnp.where(early & upper, acts_early, acts)
        gin = jnp.where(early & jnp.logical_not(upper), gin_early, gin)
    else:
        totals = [weight_grad(a, r).astype(BF), weight_grad(o, f).astype(BF), weight_grad(a2, dz).astype(BF),
                  weight_grad(u, g).astype(BF), small_total]
        shards = [lax.psum_scatter(t[None], "dp", scatter_dimension=1, tiled=True).astype(F32) for t in totals]
        squares = jnp.sum(jnp.stack([jnp.sum(s * s) for s in shards]))
        grad_norm = jnp.sqrt(lax.psum(squares, ("dp", "section")))
    factor = 1.0 / jnp.maximum(grad_norm, 1.0)
    fix = 1.0 - 0.5**STEP
    results = []
    for kind in range(5):
        grad = shards[kind] * factor
        first = 0.5 * firsts[kind] + 0.5 * grad
        second = 0.5 * seconds[kind] + 0.5 * grad * grad
        update = first / fix / (jnp.sqrt(second / fix) + adam_eps)
        rate = small_rate
        if kind < 4:
            update = update + decay_rate * masters[kind]
            rate = learn_rate
        results += [grad, masters[kind] - rate * update, first, second]
    return (acts[:, :length][None], gin[:, :length][None], grad_norm.reshape(1)) + tuple(results)


def solution(mesh):
    matrix, vector = P("section", "dp", None), P("section", "dp")
    states = (matrix,) * 4 + (vector,)
    return jax.shard_map(
        per_device,
        mesh=mesh,
        in_specs=(P("dp", None, None), P("dp", None, None), P("dp", None), P("dp")) + states * 3,
        out_specs=(P("section", "dp", None, None), P("section", "dp", None, None), P())
        + (matrix,) * 16 + (vector,) * 4,
        check_vma=False,
    )
```

```python
import functools

import jax
import jax.numpy as jnp
from jax import lax
from jax.experimental import pallas as pl
from jax.experimental.pallas import tpu as pltpu
from jax.sharding import PartitionSpec as P

HEADS = 12
STEP = 3
F32 = jnp.float32
BF = jnp.bfloat16
MESH = pl.DeviceIdType.MESH
VMEM_CAP = 60 * 1024 * 1024

norm_eps = 1e-06
masked_score = -1e30
learn_rate = 0.05
small_rate = 0.3
decay_rate = 0.05
adam_eps = 1e-08

NT = (((1,), (1,)), ((), ()))
TN = (((0,), (0,)), ((), ()))


def mm(a, b):
    return jnp.dot(a, b, preferred_element_type=F32)


def mm_nt(a, b):
    return lax.dot_general(a, b, NT, preferred_element_type=F32)


def norm_parts(values):
    center = values - jnp.mean(values, axis=-1, keepdims=True)
    spread = jnp.mean(center * center, axis=-1, keepdims=True)
    inv = lax.rsqrt(spread + norm_eps)
    return center * inv, inv


def norm_back(y, normed, inv):
    pull = jnp.mean(y * normed, axis=-1, keepdims=True)
    return (y - jnp.mean(y, axis=-1, keepdims=True) - normed * pull) * inv


def column_sum(values):
    return jnp.sum(values, axis=0, keepdims=True)


def mask_bias(seg_row, seg_col, cls_row, length):
    size = seg_col.shape[0]
    key_at = lax.broadcasted_iota(jnp.int32, (size, size), 0)
    query_at = lax.broadcasted_iota(jnp.int32, (size, size), 1)
    allowed = (seg_row == seg_col) | (key_at == cls_row) | (query_at == cls_row)
    allowed = allowed & (key_at < length)
    return jnp.where(allowed, 0.0, masked_score).astype(F32)


def micro_bias(words, m, micro, length):
    seg_row, cls_row = words[pl.ds(m, 1), :], words[pl.ds(micro + m, 1), :]
    size = seg_row.shape[1]
    on_diagonal = lax.broadcasted_iota(jnp.int32, (size, size), 0) == lax.broadcasted_iota(jnp.int32, (size, size), 1)
    seg_col = jnp.sum(jnp.where(on_diagonal, seg_row.astype(F32), 0.0), axis=1, keepdims=True)
    return mask_bias(seg_row.astype(F32), seg_col, cls_row, length)


def spread_small(table, small):
    width = small.shape[1]
    share, ups = width // 8, width // 256
    small[...] = jnp.zeros_like(small)
    for i in range(8):
        small[0:8, i * share : (i + 1) * share] = table[16 * i : 16 * i + 8, 0:share]
        for j in range(ups):
            at = i % 2 * (width // 2) + j * 128
            small[8 + i // 2 : 9 + i // 2, at : at + 128] = table[16 * i + 8 + j : 16 * i + 9 + j, :]


def share_small(sums, table):
    width = sums.shape[1]
    share, ups = width // 8, width // 256
    table[...] = jnp.zeros_like(table)
    for i in range(8):
        table[16 * i : 16 * i + 8, 0:share] = sums[0:8, i * share : (i + 1) * share]
        for j in range(ups):
            at = i % 2 * (width // 2) + j * 128
            table[16 * i + 8 + j : 16 * i + 9 + j, :] = sums[8 + i // 2 : 9 + i // 2, at : at + 128]


def gelu_parts(z):
    density = jnp.exp(z * z * -0.5) * 0.3989422804014327
    below = 0.5 + 0.5 * lax.erf(z * 0.7071067811865476)
    return z * below, below + z * density


def layer_forward(x_ref, bias_ref, wqkv, wproj, wup, wdown, small, a_ref, qkv_ref, lse_ref, o_ref,
                  h_ref, a2_ref, gp_ref, u_ref, out_ref, ot_ref, before_up):
    rows, width = x_ref.shape
    hidden = wup.shape[1]
    normed, _ = norm_parts(x_ref[...].astype(F32))
    a_ref[...] = (normed * small[0:1, :] + small[1:2, :]).astype(BF)
    for part in range(3):
        cols = slice(part * width, (part + 1) * width)
        mixed = mm(a_ref[...], wqkv[:, cols])
        if part == 0:
            mixed = mixed + small[2:3, :]
        if part == 2:
            mixed = mixed + small[3:4, :]
        qkv_ref[:, cols] = mixed.astype(BF)
    lane = lax.broadcasted_iota(jnp.int32, (rows, 128), 1)
    scores, raised, inverse = {}, {}, {}
    for step in range(HEADS + 2):
        if step < HEADS:
            at = step // 2 * 128
            half = (lane < 64) if step % 2 == 0 else (lane >= 64)
            k = qkv_ref[:, width + at : width + at + 128]
            k = jnp.where(half, k, jnp.zeros_like(k)) * jnp.asarray(0.125, BF)
            scores[step] = mm_nt(k, qkv_ref[:, at : at + 128])
        head = step - 1
        if 0 <= head < HEADS:
            shifted = scores.pop(head) + bias_ref[...]
            peak = jnp.max(shifted, axis=0, keepdims=True)
            grown = jnp.exp(shifted - peak)
            summed = jnp.sum(grown, axis=0, keepdims=True)
            raised[head] = grown.astype(BF)
            inverse[head] = 1.0 / summed
            lse_ref[head : head + 1, :] = peak + jnp.log(summed)
        head = step - 2
        if 0 <= head < HEADS:
            if head % 2 == 0:
                vt = qkv_ref[:, 2 * width + head * 64 : 2 * width + head * 64 + 128].T
            mixed = mm(vt[head % 2 * 64 : head % 2 * 64 + 64, :], raised.pop(head)) * inverse.pop(head)
            ot_ref[head * 64 : head * 64 + 64, :] = mixed.astype(BF)
    o_ref[...] = ot_ref[...].T
    h = x_ref[...].astype(F32) + (mm(o_ref[...], wproj[...]) + small[4:5, :])
    h_ref[...] = h
    normed, _ = norm_parts(h)
    a2_ref[...] = (normed * small[5:6, :] + small[6:7, :]).astype(BF)
    before_up()
    chunk = width
    z = {}
    for step in range(hidden // chunk + 1):
        cols = slice(step * chunk, (step + 1) * chunk)
        if step < hidden // chunk:
            row, start = 8 + step * chunk // width, step * chunk % width
            z[step] = mm(a2_ref[...], wup[:, cols]) + small[row : row + 1, start : start + chunk]
        part = step - 1
        if 0 <= part < hidden // chunk:
            cols = slice(part * chunk, (part + 1) * chunk)
            u, slope = gelu_parts(z.pop(part))
            u_ref[:, cols] = u.astype(BF)
            gp_ref[:, cols] = slope.astype(BF)
    total = mm(u_ref[...], wdown[...])
    out_ref[...] = (h_ref[...] + (total + small[7:8, :])).astype(BF)


def layer_backward(g_ref, x_ref, bias_ref, qkv_ref, lse_ref, h_ref, gp_ref, wqkv, wproj, wup, wdown,
                   small, dz_ref, f_ref, r_ref, gin_ref, sums_ref, do_ref, dh_ref, dqt_ref):
    rows, width = x_ref.shape
    hidden = wup.shape[1]
    carried = g_ref[...].astype(F32)
    sums_ref[7:8, :] += column_sum(carried)
    back = {}
    for step in range(hidden // width + 1):
        if step < hidden // width:
            back[step] = mm_nt(g_ref[...], wdown[step * width : (step + 1) * width, :])
        part = step - 1
        if part >= 0:
            cols = slice(part * width, (part + 1) * width)
            dz = (back.pop(part) * gp_ref[:, cols].astype(F32)).astype(BF)
            dz_ref[:, cols] = dz
            sums_ref[8 + part : 9 + part, :] += column_sum(dz.astype(F32))
    back = mm_nt(dz_ref[...], wup[...])
    normed, inv = norm_parts(h_ref[...])
    sums_ref[5:6, :] += column_sum(back * normed)
    sums_ref[6:7, :] += column_sum(back)
    dh = carried + norm_back(back * small[5:6, :], normed, inv)
    dh_ref[...] = dh
    f = dh.astype(BF)
    f_ref[...] = f
    sums_ref[4:5, :] += column_sum(f.astype(F32))
    do_ref[...] = mm_nt(f_ref[...], wproj[...]).astype(BF)
    lane = lax.broadcasted_iota(jnp.int32, (rows, 128), 1)
    scores, grads, probs, slopes, dks, dvs = {}, {}, {}, {}, {}, {}
    eighth = jnp.asarray(0.125, BF)
    for step in range(HEADS + 2):
        if step < HEADS:
            at = step // 2 * 128
            half = (lane < 64) if step % 2 == 0 else (lane >= 64)
            k = qkv_ref[:, width + at : width + at + 128]
            v = qkv_ref[:, 2 * width + at : 2 * width + at + 128]
            scores[step] = mm_nt(jnp.where(half, k, jnp.zeros_like(k)) * eighth, qkv_ref[:, at : at + 128])
            grads[step] = mm_nt(jnp.where(half, v, jnp.zeros_like(v)), do_ref[:, at : at + 128])
        head = step - 1
        if 0 <= head < HEADS:
            p = jnp.exp(scores.pop(head) + bias_ref[...] - lse_ref[head : head + 1, :])
            dp = grads.pop(head)
            inner = jnp.sum(p * dp, axis=0, keepdims=True)
            slopes[head] = (p * (dp - inner)).astype(BF)
            probs[head] = p.astype(BF)
        head = step - 2
        if 0 <= head < HEADS:
            at = head // 2 * 128
            side = head % 2
            ds = slopes.pop(head)
            dvs[side] = mm(probs.pop(head), do_ref[:, at : at + 128])
            dks[side] = mm(ds, qkv_ref[:, at : at + 128] * eighth)
            if side == 0:
                kt = (qkv_ref[:, width + at : width + at + 128] * eighth).T
            dqt_ref[head * 64 : head * 64 + 64, :] = mm(kt[side * 64 : side * 64 + 64, :], ds).astype(BF)
            if side == 1:
                r_ref[:, width + at : width + at + 128] = jnp.where(lane < 64, dks[0], dks[1]).astype(BF)
                r_ref[:, 2 * width + at : 2 * width + at + 128] = jnp.where(lane < 64, dvs[0], dvs[1]).astype(BF)
    r_ref[:, 0:width] = dqt_ref[...].T
    sums_ref[2:3, :] += column_sum(r_ref[:, 0:width].astype(F32))
    sums_ref[3:4, :] += column_sum(r_ref[:, 2 * width :].astype(F32))
    back = mm_nt(r_ref[...], wqkv[...])
    normed, inv = norm_parts(x_ref[...].astype(F32))
    sums_ref[0:1, :] += column_sum(back * normed)
    sums_ref[1:2, :] += column_sum(back)
    gin_ref[...] = (dh_ref[...] + norm_back(back * small[0:1, :], normed, inv)).astype(BF)


class Line:
    def __init__(self, axis, count, stride):
        self.axis, self.count, self.stride = axis, count, stride

    def stage(self):
        return lax.axis_index(self.axis) // self.stride

    def beside(self, by):
        return {self.axis: lax.axis_index(self.axis) + by * self.stride}


class Spot:
    def __init__(self, x, y, z, c):
        self.x, self.y, self.z, self.c = x, y, z, c

    @staticmethod
    def here():
        dp, section = lax.axis_index("dp"), lax.axis_index("section")
        return Spot(dp % 2, section // 2, dp // 2, section % 2)

    def dp(self):
        return self.z * 2 + self.x

    def section(self):
        return self.y * 2 + self.c

    def id(self):
        return (self.dp(), self.section())

    def flip(self, x=0, y=0, c=0):
        return Spot(1 - self.x if x else self.x, 1 - self.y if y else self.y, self.z, 1 - self.c if c else self.c)

    def ahead(self):
        return Spot(self.x, self.z % 2, self.section(), self.z // 2)

    def back(self):
        return Spot(self.x, self.z // 2, 2 * self.c + self.y, self.z % 2)

    def feeds(self, stage, core):
        return ((self.y == self.z % 2) & (self.c == core)) & (self.z >= 0)

    def fed_at(self, stage):
        return Spot(self.x, self.y, stage, self.z // 2)

    def feeder(self, core):
        return Spot(self.x, self.y, 2 * self.c + self.y, core)

    def crosses(self):
        return (self.z + self.c) % 2 == 1

    def drop(self):
        return Spot(self.x, self.y, 2 * ((self.y + self.z + self.c) % 2) + self.c, self.z // 2)

    def source(self):
        c = self.z % 2
        return Spot(self.x, self.y, 2 * self.c + (self.y + self.z // 2 + c) % 2, c)

    def part(self):
        return self.source().dp()


def same(one, other):
    return (one.dp() == other.dp()) & (one.section() == other.section())


def hail(spot):
    pl.semaphore_signal(pltpu.get_barrier_semaphore(), inc=1, device_id=spot.id(), device_id_type=MESH)


def hail_feeding(me, stage, core):
    gives = me.feeds(stage, core) & jnp.logical_not(same(me, me.fed_at(stage)))
    takes = (me.z == stage) & jnp.logical_not(same(me, me.feeder(core)))
    pl.when(gives)(lambda: hail(me.fed_at(stage)))
    pl.when(takes)(lambda: hail(me.feeder(core)))
    return jnp.where(gives, 1, 0) + jnp.where(takes, 1, 0)


def greet(line, turned, feeding=False):
    stage = line.stage()
    barrier = pltpu.get_barrier_semaphore()

    @pl.when(stage > 0)
    def _():
        pl.semaphore_signal(barrier, inc=1, device_id=line.beside(-1), device_id_type=MESH)

    @pl.when(stage < line.count - 1)
    def _():
        pl.semaphore_signal(barrier, inc=1, device_id=line.beside(1), device_id_type=MESH)

    expected = jnp.where(stage > 0, 1, 0) + jnp.where(stage < line.count - 1, 1, 0)
    if turned:
        me = Spot.here()
        alone = same(me, me.back())

        @pl.when(jnp.logical_not(alone))
        def _():
            hail(me.back())
            hail(me.ahead())

        expected = expected + jnp.where(alone, 0, 2)
        if feeding:
            expected = expected + hail_feeding(me, 0, 0)
    pl.semaphore_wait(barrier, expected)


def forward_kernel(line, length, turned, x_first, x_in, words, wqkv_h, wproj_h, wup_h, wdown_h, small_in,
                   x_o, a_o, qkv_o, lse_o, o_o, h_o, a2_o, gp_o, u_o, acts_o, home_o,
                   wqkv, wproj, wup, wdown, xs, outs, a, qkv, lse, o, h, a2, gp, u, bias, ot, small,
                   w_sem, in_sem, x_sem, save_sem, act_sem, send_sem, recv_sem, home_sem):
    micro = xs.shape[0]
    stage = line.stage()
    loads = [
        pltpu.make_async_copy(src, dst, w_sem.at[i])
        for i, (src, dst) in enumerate(((wqkv_h, wqkv), (wproj_h, wproj), (wup_h, wup), (wdown_h, wdown)))
    ]
    for load in loads:
        load.start()

    def first_in(m):
        return pltpu.make_async_copy(x_in.at[m], xs.at[m], in_sem.at[m])

    if turned:
        spread_small(small_in, small)
    else:
        small[...] = small_in[...]
    greet(line, turned, feeding=True)
    if turned:
        me = Spot.here()
        back = me.back()
        alone = same(me, back)

        def turn_in(m):
            return pltpu.make_async_remote_copy(
                src_ref=x_in.at[m], dst_ref=xs.at[m], send_sem=in_sem.at[m], recv_sem=recv_sem.at[m],
                device_id=taker.id(), device_id_type=MESH)

        taker, feeder = me.fed_at(0), me.feeder(0)
        feeds = me.feeds(0, 0) & jnp.logical_not(same(me, taker))
        feeds_self = me.feeds(0, 0) & same(me, taker)
        homing = jnp.logical_and(stage >= 2, jnp.logical_not(alone))
        homed = jnp.logical_and(me.section() >= 2, jnp.logical_not(alone))
        settled = jnp.logical_and(stage >= 2, alone)

        def home(m):
            return pltpu.make_async_remote_copy(
                src_ref=outs.at[m], dst_ref=home_o.at[m], send_sem=home_sem.at[0, m], recv_sem=home_sem.at[1, m],
                device_id=back.id(), device_id_type=MESH)

        def settle(m):
            return pltpu.make_async_copy(outs.at[m], home_o.at[m], home_sem.at[0, m])

        @pl.when(stage == 0)
        def _():
            pltpu.make_async_copy(x_first, xs.at[0], in_sem.at[0]).start()

        for m in range(1, micro):
            @pl.when(feeds)
            def _():
                turn_in(m).start()

            @pl.when(feeds_self)
            def _():
                first_in(m).start()
    else:
        @pl.when(stage == 0)
        def _():
            for m in range(micro):
                first_in(m).start()

    saved = ((a, a_o), (qkv, qkv_o), (lse, lse_o), (o, o_o), (h, h_o), (a2, a2_o), (gp, gp_o), (u, u_o))

    def saves(m, slot):
        return [
            pltpu.make_async_copy(here.at[slot], there.at[m], save_sem.at[slot, i])
            for i, (here, there) in enumerate(saved)
        ]

    def hop(m):
        return pltpu.make_async_remote_copy(
            src_ref=outs.at[m], dst_ref=xs.at[m], send_sem=send_sem.at[m], recv_sem=recv_sem.at[m],
            device_id=line.beside(1), device_id_type=MESH)

    def step(m, carry):
        slot = lax.rem(m, 2)

        if turned:
            here = jnp.logical_or(feeds_self, jnp.logical_and(stage == 0, m == 0))
        else:
            here = stage == 0

        @pl.when(here)
        def _():
            first_in(m).wait()

        @pl.when(jnp.logical_not(here))
        def _():
            hop(m).wait_recv()

        pltpu.make_async_copy(xs.at[m], x_o.at[m], x_sem.at[m]).start()

        @pl.when(m >= 2)
        def _():
            for save in saves(m - 2, slot):
                save.wait()

        @pl.when(m == 0)
        def _():
            loads[0].wait()
            loads[1].wait()

        bias[...] = micro_bias(words, m, micro, length)

        def before_up():
            @pl.when(m == 0)
            def _():
                loads[2].wait()
                loads[3].wait()

        layer_forward(xs.at[m], bias, wqkv, wproj, wup, wdown, small, a.at[slot], qkv.at[slot],
                      lse.at[slot], o.at[slot], h.at[slot], a2.at[slot], gp.at[slot], u.at[slot],
                      outs.at[m], ot, before_up)

        @pl.when(stage < line.count - 1)
        def _():
            hop(m).start()

        for save in saves(m, slot):
            save.start()
        pltpu.make_async_copy(outs.at[m], acts_o.at[m], act_sem.at[m]).start()
        if turned:
            pl.when(homing & (m < micro - 1))(lambda: home(m).start())
            pl.when(settled & (m < micro - 1))(lambda: settle(m).start())
        return carry

    lax.fori_loop(0, micro, step, 0)

    for m in range(max(micro - 2, 0), micro):
        for save in saves(m, m % 2):
            save.wait()
    for m in range(micro):
        pltpu.make_async_copy(xs.at[m], x_o.at[m], x_sem.at[m]).wait()
        pltpu.make_async_copy(outs.at[m], acts_o.at[m], act_sem.at[m]).wait()

    @pl.when(stage < line.count - 1)
    def _():
        for m in range(micro):
            hop(m).wait_send()

    if turned:
        @pl.when(feeds)
        def _():
            for m in range(1, micro):
                turn_in(m).wait_send()

        for m in range(micro - 1):
            pl.when(homing)(lambda: home(m).wait_send())
            pl.when(homed)(lambda: home(m).wait_recv())
            pl.when(settled)(lambda: settle(m).wait())


def backward_kernel(line, length, turned, acts_h, g_in, x_h, qkv_h, lse_h, h_h, gp_h, words,
                    wqkv_h, wproj_h, wup_h, wdown_h, small_in,
                    acts_o, home_o, g_o, dz_o, f_o, r_o, gin_o, sums_out,
                    wqkv, wproj, wup, wdown, gs, gins, x, qkv, lse, h, gp, dz, f, r, bias, do, dh, dqt, small, sums_o,
                    w_sem, in_sem, g_sem, load_sem, save_sem, act_sem, send_sem, recv_sem, home_sem, back_sem):
    micro = gs.shape[0]
    stage = line.stage()
    loads = [
        pltpu.make_async_copy(src, dst, w_sem.at[i])
        for i, (src, dst) in enumerate(((wdown_h, wdown), (wup_h, wup), (wproj_h, wproj), (wqkv_h, wqkv)))
    ]

    def last_in(m):
        return pltpu.make_async_copy(g_in.at[m], gs.at[m], in_sem.at[m])

    @pl.when(stage == line.count - 1)
    def _():
        for m in range(micro):
            last_in(m).start()

    kept = ((gp_h, gp), (h_h, h), (qkv_h, qkv), (lse_h, lse), (x_h, x))

    def fetches(m, slot):
        return [
            pltpu.make_async_copy(there.at[m], here.at[slot], load_sem.at[slot, i])
            for i, (there, here) in enumerate(kept)
        ]

    loads[0].start()
    for fetch in fetches(0, 0):
        fetch.start()
    for load in loads[1:]:
        load.start()
    sums_o[...] = jnp.zeros_like(sums_o)
    if turned:
        spread_small(small_in, small)
    else:
        small[...] = small_in[...]
    greet(line, turned)
    if turned:
        me = Spot.here()
        back = me.back()
        alone = same(me, back)

        def home(m):
            return pltpu.make_async_remote_copy(
                src_ref=acts_h.at[m], dst_ref=acts_o.at[m], send_sem=home_sem.at[0, m], recv_sem=home_sem.at[1, m],
                device_id=back.id(), device_id_type=MESH)

        def stay(m):
            return pltpu.make_async_copy(acts_h.at[m], acts_o.at[m], home_sem.at[0, m])

        pairs = jnp.logical_not(alone)
        low, low_home = stage < 2, me.section() < 2

        def home_back(m):
            return pltpu.make_async_remote_copy(
                src_ref=gins.at[m], dst_ref=home_o.at[m], send_sem=back_sem.at[0, m], recv_sem=back_sem.at[1, m],
                device_id=back.id(), device_id_type=MESH)

        def settle_back(m):
            return pltpu.make_async_copy(gins.at[m], home_o.at[m], back_sem.at[0, m])

        for m in range(micro):
            now = low | (m == micro - 1)
            pl.when(alone & now)(lambda: stay(m).start())
            pl.when(pairs & now)(lambda: home(m).start())
    else:
        for m in range(micro):
            pltpu.make_async_copy(acts_h.at[m], acts_o.at[m], home_sem.at[0, m]).start()

    saved = ((dz, dz_o), (f, f_o), (r, r_o))

    def saves(m, slot):
        return [
            pltpu.make_async_copy(here.at[slot], there.at[m], save_sem.at[slot, i])
            for i, (here, there) in enumerate(saved)
        ]

    def hop(m):
        return pltpu.make_async_remote_copy(
            src_ref=gins.at[m], dst_ref=gs.at[m], send_sem=send_sem.at[m], recv_sem=recv_sem.at[m],
            device_id=line.beside(-1), device_id_type=MESH)

    def step(m, carry):
        slot = lax.rem(m, 2)

        @pl.when(m + 1 < micro)
        def _():
            for fetch in fetches(m + 1, 1 - slot):
                fetch.start()

        @pl.when(m == 0)
        def _():
            for load in loads:
                load.wait()

        for fetch in fetches(m, slot):
            fetch.wait()
        bias[...] = micro_bias(words, m, micro, length)

        @pl.when(m >= 2)
        def _():
            for save in saves(m - 2, slot):
                save.wait()

        @pl.when(stage == line.count - 1)
        def _():
            last_in(m).wait()

        @pl.when(stage < line.count - 1)
        def _():
            hop(m).wait_recv()

        pltpu.make_async_copy(gs.at[m], g_o.at[m], g_sem.at[m]).start()
        layer_backward(gs.at[m], x.at[slot], bias, qkv.at[slot], lse.at[slot], h.at[slot], gp.at[slot],
                       wqkv, wproj, wup, wdown, small, dz.at[slot], f.at[slot], r.at[slot], gins.at[m],
                       sums_o, do, dh, dqt)

        @pl.when(stage > 0)
        def _():
            hop(m).start()

        for save in saves(m, slot):
            save.start()
        pltpu.make_async_copy(gins.at[m], gin_o.at[m], act_sem.at[m]).start()
        if turned:
            pl.when(pairs & low & (m < micro - 1))(lambda: home_back(m).start())
            pl.when(alone & low & (m < micro - 1))(lambda: settle_back(m).start())
        return carry

    lax.fori_loop(0, micro, step, 0)
    if turned:
        share_small(sums_o, sums_out)
    else:
        sums_out[...] = sums_o[...]

    for m in range(max(micro - 2, 0), micro):
        for save in saves(m, m % 2):
            save.wait()
    for m in range(micro):
        pltpu.make_async_copy(gs.at[m], g_o.at[m], g_sem.at[m]).wait()
        pltpu.make_async_copy(gins.at[m], gin_o.at[m], act_sem.at[m]).wait()

    @pl.when(stage > 0)
    def _():
        for m in range(micro):
            hop(m).wait_send()

    for m in range(micro):
        if turned:
            now, then = low | (m == micro - 1), low_home | (m == micro - 1)
            pl.when(alone & now)(lambda: stay(m).wait())
            pl.when(pairs & now)(lambda: home(m).wait_send())
            pl.when(pairs & then)(lambda: home(m).wait_recv())
            if m < micro - 1:
                pl.when(pairs & low)(lambda: home_back(m).wait_send())
                pl.when(pairs & low_home)(lambda: home_back(m).wait_recv())
                pl.when(alone & low)(lambda: settle_back(m).wait())
        else:
            pltpu.make_async_copy(acts_h.at[m], acts_o.at[m], home_sem.at[0, m]).wait()


IN_VMEM = pl.BlockSpec(memory_space=pltpu.VMEM)
IN_SMEM = pl.BlockSpec(memory_space=pltpu.SMEM)
ANYWHERE = pl.BlockSpec(memory_space=pl.ANY)
DMA = pltpu.SemaphoreType.DMA


def run_forward(line, length, turned, x_first, x_in, words, weights, small):
    micro, rows, width = x_in.shape
    hidden = weights[2].shape[1]
    shape = jax.ShapeDtypeStruct
    saved = (
        ((rows, width), BF), ((rows, 3 * width), BF), ((16, rows), F32), ((rows, width), BF),
        ((rows, width), F32), ((rows, width), BF), ((rows, hidden), BF), ((rows, hidden), BF))
    many = shape((micro, rows, width), BF)
    return pl.pallas_call(
        functools.partial(forward_kernel, line, length, turned),
        out_shape=[many] + [shape((micro,) + s, t) for s, t in saved] + [many, many],
        in_specs=[ANYWHERE, ANYWHERE, IN_VMEM] + [ANYWHERE] * 4 + [IN_VMEM],
        out_specs=[ANYWHERE] * 11,
        scratch_shapes=[pltpu.VMEM(w.shape, BF) for w in weights]
        + [pltpu.VMEM((micro, rows, width), BF)] * 2
        + [pltpu.VMEM((2,) + s, t) for s, t in saved]
        + [pltpu.VMEM((rows, rows), F32), pltpu.VMEM((width, rows), BF), pltpu.VMEM((16, width), F32)]
        + [DMA((4,)), DMA((micro,)), DMA((micro,)), DMA((2, 8)), DMA((micro,)), DMA((micro,)), DMA((micro,)),
           DMA((2, micro))],
        compiler_params=pltpu.CompilerParams(
            collective_id=0, has_side_effects=True, vmem_limit_bytes=VMEM_CAP),
        name="forward_line",
    )(x_first, x_in, words, *weights, small)


def run_backward(line, length, turned, acts, g_in, x, qkv, lse, h, gp, words, weights, small):
    micro, rows, width = g_in.shape
    hidden = weights[2].shape[1]
    shape = jax.ShapeDtypeStruct
    many = shape((micro, rows, width), BF)
    wqkv, wproj, wup, wdown = weights
    return pl.pallas_call(
        functools.partial(backward_kernel, line, length, turned),
        out_shape=[many, many, many, shape((micro, rows, hidden), BF), many, shape((micro, rows, 3 * width), BF), many,
                   shape(small.shape, F32)],
        in_specs=[ANYWHERE] * 7 + [IN_VMEM] + [ANYWHERE] * 4 + [IN_VMEM],
        out_specs=[ANYWHERE] * 7 + [IN_VMEM],
        scratch_shapes=[pltpu.VMEM(w.shape, BF) for w in weights]
        + [pltpu.VMEM((micro, rows, width), BF)] * 2
        + [pltpu.VMEM((2, rows, width), BF), pltpu.VMEM((2, rows, 3 * width), BF), pltpu.VMEM((2, 16, rows), F32),
           pltpu.VMEM((2, rows, width), F32), pltpu.VMEM((2, rows, hidden), BF),
           pltpu.VMEM((2, rows, hidden), BF), pltpu.VMEM((2, rows, width), BF), pltpu.VMEM((2, rows, 3 * width), BF),
           pltpu.VMEM((rows, rows), F32), pltpu.VMEM((rows, width), BF), pltpu.VMEM((rows, width), F32),
           pltpu.VMEM((width, rows), BF), pltpu.VMEM((16, width), F32), pltpu.VMEM((16, width), F32)]
        + [DMA((4,)), DMA((micro,)), DMA((micro,)), DMA((2, 5)), DMA((2, 3)), DMA((micro,)), DMA((micro,)),
           DMA((micro,)), DMA((2, micro)), DMA((2, micro))],
        compiler_params=pltpu.CompilerParams(
            collective_id=1, has_side_effects=True, vmem_limit_bytes=VMEM_CAP),
        name="backward_line",
    )(acts, g_in, x, qkv, lse, h, gp, words, wqkv, wproj, wup, wdown, small)


GATHER_PIECES = ((0, 0, 48, "c"), (0, 48, 48, "x"), (4, 0, 16, "x"), (1, 0, 96, "c"), (2, 0, 48, "x"), (2, 48, 48, "c"),
                 (3, 0, 192, "x"), (3, 192, 192, "c"))


def gather_kernel(pieces, micro, *refs):
    count = 5
    masters, (x_in, g_in, seg_in) = refs[:count], refs[count : count + 3]
    wholes, (x_o, x_all, g_o, seg_o) = refs[count + 3 : 2 * count + 3], refs[2 * count + 3 : 2 * count + 7]
    refs = refs[2 * count + 7 :]
    swap, wide, narrow, (x_raw, g_raw, x_pad, g_pad) = refs[:5], refs[5:9], refs[9:13], refs[13:17]
    send, recv, local, turn_send, turn_recv, load_sem = refs[17:]
    shares = narrow + (masters[4],)
    loads = [pltpu.make_async_copy(masters[i], wide[i], load_sem.at[i]) for i in range(4)]
    loads += [pltpu.make_async_copy(x_in, x_raw, load_sem.at[4]), pltpu.make_async_copy(g_in, g_raw, load_sem.at[5])]
    for i in (0, 1, 2, 3, 4, 5):
        loads[i].start()
    me = Spot.here()
    xn, yn, cn = me.flip(x=1), me.flip(y=1), me.flip(c=1)
    target, source, ahead, back = me.drop(), me.source(), me.ahead(), me.back()
    stays, alone = same(me, target), same(me, back)
    moves, pairs = jnp.logical_not(stays), jnp.logical_not(alone)
    crosses = me.crosses()
    direct = jnp.logical_and(moves, jnp.logical_not(crosses))
    for spot in (xn, yn, cn):
        hail(spot)

    @pl.when(moves)
    def _():
        hail(target)
        hail(source)

    @pl.when(pairs)
    def _():
        hail(ahead)
        hail(back)

    fed = hail_feeding(me, 0, 0) + hail_feeding(me, 3, 1)
    expected = 3 + jnp.where(stays, 0, 2) + jnp.where(alone, 0, 2) + fed

    def rows(k, part):
        array, first, size, _ = pieces[k]
        share = shares[array].shape[0]
        return wholes[array].at[pl.ds(pl.multiple_of(part * share + first, 16), size)]

    def mine(k):
        array, first, size, _ = pieces[k]
        return shares[array].at[pl.ds(first, size)]

    def swapped(k):
        array, first, size, _ = pieces[k]
        return swap[array].at[pl.ds(first, size)]

    def remote(src, dst, kind, k, spot):
        return pltpu.make_async_remote_copy(
            src_ref=src, dst_ref=dst, send_sem=send.at[kind, k], recv_sem=recv.at[kind, k],
            device_id=spot.id(), device_id_type=MESH)

    def crossed(k):
        return remote(mine(k), swapped(k), 8, k, yn)

    def brought(k, part):
        return remote(mine(k), rows(k, part), 0, k, target)

    def brought_on(k, part):
        return remote(swapped(k), rows(k, part), 0, k, target)

    def kept(k):
        return pltpu.make_async_copy(mine(k), rows(k, me.dp()), local.at[k])

    def passed(kind, k, part, spot):
        return remote(rows(k, part), rows(k, part), kind, k, spot)

    def parts(spot):
        return [s.part() for s in (spot, spot.flip(x=1), spot.flip(y=1), spot.flip(x=1, y=1))]

    own, own_x, own_y, own_d = parts(me)
    beside = parts(cn)
    turns = [(x_pad.at[0], x_o), (seg_in, seg_o)] + [(g_pad.at[m], g_o.at[m]) for m in range(micro)]
    gives = [me.feeds(0, 0), me.z >= 0] + [me.feeds(3, 1)] * micro
    takes = [me.z == 0, me.z >= 0] + [me.z == 3] * micro
    takers = [me.fed_at(0), ahead] + [me.fed_at(3)] * micro
    givers = [me.feeder(0), back] + [me.feeder(1)] * micro

    def turn(i):
        return pltpu.make_async_remote_copy(
            src_ref=turns[i][0], dst_ref=turns[i][1], send_sem=turn_send.at[i], recv_sem=turn_recv.at[i],
            device_id=takers[i].id(), device_id_type=MESH)

    def turn_start(i):
        here = same(me, takers[i])
        pl.when(gives[i] & here)(lambda: pltpu.make_async_copy(*turns[i], turn_send.at[i]).start())
        pl.when(gives[i] & jnp.logical_not(here))(lambda: turn(i).start())

    def turn_end(i):
        here = same(me, takers[i])
        pl.when(gives[i] & here)(lambda: pltpu.make_async_copy(*turns[i], turn_send.at[i]).wait())
        pl.when(gives[i] & jnp.logical_not(here))(lambda: turn(i).wait_send())
        pl.when(takes[i] & jnp.logical_not(same(me, givers[i])))(lambda: turn(i).wait_recv())

    def pad(raw, padded):
        for m in range(micro):
            short = raw[m]
            rest = jnp.zeros((padded.shape[1] - short.shape[0], short.shape[1]), short.dtype)
            padded[m] = jnp.concatenate([short, rest], axis=0)

    ready = set()
    for k in range(len(pieces)):
        array = pieces[k][0]
        if array < 4 and array not in ready:
            ready.add(array)
            loads[array].wait()
            size = wide[array].shape[0]
            for first in range(0, size, 48):
                narrow[array][first : first + 48, :] = wide[array][first : first + 48, :].astype(BF)
        if k == 0:
            pl.semaphore_wait(pltpu.get_barrier_semaphore(), expected)
        pl.when(stays)(lambda: kept(k).start())
        pl.when(direct)(lambda: brought(k, me.dp()).start())
        pl.when(crosses)(lambda: crossed(k).start())
    turn_start(1)
    loads[4].wait()
    pad(x_raw, x_pad)
    turn_start(0)
    x_save = pltpu.make_async_copy(x_pad, x_all, load_sem.at[4])
    x_save.start()
    loads[5].wait()
    pad(g_raw, g_pad)
    for k in range(len(pieces) + 3):
        if k < len(pieces):
            @pl.when(crosses)
            def _():
                crossed(k).wait_recv()
                brought_on(k, me.dp()).start()

        if k == len(pieces) - 1:
            for i in range(2, 2 + micro):
                turn_start(i)
        b = k - 1
        if 0 <= b < len(pieces):
            pl.when(stays)(lambda: kept(b).wait())
            pl.when(moves)(lambda: brought(b, own).wait_recv())
            passed(1, b, own, xn).start()
            passed(2, b, own, yn).start()
            passed(4, b, own, cn).start()
        b = k - 2
        if 0 <= b < len(pieces):
            turn_x = (me.c == 0) if pieces[b][3] == "c" else (me.c < 0)
            passed(1, b, own_x, xn).wait_recv()
            pl.when(turn_x)(lambda: passed(3, b, own_x, yn).start())
            passed(5, b, own_x, cn).start()
            passed(2, b, own_y, yn).wait_recv()
            pl.when(jnp.logical_not(turn_x))(lambda: passed(3, b, own_y, xn).start())
            passed(6, b, own_y, cn).start()
        b = k - 3
        if 0 <= b < len(pieces):
            passed(3, b, own_d, yn).wait_recv()
            passed(7, b, own_d, cn).start()
    for k in range(len(pieces)):
        for kind in range(4, 8):
            passed(kind, k, beside[kind - 4], cn).wait_recv()
        pl.when(moves)(lambda: brought(k, own).wait_send())
        pl.when(crosses)(lambda: crossed(k).wait_send())
        for kind in range(1, 8):
            passed(kind, k, own, cn).wait_send()
    for i in range(len(turns)):
        turn_end(i)
    x_save.wait()


def run_gather(masters, inputs, g, words, rows):
    pieces = GATHER_PIECES
    micro, _, width = g.shape
    shape = jax.ShapeDtypeStruct
    shares = [shape(m.shape, BF) for m in masters[:4]] + [shape(masters[4].shape, F32)]
    many = shape((micro, rows, width), BF)
    outs = [shape((s.shape[0] * 8,) + s.shape[1:], s.dtype) for s in shares]
    outs += [shape((rows, width), BF), many, many, shape(words.shape, words.dtype)]
    return pl.pallas_call(
        functools.partial(gather_kernel, pieces, micro),
        out_shape=outs,
        in_specs=[ANYWHERE] * 8,
        out_specs=[ANYWHERE] * 9,
        scratch_shapes=[pltpu.VMEM(s.shape, s.dtype) for s in shares] + [pltpu.VMEM(m.shape, F32) for m in masters[:4]]
        + [pltpu.VMEM(s.shape, BF) for s in shares[:4]] + [pltpu.VMEM(g.shape, BF)] * 2
        + [pltpu.VMEM((micro, rows, width), BF)] * 2
        + [DMA((9, len(pieces))), DMA((9, len(pieces))), DMA((len(pieces),)), DMA((2 + micro,)), DMA((2 + micro,)),
           DMA((6,))],
        compiler_params=pltpu.CompilerParams(collective_id=2, has_side_effects=True, vmem_limit_bytes=VMEM_CAP),
        name="gather_layers",
    )(*masters, inputs, g, words)


SCATTER_PIECES = ((3, 0, 128, 0, 768, "x"), (3, 128, 128, 0, 768, "x"), (3, 256, 128, 0, 768, "x"),
                  (2, 0, 96, 0, 1024, "x"), (2, 0, 96, 1024, 1024, "x"), (2, 0, 96, 2048, 1024, "x"),
                  (0, 0, 96, 0, 768, "x"), (0, 0, 96, 768, 768, "x"), (0, 0, 96, 1536, 768, "x"),
                  (1, 0, 96, 0, 768, "x"), (4, 0, 16, 0, 128, "x"))


def scatter_kernel(pieces, micro, *refs):
    count = 5
    a_h, r_h, o_h, f_h, a2_h, dz_h, u_h, g_h, small_h, gin_in = refs[:10]
    outs, gin_o, norm_o = refs[10:15], refs[15], refs[16]
    at = 17
    totals, beside, diag, from_x, from_y, done, swap, home = (refs[at + i * count : at + (i + 1) * count] for i in range(8))
    (stream, fixed, flipped, sums, tallies, stream_sem, fixed_sem, send, recv, local, turn_sem, note_send, note_recv,
     out_sem) = refs[at + 8 * count :]
    me = Spot.here()
    xn, yn, cn = me.flip(x=1), me.flip(y=1), me.flip(c=1)
    target, giver, back, ahead = me.source(), me.drop(), me.back(), me.ahead()
    stays, alone = same(me, target), same(me, back)
    moves, pairs = jnp.logical_not(stays), jnp.logical_not(alone)
    crosses, target_crosses = me.crosses(), target.crosses()
    slab = [me.flip(x=i & 1, y=(i >> 1) & 1, c=i >> 2) for i in range(1, 8)]
    column = [Spot(me.x, me.y, (me.z + i) % 4, me.c) for i in range(1, 4)]
    left_right = {0: (a_h, r_h), 1: (o_h, f_h), 2: (a2_h, dz_h), 3: (u_h, g_h)}
    resting = (g_h, a2_h, a_h, o_h)
    rest_at = {3: 0, 2: 1, 0: 2, 1: 3}

    def streamed(k):
        array, first, size, column_at, columns, _ = pieces[k]
        slot = k % 2
        if array == 3:
            share = totals[3].shape[0] // 8
            return [pltpu.make_async_copy(u_h.at[:, pl.ds(p * share + first, size)],
                                          stream.at[slot, :, pl.ds(p * size, size)], stream_sem.at[slot, p])
                    for p in range(8)]
        if array == 4:
            return [pltpu.make_async_copy(small_h, totals[4], stream_sem.at[slot, 0])]
        return [pltpu.make_async_copy(left_right[array][1].at[:, pl.ds(column_at, columns)],
                                      stream.at[slot, :, pl.ds(0, columns)], stream_sem.at[slot, 0])]

    def rested(i):
        return pltpu.make_async_copy(resting[i], fixed.at[i], fixed_sem.at[i])

    for copy in streamed(0):
        copy.start()
    rested(0).start()
    for copy in streamed(1):
        copy.start()
    for i in range(1, 4):
        rested(i).start()
    for spot in slab + column:
        hail(spot)

    @pl.when(moves)
    def _():
        hail(target)
        hail(giver)

    @pl.when(pairs)
    def _():
        hail(back)
        hail(ahead)

    def work(k):
        array, first, size, column_at, columns, _ = pieces[k]
        slot = k % 2
        for copy in streamed(k):
            copy.wait()
        if array == 4:
            return
        if array == 3:
            if first == 0:
                rested(rest_at[3]).wait()
            share = totals[3].shape[0] // 8
            for p in range(0, 8, 2):
                both = lax.dot_general(stream[slot, :, p * size : (p + 2) * size], fixed[rest_at[3]], TN,
                                       preferred_element_type=F32).astype(BF)
                for i in range(2):
                    totals[3][(p + i) * share + first : (p + i) * share + first + size, :] = both[i * size : (i + 1) * size]
        else:
            if column_at == 0:
                rested(rest_at[array]).wait()
                flipped[...] = fixed[rest_at[array]].T
            for c in range(0, columns, 256):
                totals[array][:, column_at + c : column_at + c + 256] = mm(flipped[...], stream[slot, :, c : c + 256]).astype(BF)
        if k + 2 < len(pieces):
            for copy in streamed(k + 2):
                copy.start()

    def parts(spot):
        return [s.part() for s in (spot, spot.flip(x=1), spot.flip(y=1), spot.flip(x=1, y=1))]

    kept, given = parts(me), parts(cn)

    def box(k):
        _, first, size, column_at, columns, _ = pieces[k]
        return pl.ds(first, size), pl.ds(column_at, columns)

    def whole(k, part):
        array, first, size, column_at, columns, _ = pieces[k]
        share = done[array].shape[0]
        return totals[array].at[pl.ds(pl.multiple_of(part * share + first, 16), size), pl.ds(column_at, columns)]

    def remote(src, dst, kind, k, spot):
        return pltpu.make_async_remote_copy(
            src_ref=src, dst_ref=dst, send_sem=send.at[kind, k], recv_sem=recv.at[kind, k],
            device_id=spot.id(), device_id_type=MESH)

    def of(refs_, k):
        return refs_[pieces[k][0]].at[box(k)]

    def crossed(k, j):
        return remote(whole(k, given[j]), beside[pieces[k][0]].at[(j,) + box(k)], j, k, cn)

    def to_diag(k, spot):
        return remote(whole(k, kept[3]), of(diag, k), 4, k, spot)

    def to_x(k):
        return remote(whole(k, kept[1]), of(from_x, k), 5, k, xn)

    def to_y(k):
        return remote(whole(k, kept[2]), of(from_y, k), 6, k, yn)

    def to_home(k):
        return remote(of(done, k), of(home, k), 7, k, target)

    def to_swap(k):
        return remote(of(done, k), of(swap, k), 7, k, target)

    def stay_home(k):
        return pltpu.make_async_copy(of(done, k), of(home, k), local.at[k])

    def over(k):
        return remote(of(swap, k), of(home, k), 8, k, yn)

    def add(k, j, extra):
        here = whole(k, kept[j])
        here[...] = (here[...].astype(F32) + extra.astype(F32)).astype(here.dtype)

    def turn(m):
        return pltpu.make_async_remote_copy(
            src_ref=gin_in.at[m], dst_ref=gin_o.at[m], send_sem=turn_sem.at[0, m], recv_sem=turn_sem.at[1, m],
            device_id=back.id(), device_id_type=MESH)

    def turn_stay(m):
        return pltpu.make_async_copy(gin_in.at[m], gin_o.at[m], turn_sem.at[0, m])

    work(0)
    pl.semaphore_wait(pltpu.get_barrier_semaphore(), 10 + jnp.where(stays, 0, 2) + jnp.where(alone, 0, 2))
    for m in range(micro):
        now = (me.z >= 2) | (m == micro - 1)
        pl.when(alone & now)(lambda: turn_stay(m).start())
        pl.when(pairs & now)(lambda: turn(m).start())
    tally = jnp.zeros((8, 128), F32)
    for k in range(len(pieces) + 4):
        if k < len(pieces):
            if k > 0:
                work(k)
            for j in (3, 2, 1, 0):
                crossed(k, j).start()
        b = k - 1
        if 0 <= b < len(pieces):
            turn_x = (me.c == 0) if pieces[b][5] == "c" else (me.c < 0)
            for j in (3, 2, 1, 0):
                crossed(b, j).wait_recv()
                add(b, j, beside[pieces[b][0]][(j,) + box(b)])
                if j == 3:
                    pl.when(turn_x)(lambda: to_diag(b, yn).start())
                    pl.when(jnp.logical_not(turn_x))(lambda: to_diag(b, xn).start())
                if j == 2:
                    pl.when(turn_x)(lambda: to_y(b).start())
                if j == 1:
                    pl.when(jnp.logical_not(turn_x))(lambda: to_x(b).start())
        b = k - 2
        if 0 <= b < len(pieces):
            to_diag(b, yn).wait_recv()
            turn_x = (me.c == 0) if pieces[b][5] == "c" else (me.c < 0)

            @pl.when(turn_x)
            def _():
                add(b, 1, of(diag, b)[...])
                to_x(b).start()

            @pl.when(jnp.logical_not(turn_x))
            def _():
                add(b, 2, of(diag, b)[...])
                to_y(b).start()
        b = k - 3
        if 0 <= b < len(pieces):
            to_x(b).wait_recv()
            to_y(b).wait_recv()
            total = (whole(b, kept[0])[...].astype(F32) + of(from_x, b)[...].astype(F32) + of(from_y, b)[...].astype(F32))
            total = total.astype(done[pieces[b][0]].dtype)
            done[pieces[b][0]][box(b)] = total
            square = total.astype(F32) * total.astype(F32)
            for c in range(0, square.shape[1], 128):
                tally = tally + jnp.sum(square[:, c : c + 128].reshape(-1, 8, 128), axis=0)
            pl.when(stays)(lambda: stay_home(b).start())
            pl.when(moves & jnp.logical_not(target_crosses))(lambda: to_home(b).start())
            pl.when(target_crosses)(lambda: to_swap(b).start())
        b = k - 4
        if 0 <= b < len(pieces):
            @pl.when(crosses)
            def _():
                to_swap(b).wait_recv()
                over(b).start()
    sums[0] = tally

    def note(i, src, slot, spot):
        return pltpu.make_async_remote_copy(
            src_ref=src, dst_ref=tallies.at[slot], send_sem=note_send.at[i], recv_sem=note_recv.at[slot],
            device_id=spot.id(), device_id_type=MESH)

    for i, spot in enumerate(column):
        note(i, sums.at[0], i, spot).start()
    for i, spot in enumerate(column):
        note(i, sums.at[0], i, spot).wait_recv()
        tally = tally + tallies[i]
    sums[1] = tally
    for i, spot in enumerate(slab):
        note(3 + i, sums.at[1], 3 + i, spot).start()
    for i, spot in enumerate(slab):
        note(3 + i, sums.at[1], 3 + i, spot).wait_recv()
        tally = tally + tallies[3 + i]
    whole_norm = jnp.sqrt(jnp.sum(jnp.sum(tally, axis=0, keepdims=True), axis=1, keepdims=True))
    norm_o[...] = jnp.broadcast_to(whole_norm, norm_o.shape)
    last = {}
    for k in range(len(pieces)):
        last[pieces[k][0]] = k
    for k in range(len(pieces)):
        pl.when(stays)(lambda: stay_home(k).wait())
        pl.when(moves & jnp.logical_not(crosses))(lambda: to_home(k).wait_recv())
        pl.when(crosses)(lambda: over(k).wait_recv())
        array = pieces[k][0]
        if last[array] == k:
            pltpu.make_async_copy(home[array], outs[array], out_sem.at[array]).start()
    for i, spot in enumerate(column):
        note(i, sums.at[0], i, spot).wait_send()
    for i, spot in enumerate(slab):
        note(3 + i, sums.at[1], 3 + i, spot).wait_send()
    for k in range(len(pieces)):
        for j in range(4):
            crossed(k, j).wait_send()
        to_diag(k, yn).wait_send()
        to_x(k).wait_send()
        to_y(k).wait_send()
        pl.when(moves)(lambda: to_home(k).wait_send())
        pl.when(crosses)(lambda: over(k).wait_send())
    for m in range(micro):
        now, then = (me.z >= 2) | (m == micro - 1), (me.section() >= 2) | (m == micro - 1)
        pl.when(alone & now)(lambda: turn_stay(m).wait())
        pl.when(pairs & now)(lambda: turn(m).wait_send())
        pl.when(pairs & then)(lambda: turn(m).wait_recv())
    for array in range(count):
        pltpu.make_async_copy(home[array], outs[array], out_sem.at[array]).wait()


def run_scatter(operands, small, gin):
    pieces = SCATTER_PIECES
    micro = gin.shape[0]
    shape = jax.ShapeDtypeStruct
    a, r, o, f, a2, dz, u, g = operands = [v.reshape(-1, v.shape[-1]) for v in operands]
    rows = a.shape[0]
    sizes = [((left.shape[1], right.shape[1]), BF) for left, right in ((a, r), (o, f), (a2, dz), (u, g))]
    sizes.append((small.shape, F32))
    shares = [((s[0] // 8, s[1]), t) for s, t in sizes]
    one = [pltpu.VMEM(s, t) for s, t in shares]
    return pl.pallas_call(
        functools.partial(scatter_kernel, pieces, micro),
        out_shape=[shape(s, t) for s, t in shares] + [shape(gin.shape, gin.dtype), shape((8, 128), F32)],
        in_specs=[ANYWHERE] * 10,
        out_specs=[ANYWHERE] * 6 + [IN_VMEM],
        scratch_shapes=[pltpu.VMEM(s, t) for s, t in sizes] + [pltpu.VMEM((4,) + s, t) for s, t in shares] + one * 6
        + [pltpu.VMEM((2, rows, 1024), BF), pltpu.VMEM((4, rows, a.shape[1]), BF), pltpu.VMEM((a.shape[1], rows), BF),
           pltpu.VMEM((2, 8, 128), F32), pltpu.VMEM((10, 8, 128), F32), DMA((2, 8)), DMA((4,)),
           DMA((9, len(pieces))), DMA((9, len(pieces))), DMA((len(pieces),)), DMA((2, micro)), DMA((10,)), DMA((10,)),
           DMA((5,))],
        compiler_params=pltpu.CompilerParams(collective_id=3, has_side_effects=True, vmem_limit_bytes=VMEM_CAP),
        name="scatter_layers",
    )(*operands, small, gin)


def finish_kernel(order, micro, norm, *refs):
    shards_h, state_h, (acts_early, acts_late, gin_early, gin_late) = refs[:4], refs[4:16], refs[16:20]
    state_o, acts_o, gin_o = refs[20:36], refs[36], refs[37]
    shards, state, (acts, gin, acts_cut, gin_cut) = refs[38:42], refs[42:58], refs[58:62]
    load_sem, pick_sem, out_sem = refs[62:]
    upper = lax.axis_index("section") >= 2

    def loads(array):
        copies = [pltpu.make_async_copy(shards_h[array], shards[array], load_sem.at[array, 0])]
        for i in range(3):
            copies.append(pltpu.make_async_copy(state_h[4 * i + array], state[4 * (i + 1) + array], load_sem.at[array, 1 + i]))
        return copies

    def pick(i, m, src, dst):
        return pltpu.make_async_copy(src.at[m], dst.at[m], pick_sem.at[i, m])

    def saves(array):
        return [pltpu.make_async_copy(state[4 * i + array], state_o[4 * array + i], out_sem.at[array, i]) for i in range(4)]

    for array in order:
        for copy in loads(array):
            copy.start()
    for i, (early, late, dst, is_early) in enumerate(
            ((acts_early, acts_late, acts, upper), (gin_early, gin_late, gin, jnp.logical_not(upper)))):
        for m in range(micro):
            if m == micro - 1:
                pick(i, m, late, dst).start()
            else:
                pl.when(is_early)(lambda: pick(i, m, early, dst).start())
                pl.when(jnp.logical_not(is_early))(lambda: pick(i, m, late, dst).start())
    factor = 1.0 / jnp.maximum(norm[0:1, 0:1], 1.0)
    fix = 1.0 / (1.0 - 0.5**STEP)
    strip = 16
    for array in order:
        for copy in loads(array):
            copy.wait()
        grads, master, first, second = state[array], state[4 + array], state[8 + array], state[12 + array]

        def update(i, carry):
            rows = pl.ds(pl.multiple_of(i * strip, strip), strip)
            grad = shards[array][rows, :].astype(F32) * factor
            first_new = 0.5 * first[rows, :] + 0.5 * grad
            second_new = 0.5 * second[rows, :] + 0.5 * grad * grad
            old = master[rows, :]
            change = (first_new * fix) / (jnp.sqrt(second_new * fix) + adam_eps) + decay_rate * old
            grads[rows, :] = grad
            first[rows, :] = first_new
            second[rows, :] = second_new
            master[rows, :] = old - learn_rate * change
            return carry

        lax.fori_loop(0, grads.shape[0] // strip, update, 0)
        for copy in saves(array):
            copy.start()
    length = acts_cut.shape[1]
    for i, (src, cut, out) in enumerate(((acts, acts_cut, acts_o), (gin, gin_cut, gin_o))):
        for m in range(micro):
            pick(i, m, gin_late, src).wait()
            cut[m] = src[m, 0:length, :]
        pltpu.make_async_copy(cut, out, out_sem.at[4, i]).start()
    for array in order:
        for copy in saves(array):
            copy.wait()
    for i, (cut, out) in enumerate(((acts_cut, acts_o), (gin_cut, gin_o))):
        pltpu.make_async_copy(cut, out, out_sem.at[4, i]).wait()


def run_finish(norm, shards, states, tall, length):
    micro, rows, width = tall[0].shape
    shape = jax.ShapeDtypeStruct
    return pl.pallas_call(
        functools.partial(finish_kernel, (1, 0, 2, 3), micro),
        out_shape=[shape(s.shape, F32) for s in shards for _ in range(4)] + [shape((micro, length, width), BF)] * 2,
        in_specs=[IN_VMEM] + [ANYWHERE] * 20,
        out_specs=[ANYWHERE] * 18,
        scratch_shapes=[pltpu.VMEM(s.shape, BF) for s in shards]
        + [pltpu.VMEM(s.shape, F32) for _ in range(4) for s in shards]
        + [pltpu.VMEM((micro, rows, width), BF)] * 2 + [pltpu.VMEM((micro, length, width), BF)] * 2
        + [DMA((4, 4)), DMA((2, micro)), DMA((5, 4))],
        compiler_params=pltpu.CompilerParams(vmem_limit_bytes=VMEM_CAP),
        name="finish",
    )(norm, *shards, *states, *tall)


def split_small(small, width, slices):
    share = width // slices
    stacked = small.reshape(slices, small.shape[0] // slices)
    eight = stacked[:, : 8 * share].reshape(slices, 8, share).transpose(1, 0, 2).reshape(8, width)
    up = stacked[:, 8 * share :].reshape(-1, width)
    return jnp.concatenate([eight, up, jnp.zeros((16 - 8 - up.shape[0], width), small.dtype)], axis=0)


def join_small(table, total, slices):
    width = table.shape[1]
    share = width // slices
    ups = total // width - 8
    eight = table[:8].reshape(8, slices, share).transpose(1, 0, 2).reshape(slices, 8 * share)
    up = table[8 : 8 + ups].reshape(slices, -1)
    return jnp.concatenate([eight, up], axis=1).reshape(-1)


def weight_grad(left, right):
    rows = left.shape[0] * left.shape[1]
    return lax.dot_general(left.reshape(rows, -1), right.reshape(rows, -1), (((0,), (0,)), ((), ())),
                           preferred_element_type=F32)


def adam(grad, master, first, second, rate, decay):
    fix = 1.0 - 0.5**STEP
    first = 0.5 * first + 0.5 * grad
    second = 0.5 * second + 0.5 * grad * grad
    update = first / fix / (jnp.sqrt(second / fix) + adam_eps)
    if decay:
        update = update + decay * master
    return [grad, master - rate * update, first, second]


def per_device(inputs, out_grad, segment_ids, cls_index, *states):
    masters, firsts, seconds = states[0:5], states[5:10], states[10:15]
    slices = lax.axis_size("dp")
    stages = lax.axis_size("section")
    turned = slices == 8 and stages == 4
    seq_dev, length, width = inputs.shape
    rows = -(-length // 128) * 128
    share = masters[4].shape[1]
    total = share * slices

    segs = jnp.pad(segment_ids, ((0, 0), (0, rows - length)), constant_values=-1)
    words = jnp.concatenate([segs, jnp.broadcast_to(cls_index[:, None], (seq_dev, rows))], axis=0)
    if turned:
        line = Line("dp", 4, 2)
        eighth = width // slices
        flat = masters[4][0].astype(BF).astype(F32)
        small = jnp.concatenate([
            jnp.pad(flat[: 8 * eighth].reshape(8, eighth), ((0, 0), (0, 128 - eighth))),
            flat[8 * eighth :].reshape(-1, 128), jnp.zeros((8 - (share - 8 * eighth) // 128, 128), F32)], axis=0)
        *weights, small, x_first, x_in, g_in, words = run_gather(
            [m[0] for m in masters[:4]] + [small], inputs, out_grad, words, rows)
    else:
        line = Line("section", stages, 1)
        extra = ((0, 0), (0, rows - length), (0, 0))
        x_in, g_in = jnp.pad(inputs, extra), jnp.pad(out_grad, extra)
        gathered = [lax.all_gather(m[0].astype(BF), "dp", axis=0, tiled=True) for m in masters]
        weights, x_first = gathered[:4], x_in[0]
        small = split_small(gathered[4].astype(F32), width, slices)

    x, a, qkv, lse, o, h, a2, gp, u, acts, acts_early = run_forward(
        line, length, turned, x_first, x_in, words, weights, small)
    acts, gin_early, g, dz, f, r, gin, sums = run_backward(
        line, length, turned, acts, g_in, x, qkv, lse, h, gp, words, weights, small)
    results = []
    if turned:
        matrix_states = [v[0] for group in (masters, firsts, seconds) for v in group[:4]]
        *shards, table, gin, norm = run_scatter([a, r, o, f, a2, dz, u, g], sums, gin)
        *matrices, acts, gin = run_finish(norm, shards, matrix_states, [acts_early, acts, gin_early, gin], length)
        results = [v[None] for v in matrices]
        grad_norm = norm[0, 0]
        ups = (share - 8 * eighth) // 128
        small_share = jnp.concatenate([table[:8, :eighth].reshape(-1), table[8 : 8 + ups].reshape(-1)])[None]
        factor = 1.0 / jnp.maximum(grad_norm, 1.0)
        results += adam(small_share * factor, masters[4], firsts[4], seconds[4], small_rate, 0.0)
    else:
        acts, gin = acts[:, :length], gin[:, :length]
        totals = [weight_grad(a, r).astype(BF), weight_grad(o, f).astype(BF), weight_grad(a2, dz).astype(BF),
                  weight_grad(u, g).astype(BF), join_small(sums, total, slices)]
        shards = [lax.psum_scatter(t[None], "dp", scatter_dimension=1, tiled=True).astype(F32) for t in totals]
        squares = jnp.sum(jnp.stack([jnp.sum(s * s) for s in shards]))
        grad_norm = jnp.sqrt(lax.psum(squares, ("dp", "section")))
        factor = 1.0 / jnp.maximum(grad_norm, 1.0)
        for kind in range(5):
            rate, decay = (learn_rate, decay_rate) if kind < 4 else (small_rate, 0.0)
            results += adam(shards[kind] * factor, masters[kind], firsts[kind], seconds[kind], rate, decay)
    return (acts[None], gin[None], grad_norm.reshape(1)) + tuple(results)


def solution(mesh):
    matrix, vector = P("section", "dp", None), P("section", "dp")
    states = (matrix,) * 4 + (vector,)
    return jax.shard_map(
        per_device,
        mesh=mesh,
        in_specs=(P("dp", None, None), P("dp", None, None), P("dp", None), P("dp")) + states * 3,
        out_specs=(P("section", "dp", None, None), P("section", "dp", None, None), P())
        + (matrix,) * 16 + (vector,) * 4,
        check_vma=False,
    )
```

```python
import functools

import jax
import jax.numpy as jnp
from jax import lax
from jax.experimental import pallas as pl
from jax.experimental.pallas import tpu as pltpu
from jax.sharding import PartitionSpec as P

HEADS = 12
STEP = 3
F32 = jnp.float32
BF = jnp.bfloat16
MESH = pl.DeviceIdType.MESH
VMEM_CAP = 60 * 1024 * 1024
EARLY = 3
FIRST = 2

norm_eps = 1e-06
masked_score = -1e30
learn_rate = 0.05
small_rate = 0.3
decay_rate = 0.05
adam_eps = 1e-08

NT = (((1,), (1,)), ((), ()))
TN = (((0,), (0,)), ((), ()))


def mm(a, b):
    return jnp.dot(a, b, preferred_element_type=F32)


def mm_nt(a, b):
    return lax.dot_general(a, b, NT, preferred_element_type=F32)


def norm_parts(values):
    center = values - jnp.mean(values, axis=-1, keepdims=True)
    spread = jnp.mean(center * center, axis=-1, keepdims=True)
    inv = lax.rsqrt(spread + norm_eps)
    return center * inv, inv


def norm_back(y, normed, inv):
    pull = jnp.mean(y * normed, axis=-1, keepdims=True)
    return (y - jnp.mean(y, axis=-1, keepdims=True) - normed * pull) * inv


def column_sum(values):
    return jnp.sum(values, axis=0, keepdims=True)


def mask_bias(seg_row, seg_col, cls_row, length):
    size = seg_col.shape[0]
    key_at = lax.broadcasted_iota(jnp.int32, (size, size), 0)
    query_at = lax.broadcasted_iota(jnp.int32, (size, size), 1)
    allowed = (seg_row == seg_col) | (key_at == cls_row) | (query_at == cls_row)
    allowed = allowed & (key_at < length)
    return jnp.where(allowed, 0.0, masked_score).astype(F32)


def micro_bias(words, m, micro, length):
    seg_row, cls_row = words[pl.ds(m, 1), :], words[pl.ds(micro + m, 1), :]
    size = seg_row.shape[1]
    on_diagonal = lax.broadcasted_iota(jnp.int32, (size, size), 0) == lax.broadcasted_iota(jnp.int32, (size, size), 1)
    seg_col = jnp.sum(jnp.where(on_diagonal, seg_row.astype(F32), 0.0), axis=1, keepdims=True)
    return mask_bias(seg_row.astype(F32), seg_col, cls_row, length)


def spread_small(table, small):
    width = small.shape[1]
    share, ups = width // 8, width // 256
    small[...] = jnp.zeros_like(small)
    for i in range(8):
        small[0:8, i * share : (i + 1) * share] = table[16 * i : 16 * i + 8, 0:share]
        for j in range(ups):
            at = i % 2 * (width // 2) + j * 128
            small[8 + i // 2 : 9 + i // 2, at : at + 128] = table[16 * i + 8 + j : 16 * i + 9 + j, :]


def share_small(sums, table):
    width = sums.shape[1]
    share, ups = width // 8, width // 256
    table[...] = jnp.zeros_like(table)
    for i in range(8):
        table[16 * i : 16 * i + 8, 0:share] = sums[0:8, i * share : (i + 1) * share]
        for j in range(ups):
            at = i % 2 * (width // 2) + j * 128
            table[16 * i + 8 + j : 16 * i + 9 + j, :] = sums[8 + i // 2 : 9 + i // 2, at : at + 128]


def gelu_parts(z):
    density = jnp.exp(z * z * -0.5) * 0.3989422804014327
    below = 0.5 + 0.5 * lax.erf(z * 0.7071067811865476)
    return z * below, below + z * density


def layer_forward(x_ref, bias_ref, wqkv, wproj, wup, wdown, small, a_ref, qkv_ref, lse_ref, o_ref,
                  h_ref, a2_ref, gp_ref, u_ref, out_ref, ot_ref, before):
    rows, width = x_ref.shape
    hidden = wup.shape[1]
    normed, _ = norm_parts(x_ref[...].astype(F32))
    a_ref[...] = (normed * small[0:1, :] + small[1:2, :]).astype(BF)
    for part in range(3):
        cols = slice(part * width, (part + 1) * width)
        mixed = mm(a_ref[...], wqkv[:, cols])
        if part == 0:
            mixed = mixed + small[2:3, :]
        if part == 2:
            mixed = mixed + small[3:4, :]
        qkv_ref[:, cols] = mixed.astype(BF)
    lane = lax.broadcasted_iota(jnp.int32, (rows, 128), 1)
    scores, raised, inverse = {}, {}, {}
    for step in range(HEADS + 2):
        if step < HEADS:
            at = step // 2 * 128
            half = (lane < 64) if step % 2 == 0 else (lane >= 64)
            k = qkv_ref[:, width + at : width + at + 128]
            k = jnp.where(half, k, jnp.zeros_like(k)) * jnp.asarray(0.125, BF)
            scores[step] = mm_nt(k, qkv_ref[:, at : at + 128])
        head = step - 1
        if 0 <= head < HEADS:
            shifted = scores.pop(head) + bias_ref[...]
            peak = jnp.max(shifted, axis=0, keepdims=True)
            grown = jnp.exp(shifted - peak)
            summed = jnp.sum(grown, axis=0, keepdims=True)
            raised[head] = grown.astype(BF)
            inverse[head] = 1.0 / summed
            lse_ref[head : head + 1, :] = peak + jnp.log(summed)
        head = step - 2
        if 0 <= head < HEADS:
            if head % 2 == 0:
                vt = qkv_ref[:, 2 * width + head * 64 : 2 * width + head * 64 + 128].T
            mixed = mm(vt[head % 2 * 64 : head % 2 * 64 + 64, :], raised.pop(head)) * inverse.pop(head)
            ot_ref[head * 64 : head * 64 + 64, :] = mixed.astype(BF)
    o_ref[...] = ot_ref[...].T
    before(1)
    h = x_ref[...].astype(F32) + (mm(o_ref[...], wproj[...]) + small[4:5, :])
    h_ref[...] = h
    normed, _ = norm_parts(h)
    a2_ref[...] = (normed * small[5:6, :] + small[6:7, :]).astype(BF)
    before(2)
    chunk = width
    z = {}
    for step in range(hidden // chunk + 1):
        cols = slice(step * chunk, (step + 1) * chunk)
        if step < hidden // chunk:
            row, start = 8 + step * chunk // width, step * chunk % width
            z[step] = mm(a2_ref[...], wup[:, cols]) + small[row : row + 1, start : start + chunk]
        part = step - 1
        if 0 <= part < hidden // chunk:
            cols = slice(part * chunk, (part + 1) * chunk)
            u, slope = gelu_parts(z.pop(part))
            u_ref[:, cols] = u.astype(BF)
            gp_ref[:, cols] = slope.astype(BF)
    before(3)
    total = mm(u_ref[...], wdown[...])
    out_ref[...] = (h_ref[...] + (total + small[7:8, :])).astype(BF)


def layer_backward(g_ref, x_ref, bias_ref, qkv_ref, lse_ref, h_ref, gp_ref, wqkv, wproj, wup, wdown,
                   small, dz_ref, f_ref, r_ref, gin_ref, sums_ref, do_ref, dh_ref, dqt_ref, before):
    rows, width = x_ref.shape
    hidden = wup.shape[1]
    carried = g_ref[...].astype(F32)
    sums_ref[7:8, :] += column_sum(carried)
    back = {}
    for step in range(hidden // width + 1):
        if step < hidden // width:
            back[step] = mm_nt(g_ref[...], wdown[step * width : (step + 1) * width, :])
        part = step - 1
        if part >= 0:
            cols = slice(part * width, (part + 1) * width)
            dz = (back.pop(part) * gp_ref[:, cols].astype(F32)).astype(BF)
            dz_ref[:, cols] = dz
            sums_ref[8 + part : 9 + part, :] += column_sum(dz.astype(F32))
    before(1)
    back = mm_nt(dz_ref[...], wup[...])
    normed, inv = norm_parts(h_ref[...])
    sums_ref[5:6, :] += column_sum(back * normed)
    sums_ref[6:7, :] += column_sum(back)
    dh = carried + norm_back(back * small[5:6, :], normed, inv)
    dh_ref[...] = dh
    f = dh.astype(BF)
    f_ref[...] = f
    sums_ref[4:5, :] += column_sum(f.astype(F32))
    before(2)
    do_ref[...] = mm_nt(f_ref[...], wproj[...]).astype(BF)
    lane = lax.broadcasted_iota(jnp.int32, (rows, 128), 1)
    scores, grads, probs, slopes, dks, dvs = {}, {}, {}, {}, {}, {}
    eighth = jnp.asarray(0.125, BF)
    for step in range(HEADS + 2):
        if step < HEADS:
            at = step // 2 * 128
            half = (lane < 64) if step % 2 == 0 else (lane >= 64)
            k = qkv_ref[:, width + at : width + at + 128]
            v = qkv_ref[:, 2 * width + at : 2 * width + at + 128]
            scores[step] = mm_nt(jnp.where(half, k, jnp.zeros_like(k)) * eighth, qkv_ref[:, at : at + 128])
            grads[step] = mm_nt(jnp.where(half, v, jnp.zeros_like(v)), do_ref[:, at : at + 128])
        head = step - 1
        if 0 <= head < HEADS:
            p = jnp.exp(scores.pop(head) + bias_ref[...] - lse_ref[head : head + 1, :])
            dp = grads.pop(head)
            inner = jnp.sum(p * dp, axis=0, keepdims=True)
            slopes[head] = (p * (dp - inner)).astype(BF)
            probs[head] = p.astype(BF)
        head = step - 2
        if 0 <= head < HEADS:
            at = head // 2 * 128
            side = head % 2
            ds = slopes.pop(head)
            dvs[side] = mm(probs.pop(head), do_ref[:, at : at + 128])
            dks[side] = mm(ds, qkv_ref[:, at : at + 128] * eighth)
            if side == 0:
                kt = (qkv_ref[:, width + at : width + at + 128] * eighth).T
            dqt_ref[head * 64 : head * 64 + 64, :] = mm(kt[side * 64 : side * 64 + 64, :], ds).astype(BF)
            if side == 1:
                r_ref[:, width + at : width + at + 128] = jnp.where(lane < 64, dks[0], dks[1]).astype(BF)
                r_ref[:, 2 * width + at : 2 * width + at + 128] = jnp.where(lane < 64, dvs[0], dvs[1]).astype(BF)
    r_ref[:, 0:width] = dqt_ref[...].T
    sums_ref[2:3, :] += column_sum(r_ref[:, 0:width].astype(F32))
    sums_ref[3:4, :] += column_sum(r_ref[:, 2 * width :].astype(F32))
    before(3)
    back = mm_nt(r_ref[...], wqkv[...])
    normed, inv = norm_parts(x_ref[...].astype(F32))
    sums_ref[0:1, :] += column_sum(back * normed)
    sums_ref[1:2, :] += column_sum(back)
    gin_ref[...] = (dh_ref[...] + norm_back(back * small[0:1, :], normed, inv)).astype(BF)


class Line:
    def __init__(self, axis, count, stride):
        self.axis, self.count, self.stride = axis, count, stride

    def stage(self):
        return lax.axis_index(self.axis) // self.stride

    def beside(self, by):
        return {self.axis: lax.axis_index(self.axis) + by * self.stride}


class Spot:
    def __init__(self, x, y, z, c):
        self.x, self.y, self.z, self.c = x, y, z, c

    @staticmethod
    def here():
        dp, section = lax.axis_index("dp"), lax.axis_index("section")
        return Spot(dp % 2, section // 2, dp // 2, section % 2)

    def dp(self):
        return self.z * 2 + self.x

    def section(self):
        return self.y * 2 + self.c

    def id(self):
        return (self.dp(), self.section())

    def flip(self, x=0, y=0, c=0):
        return Spot(1 - self.x if x else self.x, 1 - self.y if y else self.y, self.z, 1 - self.c if c else self.c)

    def ahead(self):
        return Spot(self.x, self.z % 2, self.section(), self.z // 2)

    def back(self):
        return Spot(self.x, self.z // 2, 2 * self.c + self.y, self.z % 2)

    def feeds(self, stage, core):
        return ((self.y == self.z % 2) & (self.c == core)) & (self.z >= 0)

    def fed_at(self, stage):
        return Spot(self.x, self.y, stage, self.z // 2)

    def feeder(self, core):
        return Spot(self.x, self.y, 2 * self.c + self.y, core)

    def gives_down(self):
        return self.back().z < self.z

    def takes_down(self):
        return self.z < self.section()

    def crosses(self):
        return (self.z + self.c) % 2 == 1

    def drop(self):
        return Spot(self.x, self.y, 2 * ((self.y + self.z + self.c) % 2) + self.c, self.z // 2)

    def source(self):
        c = self.z % 2
        return Spot(self.x, self.y, 2 * self.c + (self.y + self.z // 2 + c) % 2, c)

    def part(self):
        return self.source().dp()


def same(one, other):
    return (one.dp() == other.dp()) & (one.section() == other.section())


def hail(spot):
    pl.semaphore_signal(pltpu.get_barrier_semaphore(), inc=1, device_id=spot.id(), device_id_type=MESH)


def hail_stagger(me, leading, by):
    waits = (me.z == leading) & (me.c == 1)
    tells = (me.z == leading + by) & (me.c == 0)
    pl.when(waits)(lambda: hail(Spot(me.x, me.y, me.z + by, 0)))
    pl.when(tells)(lambda: hail(Spot(me.x, me.y, me.z - by, 1)))
    return jnp.where(waits, 1, 0) + jnp.where(tells, 1, 0)


def tell_stagger(me, leading, by, token, m):
    @pl.when((me.z == leading + by) & (me.c == 0) & (m == 0))
    def _():
        pl.semaphore_signal(token, inc=1, device_id=Spot(me.x, me.y, me.z - by, 1).id(), device_id_type=MESH)


def wait_stagger(me, leading, token, m):
    @pl.when((me.z == leading) & (me.c == 1) & (m == 0))
    def _():
        pl.semaphore_wait(token, 1)


def hail_feeding(me, stage, core):
    gives = me.feeds(stage, core) & jnp.logical_not(same(me, me.fed_at(stage)))
    takes = (me.z == stage) & jnp.logical_not(same(me, me.feeder(core)))
    pl.when(gives)(lambda: hail(me.fed_at(stage)))
    pl.when(takes)(lambda: hail(me.feeder(core)))
    return jnp.where(gives, 1, 0) + jnp.where(takes, 1, 0)


def greet(line, turned, feeding=False):
    stage = line.stage()
    barrier = pltpu.get_barrier_semaphore()

    @pl.when(stage > 0)
    def _():
        pl.semaphore_signal(barrier, inc=1, device_id=line.beside(-1), device_id_type=MESH)

    @pl.when(stage < line.count - 1)
    def _():
        pl.semaphore_signal(barrier, inc=1, device_id=line.beside(1), device_id_type=MESH)

    expected = jnp.where(stage > 0, 1, 0) + jnp.where(stage < line.count - 1, 1, 0)
    if turned:
        me = Spot.here()
        alone = same(me, me.back())

        @pl.when(jnp.logical_not(alone))
        def _():
            hail(me.back())
            hail(me.ahead())

        expected = expected + jnp.where(alone, 0, 2)
        if feeding:
            expected = expected + hail_feeding(me, 0, 0) + hail_stagger(me, 0, 1)
        else:
            expected = expected + hail_stagger(me, line.count - 1, -1)
    pl.semaphore_wait(barrier, expected)


def forward_kernel(line, length, turned, x_first, x_in, words, wqkv_h, wproj_h, wup_h, wdown_h, small_in,
                   x_o, a_o, qkv_o, lse_o, o_o, h_o, a2_o, gp_o, u_o, acts_o, home_o,
                   wqkv, wproj, wup, wdown, xs, outs, a, qkv, lse, o, h, a2, gp, u, bias, ot, small,
                   w_sem, in_sem, x_sem, save_sem, act_sem, send_sem, recv_sem, home_sem, token):
    micro = xs.shape[0]
    stage = line.stage()
    loads = [
        pltpu.make_async_copy(src, dst, w_sem.at[i])
        for i, (src, dst) in enumerate(((wqkv_h, wqkv), (wproj_h, wproj), (wup_h, wup), (wdown_h, wdown)))
    ]
    loads[0].start()

    def first_in(m):
        return pltpu.make_async_copy(x_in.at[m], xs.at[m], in_sem.at[m])

    if turned:
        spread_small(small_in, small)
    else:
        small[...] = small_in[...]
    greet(line, turned, feeding=True)
    if turned:
        me = Spot.here()
        back = me.back()

        def turn_in(m):
            return pltpu.make_async_remote_copy(
                src_ref=x_in.at[m], dst_ref=xs.at[m], send_sem=in_sem.at[m], recv_sem=recv_sem.at[m],
                device_id=taker.id(), device_id_type=MESH)

        taker, feeder = me.fed_at(0), me.feeder(0)
        feeds = me.feeds(0, 0) & jnp.logical_not(same(me, taker))
        feeds_self = me.feeds(0, 0) & same(me, taker)
        homing, homed = me.gives_down(), me.takes_down()

        def home(m):
            return pltpu.make_async_remote_copy(
                src_ref=outs.at[m], dst_ref=home_o.at[m], send_sem=home_sem.at[0, m], recv_sem=home_sem.at[1, m],
                device_id=back.id(), device_id_type=MESH)

        @pl.when(stage == 0)
        def _():
            for m in range(FIRST):
                pltpu.make_async_copy(x_first.at[m], xs.at[m], in_sem.at[m]).start()

        for m in range(FIRST, micro):
            @pl.when(feeds)
            def _():
                turn_in(m).start()

            @pl.when(feeds_self)
            def _():
                first_in(m).start()
    else:
        @pl.when(stage == 0)
        def _():
            for m in range(micro):
                first_in(m).start()

    loads[0].wait()
    for load in loads[1:]:
        load.start()

    saved = ((a, a_o), (qkv, qkv_o), (lse, lse_o), (o, o_o), (h, h_o), (a2, a2_o), (gp, gp_o), (u, u_o))

    def saves(m, slot):
        return [
            pltpu.make_async_copy(here.at[slot], there.at[m], save_sem.at[slot, i])
            for i, (here, there) in enumerate(saved)
        ]

    def hop(m):
        return pltpu.make_async_remote_copy(
            src_ref=outs.at[m], dst_ref=xs.at[m], send_sem=send_sem.at[m], recv_sem=recv_sem.at[m],
            device_id=line.beside(1), device_id_type=MESH)

    def step(m, carry):
        slot = lax.rem(m, 2)

        if turned:
            here = jnp.logical_or(feeds_self, jnp.logical_and(stage == 0, m < FIRST))
        else:
            here = stage == 0

        @pl.when(here)
        def _():
            first_in(m).wait()

        @pl.when(jnp.logical_not(here))
        def _():
            hop(m).wait_recv()

        if turned:
            tell_stagger(me, 0, 1, token, m)
        pltpu.make_async_copy(xs.at[m], x_o.at[m], x_sem.at[m]).start()

        @pl.when(m >= 2)
        def _():
            for save in saves(m - 2, slot):
                save.wait()

        bias[...] = micro_bias(words, m, micro, length)

        def before(i):
            @pl.when(m == 0)
            def _():
                loads[i].wait()

        layer_forward(xs.at[m], bias, wqkv, wproj, wup, wdown, small, a.at[slot], qkv.at[slot],
                      lse.at[slot], o.at[slot], h.at[slot], a2.at[slot], gp.at[slot], u.at[slot],
                      outs.at[m], ot, before)

        if turned:
            wait_stagger(me, 0, token, m)

        @pl.when(stage < line.count - 1)
        def _():
            hop(m).start()

        for save in saves(m, slot):
            save.start()
        pltpu.make_async_copy(outs.at[m], acts_o.at[m], act_sem.at[m]).start()
        if turned:
            pl.when(homing & (m < EARLY))(lambda: home(m).start())
        return carry

    lax.fori_loop(0, micro, step, 0)

    for m in range(max(micro - 2, 0), micro):
        for save in saves(m, m % 2):
            save.wait()
    for m in range(micro):
        pltpu.make_async_copy(xs.at[m], x_o.at[m], x_sem.at[m]).wait()
        pltpu.make_async_copy(outs.at[m], acts_o.at[m], act_sem.at[m]).wait()

    @pl.when(stage < line.count - 1)
    def _():
        for m in range(micro):
            hop(m).wait_send()

    if turned:
        @pl.when(feeds)
        def _():
            for m in range(FIRST, micro):
                turn_in(m).wait_send()

        for m in range(EARLY):
            pl.when(homing)(lambda: home(m).wait_send())
            pl.when(homed)(lambda: home(m).wait_recv())


def backward_kernel(line, length, turned, acts_h, g_in, x_h, qkv_h, lse_h, h_h, gp_h, words,
                    wqkv_h, wproj_h, wup_h, wdown_h, small_in,
                    acts_o, home_o, g_o, dz_o, f_o, r_o, gin_o, sums_out,
                    wqkv, wproj, wup, wdown, gs, gins, x, qkv, lse, h, gp, dz, f, r, bias, do, dh, dqt, small, sums_o,
                    w_sem, in_sem, g_sem, load_sem, save_sem, act_sem, send_sem, recv_sem, home_sem, back_sem, token):
    micro = gs.shape[0]
    stage = line.stage()
    loads = [
        pltpu.make_async_copy(src, dst, w_sem.at[i])
        for i, (src, dst) in enumerate(((wdown_h, wdown), (wup_h, wup), (wproj_h, wproj), (wqkv_h, wqkv)))
    ]

    def last_in(m):
        return pltpu.make_async_copy(g_in.at[m], gs.at[m], in_sem.at[m])

    @pl.when(stage == line.count - 1)
    def _():
        for m in range(micro):
            last_in(m).start()

    kept = ((gp_h, gp), (h_h, h), (qkv_h, qkv), (lse_h, lse), (x_h, x))

    def fetches(m, slot):
        return [
            pltpu.make_async_copy(there.at[m], here.at[slot], load_sem.at[slot, i])
            for i, (there, here) in enumerate(kept)
        ]

    loads[0].start()
    fetches(0, 0)[0].start()
    sums_o[...] = jnp.zeros_like(sums_o)
    if turned:
        spread_small(small_in, small)
    else:
        small[...] = small_in[...]
    greet(line, turned)
    if turned:
        me = Spot.here()
        back = me.back()
        alone = same(me, back)

        def home(m):
            return pltpu.make_async_remote_copy(
                src_ref=acts_h.at[m], dst_ref=acts_o.at[m], send_sem=home_sem.at[0, m], recv_sem=home_sem.at[1, m],
                device_id=back.id(), device_id_type=MESH)

        def stay(m):
            return pltpu.make_async_copy(acts_h.at[m], acts_o.at[m], home_sem.at[0, m])

        pairs = jnp.logical_not(alone)
        low, low_home = jnp.logical_not(me.gives_down()), jnp.logical_not(me.takes_down())

        def home_back(m):
            return pltpu.make_async_remote_copy(
                src_ref=gins.at[m], dst_ref=home_o.at[m], send_sem=back_sem.at[0, m], recv_sem=back_sem.at[1, m],
                device_id=back.id(), device_id_type=MESH)

        def settle_back(m):
            return pltpu.make_async_copy(gins.at[m], home_o.at[m], back_sem.at[0, m])

        for m in range(micro):
            now = low | (m >= EARLY)
            pl.when(alone & now)(lambda: stay(m).start())
            pl.when(pairs & now)(lambda: home(m).start())
    else:
        for m in range(micro):
            pltpu.make_async_copy(acts_h.at[m], acts_o.at[m], home_sem.at[0, m]).start()

    loads[0].wait()
    for load, some in zip(loads[1:], ((1,), (2, 3), (4,))):
        for i in some:
            fetches(0, 0)[i].start()
        load.start()
    saved = ((dz, dz_o), (f, f_o), (r, r_o))

    def saves(m, slot):
        return [
            pltpu.make_async_copy(here.at[slot], there.at[m], save_sem.at[slot, i])
            for i, (here, there) in enumerate(saved)
        ]

    def hop(m):
        return pltpu.make_async_remote_copy(
            src_ref=gins.at[m], dst_ref=gs.at[m], send_sem=send_sem.at[m], recv_sem=recv_sem.at[m],
            device_id=line.beside(-1), device_id_type=MESH)

    def step(m, carry):
        slot = lax.rem(m, 2)

        @pl.when(m + 1 < micro)
        def _():
            for fetch in fetches(m + 1, 1 - slot):
                fetch.start()

        def before(i):
            @pl.when(m == 0)
            def _():
                loads[i].wait()

            for at in ((), (1,), (2, 3), (4,))[i]:
                fetches(m, slot)[at].wait()

        fetches(m, slot)[0].wait()
        bias[...] = micro_bias(words, m, micro, length)

        @pl.when(m >= 2)
        def _():
            for save in saves(m - 2, slot):
                save.wait()

        @pl.when(stage == line.count - 1)
        def _():
            last_in(m).wait()

        @pl.when(stage < line.count - 1)
        def _():
            hop(m).wait_recv()

        if turned:
            tell_stagger(me, line.count - 1, -1, token, m)
        pltpu.make_async_copy(gs.at[m], g_o.at[m], g_sem.at[m]).start()
        layer_backward(gs.at[m], x.at[slot], bias, qkv.at[slot], lse.at[slot], h.at[slot], gp.at[slot],
                       wqkv, wproj, wup, wdown, small, dz.at[slot], f.at[slot], r.at[slot], gins.at[m],
                       sums_o, do, dh, dqt, before)

        if turned:
            wait_stagger(me, line.count - 1, token, m)

        @pl.when(stage > 0)
        def _():
            hop(m).start()

        for save in saves(m, slot):
            save.start()
        pltpu.make_async_copy(gins.at[m], gin_o.at[m], act_sem.at[m]).start()
        if turned:
            pl.when(pairs & low & (m < micro - 1))(lambda: home_back(m).start())
            pl.when(alone & low & (m < micro - 1))(lambda: settle_back(m).start())
        return carry

    lax.fori_loop(0, micro, step, 0)
    if turned:
        share_small(sums_o, sums_out)
    else:
        sums_out[...] = sums_o[...]

    for m in range(max(micro - 2, 0), micro):
        for save in saves(m, m % 2):
            save.wait()
    for m in range(micro):
        pltpu.make_async_copy(gs.at[m], g_o.at[m], g_sem.at[m]).wait()
        pltpu.make_async_copy(gins.at[m], gin_o.at[m], act_sem.at[m]).wait()

    @pl.when(stage > 0)
    def _():
        for m in range(micro):
            hop(m).wait_send()

    for m in range(micro):
        if turned:
            now, then = low | (m >= EARLY), low_home | (m >= EARLY)
            pl.when(alone & now)(lambda: stay(m).wait())
            pl.when(pairs & now)(lambda: home(m).wait_send())
            pl.when(pairs & then)(lambda: home(m).wait_recv())
            if m < micro - 1:
                pl.when(pairs & low)(lambda: home_back(m).wait_send())
                pl.when(pairs & low_home)(lambda: home_back(m).wait_recv())
                pl.when(alone & low)(lambda: settle_back(m).wait())
        else:
            pltpu.make_async_copy(acts_h.at[m], acts_o.at[m], home_sem.at[0, m]).wait()


IN_VMEM = pl.BlockSpec(memory_space=pltpu.VMEM)
IN_SMEM = pl.BlockSpec(memory_space=pltpu.SMEM)
ANYWHERE = pl.BlockSpec(memory_space=pl.ANY)
DMA = pltpu.SemaphoreType.DMA


def run_forward(line, length, turned, x_first, x_in, words, weights, small):
    micro, rows, width = x_in.shape
    hidden = weights[2].shape[1]
    shape = jax.ShapeDtypeStruct
    saved = (
        ((rows, width), BF), ((rows, 3 * width), BF), ((16, rows), F32), ((rows, width), BF),
        ((rows, width), F32), ((rows, width), BF), ((rows, hidden), BF), ((rows, hidden), BF))
    many = shape((micro, rows, width), BF)
    return pl.pallas_call(
        functools.partial(forward_kernel, line, length, turned),
        out_shape=[many] + [shape((micro,) + s, t) for s, t in saved] + [many, many],
        in_specs=[ANYWHERE, ANYWHERE, IN_VMEM] + [ANYWHERE] * 4 + [IN_VMEM],
        out_specs=[ANYWHERE] * 11,
        scratch_shapes=[pltpu.VMEM(w.shape, BF) for w in weights]
        + [pltpu.VMEM((micro, rows, width), BF)] * 2
        + [pltpu.VMEM((2,) + s, t) for s, t in saved]
        + [pltpu.VMEM((rows, rows), F32), pltpu.VMEM((width, rows), BF), pltpu.VMEM((16, width), F32)]
        + [DMA((4,)), DMA((micro,)), DMA((micro,)), DMA((2, 8)), DMA((micro,)), DMA((micro,)), DMA((micro,)),
           DMA((2, micro)), pltpu.SemaphoreType.REGULAR],
        compiler_params=pltpu.CompilerParams(
            collective_id=0, has_side_effects=True, vmem_limit_bytes=VMEM_CAP),
        name="forward_line",
    )(x_first, x_in, words, *weights, small)


def run_backward(line, length, turned, acts, g_in, x, qkv, lse, h, gp, words, weights, small):
    micro, rows, width = g_in.shape
    hidden = weights[2].shape[1]
    shape = jax.ShapeDtypeStruct
    many = shape((micro, rows, width), BF)
    wqkv, wproj, wup, wdown = weights
    return pl.pallas_call(
        functools.partial(backward_kernel, line, length, turned),
        out_shape=[many, many, many, shape((micro, rows, hidden), BF), many, shape((micro, rows, 3 * width), BF), many,
                   shape(small.shape, F32)],
        in_specs=[ANYWHERE] * 7 + [IN_VMEM] + [ANYWHERE] * 4 + [IN_VMEM],
        out_specs=[ANYWHERE] * 7 + [IN_VMEM],
        scratch_shapes=[pltpu.VMEM(w.shape, BF) for w in weights]
        + [pltpu.VMEM((micro, rows, width), BF)] * 2
        + [pltpu.VMEM((2, rows, width), BF), pltpu.VMEM((2, rows, 3 * width), BF), pltpu.VMEM((2, 16, rows), F32),
           pltpu.VMEM((2, rows, width), F32), pltpu.VMEM((2, rows, hidden), BF),
           pltpu.VMEM((2, rows, hidden), BF), pltpu.VMEM((2, rows, width), BF), pltpu.VMEM((2, rows, 3 * width), BF),
           pltpu.VMEM((rows, rows), F32), pltpu.VMEM((rows, width), BF), pltpu.VMEM((rows, width), F32),
           pltpu.VMEM((width, rows), BF), pltpu.VMEM((16, width), F32), pltpu.VMEM((16, width), F32)]
        + [DMA((4,)), DMA((micro,)), DMA((micro,)), DMA((2, 5)), DMA((2, 3)), DMA((micro,)), DMA((micro,)),
           DMA((micro,)), DMA((2, micro)), DMA((2, micro)), pltpu.SemaphoreType.REGULAR],
        compiler_params=pltpu.CompilerParams(
            collective_id=1, has_side_effects=True, vmem_limit_bytes=VMEM_CAP),
        name="backward_line",
    )(acts, g_in, x, qkv, lse, h, gp, words, wqkv, wproj, wup, wdown, small)


GATHER_PIECES = ((0, 0, 48, "c"), (0, 48, 48, "x"), (4, 0, 16, "x"), (1, 0, 96, "c"), (2, 0, 48, "x"), (2, 48, 48, "c"),
                 (3, 0, 192, "x"), (3, 192, 192, "c"))


def gather_kernel(pieces, micro, *refs):
    count = 5
    masters, (x_in, g_in, seg_in, cls_in) = refs[:count], refs[count : count + 4]
    wholes, (x_o, x_all, g_o, seg_o) = refs[count + 4 : 2 * count + 4], refs[2 * count + 4 : 2 * count + 8]
    refs = refs[2 * count + 8 :]
    swap, wide, narrow, (x_raw, g_raw, x_pad, g_pad, words, table) = refs[:5], refs[5:9], refs[9:13], refs[13:19]
    send, recv, local, turn_send, turn_recv, load_sem = refs[19:]
    shares = narrow + (table,)
    loads = [pltpu.make_async_copy(masters[i], wide[i], load_sem.at[i]) for i in range(4)]
    loads += [pltpu.make_async_copy(x_in, x_raw, load_sem.at[4]), pltpu.make_async_copy(g_in, g_raw, load_sem.at[5])]
    for i in (0, 1, 2, 3, 4, 5):
        loads[i].start()
    me = Spot.here()
    xn, yn, cn = me.flip(x=1), me.flip(y=1), me.flip(c=1)
    target, source, ahead, back = me.drop(), me.source(), me.ahead(), me.back()
    stays, alone = same(me, target), same(me, back)
    moves, pairs = jnp.logical_not(stays), jnp.logical_not(alone)
    crosses = me.crosses()
    direct = jnp.logical_and(moves, jnp.logical_not(crosses))
    for spot in (xn, yn, cn):
        hail(spot)

    @pl.when(moves)
    def _():
        hail(target)
        hail(source)

    @pl.when(pairs)
    def _():
        hail(ahead)
        hail(back)

    fed = hail_feeding(me, 0, 0) + hail_feeding(me, 3, 1)
    expected = 3 + jnp.where(stays, 0, 2) + jnp.where(alone, 0, 2) + fed

    def rows(k, part):
        array, first, size, _ = pieces[k]
        share = shares[array].shape[0]
        return wholes[array].at[pl.ds(pl.multiple_of(part * share + first, 16), size)]

    def mine(k):
        array, first, size, _ = pieces[k]
        return shares[array].at[pl.ds(first, size)]

    def swapped(k):
        array, first, size, _ = pieces[k]
        return swap[array].at[pl.ds(first, size)]

    def remote(src, dst, kind, k, spot):
        return pltpu.make_async_remote_copy(
            src_ref=src, dst_ref=dst, send_sem=send.at[kind, k], recv_sem=recv.at[kind, k],
            device_id=spot.id(), device_id_type=MESH)

    def crossed(k):
        return remote(mine(k), swapped(k), 8, k, yn)

    def brought(k, part):
        return remote(mine(k), rows(k, part), 0, k, target)

    def brought_on(k, part):
        return remote(swapped(k), rows(k, part), 0, k, target)

    def kept(k):
        return pltpu.make_async_copy(mine(k), rows(k, me.dp()), local.at[k])

    def passed(kind, k, part, spot):
        return remote(rows(k, part), rows(k, part), kind, k, spot)

    def parts(spot):
        return [s.part() for s in (spot, spot.flip(x=1), spot.flip(y=1), spot.flip(x=1, y=1))]

    own, own_x, own_y, own_d = parts(me)
    beside = parts(cn)
    turns = [(words, seg_o)] + [(x_pad.at[m], x_o.at[m]) for m in range(FIRST)] + [(g_pad.at[m], g_o.at[m]) for m in range(micro)]
    gives = [me.z >= 0] + [me.feeds(0, 0)] * FIRST + [me.feeds(3, 1)] * micro
    takes = [me.z >= 0] + [me.z == 0] * FIRST + [me.z == 3] * micro
    takers = [ahead] + [me.fed_at(0)] * FIRST + [me.fed_at(3)] * micro
    givers = [back] + [me.feeder(0)] * FIRST + [me.feeder(1)] * micro

    def turn(i):
        return pltpu.make_async_remote_copy(
            src_ref=turns[i][0], dst_ref=turns[i][1], send_sem=turn_send.at[i], recv_sem=turn_recv.at[i],
            device_id=takers[i].id(), device_id_type=MESH)

    def turn_start(i):
        here = same(me, takers[i])
        pl.when(gives[i] & here)(lambda: pltpu.make_async_copy(*turns[i], turn_send.at[i]).start())
        pl.when(gives[i] & jnp.logical_not(here))(lambda: turn(i).start())

    def turn_end(i):
        here = same(me, takers[i])
        pl.when(gives[i] & here)(lambda: pltpu.make_async_copy(*turns[i], turn_send.at[i]).wait())
        pl.when(gives[i] & jnp.logical_not(here))(lambda: turn(i).wait_send())
        pl.when(takes[i] & jnp.logical_not(same(me, givers[i])))(lambda: turn(i).wait_recv())

    flat = masters[4][...].astype(BF).astype(F32)
    share = flat.shape[1] // 12
    table[...] = jnp.zeros_like(table)
    for i in range(8):
        table[i : i + 1, 0:share] = flat[:, i * share : (i + 1) * share]
    for i in range(share // 32):
        table[8 + i : 9 + i, :] = flat[:, 8 * share + 128 * i : 8 * share + 128 * (i + 1)]
    words[...] = jnp.full_like(words, -1)
    words[0:micro, 0 : seg_in.shape[1]] = seg_in[...]
    for m in range(micro):
        words[micro + m : micro + m + 1, :] = jnp.full((1, words.shape[1]), cls_in[m], jnp.int32)

    def pad(raw, padded):
        for m in range(micro):
            short = raw[m]
            rest = jnp.zeros((padded.shape[1] - short.shape[0], short.shape[1]), short.dtype)
            padded[m] = jnp.concatenate([short, rest], axis=0)

    ready = set()
    for k in range(len(pieces)):
        array = pieces[k][0]
        if array < 4 and array not in ready:
            ready.add(array)
            loads[array].wait()
            size = wide[array].shape[0]
            for first in range(0, size, 48):
                narrow[array][first : first + 48, :] = wide[array][first : first + 48, :].astype(BF)
        if k == 0:
            pl.semaphore_wait(pltpu.get_barrier_semaphore(), expected)
        pl.when(stays)(lambda: kept(k).start())
        pl.when(direct)(lambda: brought(k, me.dp()).start())
        pl.when(crosses)(lambda: crossed(k).start())
    turn_start(0)
    loads[4].wait()
    pad(x_raw, x_pad)
    for i in range(FIRST):
        turn_start(1 + i)
    x_save = pltpu.make_async_copy(x_pad, x_all, load_sem.at[4])
    x_save.start()
    loads[5].wait()
    pad(g_raw, g_pad)
    for k in range(len(pieces) + 3):
        if k < len(pieces):
            @pl.when(crosses)
            def _():
                crossed(k).wait_recv()
                brought_on(k, me.dp()).start()

        if k == len(pieces) - 1:
            for i in range(1 + FIRST, 1 + FIRST + micro):
                turn_start(i)
        b = k - 1
        if 0 <= b < len(pieces):
            pl.when(stays)(lambda: kept(b).wait())
            pl.when(moves)(lambda: brought(b, own).wait_recv())
            passed(1, b, own, xn).start()
            passed(2, b, own, yn).start()
            passed(4, b, own, cn).start()
        b = k - 2
        if 0 <= b < len(pieces):
            turn_x = (me.c == 0) if pieces[b][3] == "c" else (me.c < 0)
            passed(1, b, own_x, xn).wait_recv()
            pl.when(turn_x)(lambda: passed(3, b, own_x, yn).start())
            passed(5, b, own_x, cn).start()
            passed(2, b, own_y, yn).wait_recv()
            pl.when(jnp.logical_not(turn_x))(lambda: passed(3, b, own_y, xn).start())
            passed(6, b, own_y, cn).start()
        b = k - 3
        if 0 <= b < len(pieces):
            passed(3, b, own_d, yn).wait_recv()
            passed(7, b, own_d, cn).start()
    for k in range(len(pieces)):
        for kind in range(4, 8):
            passed(kind, k, beside[kind - 4], cn).wait_recv()
        pl.when(moves)(lambda: brought(k, own).wait_send())
        pl.when(crosses)(lambda: crossed(k).wait_send())
        for kind in range(1, 8):
            passed(kind, k, own, cn).wait_send()
    for i in range(len(turns)):
        turn_end(i)
    x_save.wait()


def run_gather(masters, inputs, g, segs, classes, rows):
    pieces = GATHER_PIECES
    micro, _, width = g.shape
    shape = jax.ShapeDtypeStruct
    shares = [shape(m.shape, BF) for m in masters[:4]] + [shape((16, 128), F32)]
    many = shape((micro, rows, width), BF)
    outs = [shape((s.shape[0] * 8,) + s.shape[1:], s.dtype) for s in shares]
    outs += [shape((FIRST, rows, width), BF), many, many, shape((2 * micro, rows), segs.dtype)]
    return pl.pallas_call(
        functools.partial(gather_kernel, pieces, micro),
        out_shape=outs,
        in_specs=[ANYWHERE] * 4 + [IN_VMEM] + [ANYWHERE] * 2 + [IN_VMEM, IN_SMEM],
        out_specs=[ANYWHERE] * 9,
        scratch_shapes=[pltpu.VMEM(s.shape, s.dtype) for s in shares] + [pltpu.VMEM(m.shape, F32) for m in masters[:4]]
        + [pltpu.VMEM(s.shape, BF) for s in shares[:4]] + [pltpu.VMEM(g.shape, BF)] * 2
        + [pltpu.VMEM((micro, rows, width), BF)] * 2
        + [pltpu.VMEM((2 * micro, rows), segs.dtype), pltpu.VMEM((16, 128), F32)]
        + [DMA((9, len(pieces))), DMA((9, len(pieces))), DMA((len(pieces),)), DMA((1 + FIRST + micro,)),
           DMA((1 + FIRST + micro,)), DMA((6,))],
        compiler_params=pltpu.CompilerParams(collective_id=2, has_side_effects=True, vmem_limit_bytes=VMEM_CAP),
        name="gather_layers",
    )(*masters, inputs, g, segs, classes)


SCATTER_PIECES = ((3, 0, 128, 0, 768, "x"), (3, 128, 128, 0, 768, "x"), (3, 256, 128, 0, 768, "x"),
                  (2, 0, 96, 0, 1024, "x"), (2, 0, 96, 1024, 1024, "x"), (2, 0, 96, 2048, 1024, "x"),
                  (0, 0, 96, 0, 768, "x"), (0, 0, 96, 768, 768, "x"), (0, 0, 96, 1536, 768, "x"),
                  (1, 0, 96, 0, 768, "x"), (4, 0, 16, 0, 128, "x"))


SCATTER_LAGS = (1, 3, 4, 5)


def scatter_kernel(pieces, micro, *refs):
    count = 5
    a_h, r_h, o_h, f_h, a2_h, dz_h, u_h, g_h, small_h, gin_in = refs[:10]
    outs, gin_o, norm_o = refs[10:15], refs[15], refs[16]
    at = 17
    totals, beside, diag, from_x, from_y, done, swap, home = (refs[at + i * count : at + (i + 1) * count] for i in range(8))
    (stream, fixed, flipped, sums, tallies, stream_sem, fixed_sem, send, recv, local, turn_sem, note_send, note_recv,
     out_sem) = refs[at + 8 * count :]
    me = Spot.here()
    xn, yn, cn = me.flip(x=1), me.flip(y=1), me.flip(c=1)
    target, giver, back, ahead = me.source(), me.drop(), me.back(), me.ahead()
    stays, alone = same(me, target), same(me, back)
    moves, pairs = jnp.logical_not(stays), jnp.logical_not(alone)
    crosses, target_crosses = me.crosses(), target.crosses()
    slab = [me.flip(x=i & 1, y=(i >> 1) & 1, c=i >> 2) for i in range(1, 8)]
    column = [Spot(me.x, me.y, (me.z + i) % 4, me.c) for i in range(1, 4)]
    left_right = {0: (a_h, r_h), 1: (o_h, f_h), 2: (a2_h, dz_h), 3: (u_h, g_h)}
    resting = (g_h, a2_h, a_h, o_h)
    rest_at = {3: 0, 2: 1, 0: 2, 1: 3}

    openers = {}
    for k in reversed(range(len(pieces))):
        openers[pieces[k][0]] = k
    opened = sorted((k, array) for array, k in openers.items() if array < 4)

    def streamed(k):
        array, first, size, column_at, columns, _ = pieces[k]
        slot = k % 2
        if array == 3:
            share = totals[3].shape[0] // 8
            return [pltpu.make_async_copy(u_h.at[:, pl.ds(p * share + first, size)],
                                          stream.at[slot, :, pl.ds(p * size, size)], stream_sem.at[slot, p])
                    for p in range(8)]
        if array == 4:
            return [pltpu.make_async_copy(small_h, totals[4], stream_sem.at[slot, 0])]
        return [pltpu.make_async_copy(left_right[array][1].at[:, pl.ds(column_at, columns)],
                                      stream.at[slot, :, pl.ds(0, columns)], stream_sem.at[slot, 0])]

    def rested(i):
        return pltpu.make_async_copy(resting[i], fixed.at[i], fixed_sem.at[i])

    for copy in streamed(0):
        copy.start()
    rested(rest_at[opened[0][1]]).start()
    for copy in streamed(1):
        copy.start()
    for _, array in opened[1:]:
        rested(rest_at[array]).start()
    for spot in slab + column:
        hail(spot)

    @pl.when(moves)
    def _():
        hail(target)
        hail(giver)

    @pl.when(pairs)
    def _():
        hail(back)
        hail(ahead)

    def work(k):
        array, first, size, column_at, columns, _ = pieces[k]
        slot = k % 2
        for copy in streamed(k):
            copy.wait()
        if array == 4:
            pass
        elif array == 3:
            if k == openers[3]:
                rested(rest_at[3]).wait()
            share = totals[3].shape[0] // 8
            for p in range(0, 8, 2):
                both = lax.dot_general(stream[slot, :, p * size : (p + 2) * size], fixed[rest_at[3]], TN,
                                       preferred_element_type=F32).astype(BF)
                for i in range(2):
                    totals[3][(p + i) * share + first : (p + i) * share + first + size, :] = both[i * size : (i + 1) * size]
        else:
            if k == openers[array]:
                rested(rest_at[array]).wait()
                flipped[...] = fixed[rest_at[array]].T
            for c in range(0, columns, 256):
                totals[array][:, column_at + c : column_at + c + 256] = mm(flipped[...], stream[slot, :, c : c + 256]).astype(BF)
        if k + 2 < len(pieces):
            for copy in streamed(k + 2):
                copy.start()

    def parts(spot):
        return [s.part() for s in (spot, spot.flip(x=1), spot.flip(y=1), spot.flip(x=1, y=1))]

    kept, given = parts(me), parts(cn)

    def box(k):
        _, first, size, column_at, columns, _ = pieces[k]
        return pl.ds(first, size), pl.ds(column_at, columns)

    def whole(k, part):
        array, first, size, column_at, columns, _ = pieces[k]
        share = done[array].shape[0]
        return totals[array].at[pl.ds(pl.multiple_of(part * share + first, 16), size), pl.ds(column_at, columns)]

    def remote(src, dst, kind, k, spot):
        return pltpu.make_async_remote_copy(
            src_ref=src, dst_ref=dst, send_sem=send.at[kind, k], recv_sem=recv.at[kind, k],
            device_id=spot.id(), device_id_type=MESH)

    def of(refs_, k):
        return refs_[pieces[k][0]].at[box(k)]

    def crossed(k, j):
        return remote(whole(k, given[j]), beside[pieces[k][0]].at[(j,) + box(k)], j, k, cn)

    def to_diag(k, spot):
        return remote(whole(k, kept[3]), of(diag, k), 4, k, spot)

    def to_x(k):
        return remote(whole(k, kept[1]), of(from_x, k), 5, k, xn)

    def to_y(k):
        return remote(whole(k, kept[2]), of(from_y, k), 6, k, yn)

    def to_home(k):
        return remote(of(done, k), of(home, k), 7, k, target)

    def to_swap(k):
        return remote(of(done, k), of(swap, k), 7, k, target)

    def stay_home(k):
        return pltpu.make_async_copy(of(done, k), of(home, k), local.at[k])

    def over(k):
        return remote(of(swap, k), of(home, k), 8, k, yn)

    def add(k, j, extra):
        here = whole(k, kept[j])
        here[...] = (here[...].astype(F32) + extra.astype(F32)).astype(here.dtype)

    def turn(m):
        return pltpu.make_async_remote_copy(
            src_ref=gin_in.at[m], dst_ref=gin_o.at[m], send_sem=turn_sem.at[0, m], recv_sem=turn_sem.at[1, m],
            device_id=back.id(), device_id_type=MESH)

    def turn_stay(m):
        return pltpu.make_async_copy(gin_in.at[m], gin_o.at[m], turn_sem.at[0, m])

    work(0)
    pl.semaphore_wait(pltpu.get_barrier_semaphore(), 10 + jnp.where(stays, 0, 2) + jnp.where(alone, 0, 2))
    for m in range(micro):
        now = me.gives_down() | (m == micro - 1)
        pl.when(alone & now)(lambda: turn_stay(m).start())
        pl.when(pairs & now)(lambda: turn(m).start())
    tally = jnp.zeros((8, 128), F32)
    for k in range(len(pieces) + SCATTER_LAGS[3]):
        if k < len(pieces):
            if k > 0:
                work(k)
            for j in (3, 2, 1, 0):
                crossed(k, j).start()
        b = k - SCATTER_LAGS[0]
        if 0 <= b < len(pieces):
            turn_x = (me.c == 0) if pieces[b][5] == "c" else (me.c < 0)
            for j in (3, 2, 1, 0):
                crossed(b, j).wait_recv()
                add(b, j, beside[pieces[b][0]][(j,) + box(b)])
                if j == 3:
                    pl.when(turn_x)(lambda: to_diag(b, yn).start())
                    pl.when(jnp.logical_not(turn_x))(lambda: to_diag(b, xn).start())
                if j == 2:
                    pl.when(turn_x)(lambda: to_y(b).start())
                if j == 1:
                    pl.when(jnp.logical_not(turn_x))(lambda: to_x(b).start())
        b = k - SCATTER_LAGS[1]
        if 0 <= b < len(pieces):
            to_diag(b, yn).wait_recv()
            turn_x = (me.c == 0) if pieces[b][5] == "c" else (me.c < 0)

            @pl.when(turn_x)
            def _():
                add(b, 1, of(diag, b)[...])
                to_x(b).start()

            @pl.when(jnp.logical_not(turn_x))
            def _():
                add(b, 2, of(diag, b)[...])
                to_y(b).start()
        b = k - SCATTER_LAGS[2]
        if 0 <= b < len(pieces):
            to_x(b).wait_recv()
            to_y(b).wait_recv()
            total = (whole(b, kept[0])[...].astype(F32) + of(from_x, b)[...].astype(F32) + of(from_y, b)[...].astype(F32))
            total = total.astype(done[pieces[b][0]].dtype)
            done[pieces[b][0]][box(b)] = total
            square = total.astype(F32) * total.astype(F32)
            for c in range(0, square.shape[1], 128):
                tally = tally + jnp.sum(square[:, c : c + 128].reshape(-1, 8, 128), axis=0)
            pl.when(stays)(lambda: stay_home(b).start())
            pl.when(moves & jnp.logical_not(target_crosses))(lambda: to_home(b).start())
            pl.when(target_crosses)(lambda: to_swap(b).start())
        b = k - SCATTER_LAGS[3]
        if 0 <= b < len(pieces):
            @pl.when(crosses)
            def _():
                to_swap(b).wait_recv()
                over(b).start()
    sums[0] = tally

    def note(i, src, slot, spot):
        return pltpu.make_async_remote_copy(
            src_ref=src, dst_ref=tallies.at[slot], send_sem=note_send.at[i], recv_sem=note_recv.at[slot],
            device_id=spot.id(), device_id_type=MESH)

    for i, spot in enumerate(column):
        note(i, sums.at[0], i, spot).start()
    for i, spot in enumerate(column):
        note(i, sums.at[0], i, spot).wait_recv()
        tally = tally + tallies[i]
    sums[1] = tally
    for i, spot in enumerate(slab):
        note(3 + i, sums.at[1], 3 + i, spot).start()
    for i, spot in enumerate(slab):
        note(3 + i, sums.at[1], 3 + i, spot).wait_recv()
        tally = tally + tallies[3 + i]
    whole_norm = jnp.sqrt(jnp.sum(jnp.sum(tally, axis=0, keepdims=True), axis=1, keepdims=True))
    norm_o[...] = jnp.broadcast_to(whole_norm, norm_o.shape)
    last = {}
    for k in range(len(pieces)):
        last[pieces[k][0]] = k
    for k in range(len(pieces)):
        pl.when(stays)(lambda: stay_home(k).wait())
        pl.when(moves & jnp.logical_not(crosses))(lambda: to_home(k).wait_recv())
        pl.when(crosses)(lambda: over(k).wait_recv())
        array = pieces[k][0]
        if last[array] == k:
            pltpu.make_async_copy(home[array], outs[array], out_sem.at[array]).start()
    for i, spot in enumerate(column):
        note(i, sums.at[0], i, spot).wait_send()
    for i, spot in enumerate(slab):
        note(3 + i, sums.at[1], 3 + i, spot).wait_send()
    for k in range(len(pieces)):
        for j in range(4):
            crossed(k, j).wait_send()
        to_diag(k, yn).wait_send()
        to_x(k).wait_send()
        to_y(k).wait_send()
        pl.when(moves)(lambda: to_home(k).wait_send())
        pl.when(crosses)(lambda: over(k).wait_send())
    for m in range(micro):
        now, then = me.gives_down() | (m == micro - 1), me.takes_down() | (m == micro - 1)
        pl.when(alone & now)(lambda: turn_stay(m).wait())
        pl.when(pairs & now)(lambda: turn(m).wait_send())
        pl.when(pairs & then)(lambda: turn(m).wait_recv())
    for array in range(count):
        pltpu.make_async_copy(home[array], outs[array], out_sem.at[array]).wait()


def run_scatter(operands, small, gin):
    pieces = SCATTER_PIECES
    micro = gin.shape[0]
    shape = jax.ShapeDtypeStruct
    a, r, o, f, a2, dz, u, g = operands = [v.reshape(-1, v.shape[-1]) for v in operands]
    rows = a.shape[0]
    sizes = [((left.shape[1], right.shape[1]), BF) for left, right in ((a, r), (o, f), (a2, dz), (u, g))]
    sizes.append((small.shape, F32))
    shares = [((s[0] // 8, s[1]), t) for s, t in sizes]
    one = [pltpu.VMEM(s, t) for s, t in shares]
    return pl.pallas_call(
        functools.partial(scatter_kernel, pieces, micro),
        out_shape=[shape(s, t) for s, t in shares] + [shape(gin.shape, gin.dtype), shape((8, 128), F32)],
        in_specs=[ANYWHERE] * 10,
        out_specs=[ANYWHERE] * 6 + [IN_VMEM],
        scratch_shapes=[pltpu.VMEM(s, t) for s, t in sizes] + [pltpu.VMEM((4,) + s, t) for s, t in shares] + one * 6
        + [pltpu.VMEM((2, rows, 1024), BF), pltpu.VMEM((4, rows, a.shape[1]), BF), pltpu.VMEM((a.shape[1], rows), BF),
           pltpu.VMEM((2, 8, 128), F32), pltpu.VMEM((10, 8, 128), F32), DMA((2, 8)), DMA((4,)),
           DMA((9, len(pieces))), DMA((9, len(pieces))), DMA((len(pieces),)), DMA((2, micro)), DMA((10,)), DMA((10,)),
           DMA((5,))],
        compiler_params=pltpu.CompilerParams(collective_id=3, has_side_effects=True, vmem_limit_bytes=VMEM_CAP),
        name="scatter_layers",
    )(*operands, small, gin)


def finish_kernel(order, micro, norm, *refs):
    table, small_state, refs = refs[0], refs[1:4], refs[4:]
    shards_h, state_h, (acts_early, acts_late, gin_early, gin_late) = refs[:4], refs[4:16], refs[16:20]
    norm_o, small_o, refs = refs[20], refs[21:25], refs[5:]
    state_o, acts_o, gin_o = refs[20:36], refs[36], refs[37]
    shards, state, (acts, gin, acts_cut, gin_cut, row) = refs[38:42], refs[42:58], refs[58:63]
    load_sem, pick_sem, out_sem = refs[63:]
    upper = Spot.here().takes_down()

    def loads(array):
        copies = [pltpu.make_async_copy(shards_h[array], shards[array], load_sem.at[array, 0])]
        for i in range(3):
            copies.append(pltpu.make_async_copy(state_h[4 * i + array], state[4 * (i + 1) + array], load_sem.at[array, 1 + i]))
        return copies

    def pick(i, m, src, dst):
        return pltpu.make_async_copy(src.at[m], dst.at[m], pick_sem.at[i, m])

    def saves(array):
        return [pltpu.make_async_copy(state[4 * i + array], state_o[4 * array + i], out_sem.at[array, i]) for i in range(4)]

    for array in order:
        for copy in loads(array):
            copy.start()
    for i, (early, late, dst, is_early) in enumerate(
            ((acts_early, acts_late, acts, upper), (gin_early, gin_late, gin, jnp.logical_not(upper)))):
        for m in range(micro):
            if m >= (EARLY if i == 0 else micro - 1):
                pick(i, m, late, dst).start()
            else:
                pl.when(is_early)(lambda: pick(i, m, early, dst).start())
                pl.when(jnp.logical_not(is_early))(lambda: pick(i, m, late, dst).start())
    factor = 1.0 / jnp.maximum(norm[0:1, 0:1], 1.0)
    fix = 1.0 / (1.0 - 0.5**STEP)
    strip = 16
    norm_o[0] = norm[0, 0]
    share = row.shape[1] // 12
    for i in range(8):
        row[:, i * share : (i + 1) * share] = table[i : i + 1, 0:share]
    for i in range(share // 32):
        row[:, 8 * share + 128 * i : 8 * share + 128 * (i + 1)] = table[8 + i : 9 + i, :]
    grad = row[...] * factor
    first_new = 0.5 * small_state[1][...] + 0.5 * grad
    second_new = 0.5 * small_state[2][...] + 0.5 * grad * grad
    small_o[0][...] = grad
    small_o[1][...] = small_state[0][...] - small_rate * ((first_new * fix) / (jnp.sqrt(second_new * fix) + adam_eps))
    small_o[2][...] = first_new
    small_o[3][...] = second_new
    for array in order:
        for copy in loads(array):
            copy.wait()
        grads, master, first, second = state[array], state[4 + array], state[8 + array], state[12 + array]

        def update(i, carry):
            rows = pl.ds(pl.multiple_of(i * strip, strip), strip)
            grad = shards[array][rows, :].astype(F32) * factor
            first_new = 0.5 * first[rows, :] + 0.5 * grad
            second_new = 0.5 * second[rows, :] + 0.5 * grad * grad
            old = master[rows, :]
            change = (first_new * fix) / (jnp.sqrt(second_new * fix) + adam_eps) + decay_rate * old
            grads[rows, :] = grad
            first[rows, :] = first_new
            second[rows, :] = second_new
            master[rows, :] = old - learn_rate * change
            return carry

        lax.fori_loop(0, grads.shape[0] // strip, update, 0)
        for copy in saves(array):
            copy.start()
    length = acts_cut.shape[1]
    for i, (src, cut, out) in enumerate(((acts, acts_cut, acts_o), (gin, gin_cut, gin_o))):
        for m in range(micro):
            pick(i, m, gin_late, src).wait()
            cut[m] = src[m, 0:length, :]
        pltpu.make_async_copy(cut, out, out_sem.at[4, i]).start()
    for array in order:
        for copy in saves(array):
            copy.wait()
    for i, (cut, out) in enumerate(((acts_cut, acts_o), (gin_cut, gin_o))):
        pltpu.make_async_copy(cut, out, out_sem.at[4, i]).wait()


def run_finish(norm, table, small_states, shards, states, tall, length):
    micro, rows, width = tall[0].shape
    shape = jax.ShapeDtypeStruct
    return pl.pallas_call(
        functools.partial(finish_kernel, (1, 0, 2, 3), micro),
        out_shape=[shape((1,), F32)] + [shape(small_states[0].shape, F32)] * 4
        + [shape(s.shape, F32) for s in shards for _ in range(4)] + [shape((micro, length, width), BF)] * 2,
        in_specs=[IN_VMEM] * 5 + [ANYWHERE] * 20,
        out_specs=[IN_SMEM] + [IN_VMEM] * 4 + [ANYWHERE] * 18,
        scratch_shapes=[pltpu.VMEM(s.shape, BF) for s in shards]
        + [pltpu.VMEM(s.shape, F32) for _ in range(4) for s in shards]
        + [pltpu.VMEM((micro, rows, width), BF)] * 2 + [pltpu.VMEM((micro, length, width), BF)] * 2
        + [pltpu.VMEM(small_states[0].shape, F32)] + [DMA((4, 4)), DMA((2, micro)), DMA((5, 4))],
        compiler_params=pltpu.CompilerParams(vmem_limit_bytes=VMEM_CAP),
        name="finish",
    )(norm, table, *small_states, *shards, *states, *tall)


def split_small(small, width, slices):
    share = width // slices
    stacked = small.reshape(slices, small.shape[0] // slices)
    eight = stacked[:, : 8 * share].reshape(slices, 8, share).transpose(1, 0, 2).reshape(8, width)
    up = stacked[:, 8 * share :].reshape(-1, width)
    return jnp.concatenate([eight, up, jnp.zeros((16 - 8 - up.shape[0], width), small.dtype)], axis=0)


def join_small(table, total, slices):
    width = table.shape[1]
    share = width // slices
    ups = total // width - 8
    eight = table[:8].reshape(8, slices, share).transpose(1, 0, 2).reshape(slices, 8 * share)
    up = table[8 : 8 + ups].reshape(slices, -1)
    return jnp.concatenate([eight, up], axis=1).reshape(-1)


def weight_grad(left, right):
    rows = left.shape[0] * left.shape[1]
    return lax.dot_general(left.reshape(rows, -1), right.reshape(rows, -1), (((0,), (0,)), ((), ())),
                           preferred_element_type=F32)


def adam(grad, master, first, second, rate, decay):
    fix = 1.0 - 0.5**STEP
    first = 0.5 * first + 0.5 * grad
    second = 0.5 * second + 0.5 * grad * grad
    update = first / fix / (jnp.sqrt(second / fix) + adam_eps)
    if decay:
        update = update + decay * master
    return [grad, master - rate * update, first, second]


def per_device(inputs, out_grad, segment_ids, cls_index, *states):
    masters, firsts, seconds = states[0:5], states[5:10], states[10:15]
    slices = lax.axis_size("dp")
    stages = lax.axis_size("section")
    turned = slices == 8 and stages == 4
    seq_dev, length, width = inputs.shape
    rows = -(-length // 128) * 128
    share = masters[4].shape[1]
    total = share * slices

    if turned:
        line = Line("dp", 4, 2)
        *weights, small, x_first, x_in, g_in, words = run_gather(
            [m[0] for m in masters[:4]] + [masters[4]], inputs, out_grad, segment_ids, cls_index, rows)
    else:
        line = Line("section", stages, 1)
        extra = ((0, 0), (0, rows - length), (0, 0))
        x_in, g_in = jnp.pad(inputs, extra), jnp.pad(out_grad, extra)
        segs = jnp.pad(segment_ids, ((0, 0), (0, rows - length)), constant_values=-1)
        words = jnp.concatenate([segs, jnp.broadcast_to(cls_index[:, None], (seq_dev, rows))], axis=0)
        gathered = [lax.all_gather(m[0].astype(BF), "dp", axis=0, tiled=True) for m in masters]
        weights, x_first = gathered[:4], x_in[0]
        small = split_small(gathered[4].astype(F32), width, slices)

    x, a, qkv, lse, o, h, a2, gp, u, acts, acts_early = run_forward(
        line, length, turned, x_first, x_in, words, weights, small)
    acts, gin_early, g, dz, f, r, gin, sums = run_backward(
        line, length, turned, acts, g_in, x, qkv, lse, h, gp, words, weights, small)
    results = []
    if turned:
        matrix_states = [v[0] for group in (masters, firsts, seconds) for v in group[:4]]
        *shards, table, gin, norm = run_scatter([a, r, o, f, a2, dz, u, g], sums, gin)
        grad_norm, *rest = run_finish(norm, table, [masters[4], firsts[4], seconds[4]], shards, matrix_states,
                                      [acts_early, acts, gin_early, gin], length)
        acts, gin = rest[20:]
        results = [v[None] for v in rest[4:20]] + rest[:4]
    else:
        acts, gin = acts[:, :length], gin[:, :length]
        totals = [weight_grad(a, r).astype(BF), weight_grad(o, f).astype(BF), weight_grad(a2, dz).astype(BF),
                  weight_grad(u, g).astype(BF), join_small(sums, total, slices)]
        shards = [lax.psum_scatter(t[None], "dp", scatter_dimension=1, tiled=True).astype(F32) for t in totals]
        squares = jnp.sum(jnp.stack([jnp.sum(s * s) for s in shards]))
        grad_norm = jnp.sqrt(lax.psum(squares, ("dp", "section")))
        factor = 1.0 / jnp.maximum(grad_norm, 1.0)
        for kind in range(5):
            rate, decay = (learn_rate, decay_rate) if kind < 4 else (small_rate, 0.0)
            results += adam(shards[kind] * factor, masters[kind], firsts[kind], seconds[kind], rate, decay)
    return (acts[None], gin[None], grad_norm.reshape(1)) + tuple(results)


def solution(mesh):
    matrix, vector = P("section", "dp", None), P("section", "dp")
    states = (matrix,) * 4 + (vector,)
    return jax.shard_map(
        per_device,
        mesh=mesh,
        in_specs=(P("dp", None, None), P("dp", None, None), P("dp", None), P("dp")) + states * 3,
        out_specs=(P("section", "dp", None, None), P("section", "dp", None, None), P())
        + (matrix,) * 16 + (vector,) * 4,
        check_vma=False,
    )
```

```python
import functools

import jax
import jax.numpy as jnp
from jax import lax
from jax.experimental import pallas as pl
from jax.experimental.pallas import tpu as pltpu
from jax.sharding import PartitionSpec as P

HEADS = 12
STEP = 3
F32 = jnp.float32
BF = jnp.bfloat16
MESH = pl.DeviceIdType.MESH
VMEM_CAP = 60 * 1024 * 1024
EARLY = 3
FIRST = 2

norm_eps = 1e-06
masked_score = -1e30
learn_rate = 0.05
small_rate = 0.3
decay_rate = 0.05
adam_eps = 1e-08

NT = (((1,), (1,)), ((), ()))
TN = (((0,), (0,)), ((), ()))


def mm(a, b):
    return jnp.dot(a, b, preferred_element_type=F32)


def mm_nt(a, b):
    return lax.dot_general(a, b, NT, preferred_element_type=F32)


def norm_parts(values):
    center = values - jnp.mean(values, axis=-1, keepdims=True)
    spread = jnp.mean(center * center, axis=-1, keepdims=True)
    inv = lax.rsqrt(spread + norm_eps)
    return center * inv, inv


def norm_back(y, normed, inv):
    pull = jnp.mean(y * normed, axis=-1, keepdims=True)
    return (y - jnp.mean(y, axis=-1, keepdims=True) - normed * pull) * inv


def column_sum(values):
    return jnp.sum(values, axis=0, keepdims=True)


def mask_bias(seg_row, seg_col, cls_row, length):
    size = seg_col.shape[0]
    key_at = lax.broadcasted_iota(jnp.int32, (size, size), 0)
    query_at = lax.broadcasted_iota(jnp.int32, (size, size), 1)
    allowed = (seg_row == seg_col) | (key_at == cls_row) | (query_at == cls_row)
    allowed = allowed & (key_at < length)
    return jnp.where(allowed, 0.0, masked_score).astype(F32)


def micro_bias(words, m, micro, length):
    seg_row, cls_row = words[pl.ds(m, 1), :], words[pl.ds(micro + m, 1), :]
    size = seg_row.shape[1]
    on_diagonal = lax.broadcasted_iota(jnp.int32, (size, size), 0) == lax.broadcasted_iota(jnp.int32, (size, size), 1)
    seg_col = jnp.sum(jnp.where(on_diagonal, seg_row.astype(F32), 0.0), axis=1, keepdims=True)
    return mask_bias(seg_row.astype(F32), seg_col, cls_row, length)


def spread_small(table, small):
    width = small.shape[1]
    share, ups = width // 8, width // 256
    small[...] = jnp.zeros_like(small)
    for i in range(8):
        small[0:8, i * share : (i + 1) * share] = table[16 * i : 16 * i + 8, 0:share]
        for j in range(ups):
            at = i % 2 * (width // 2) + j * 128
            small[8 + i // 2 : 9 + i // 2, at : at + 128] = table[16 * i + 8 + j : 16 * i + 9 + j, :]


def share_small(sums, table):
    width = sums.shape[1]
    share, ups = width // 8, width // 256
    table[...] = jnp.zeros_like(table)
    for i in range(8):
        table[16 * i : 16 * i + 8, 0:share] = sums[0:8, i * share : (i + 1) * share]
        for j in range(ups):
            at = i % 2 * (width // 2) + j * 128
            table[16 * i + 8 + j : 16 * i + 9 + j, :] = sums[8 + i // 2 : 9 + i // 2, at : at + 128]


def gelu_parts(z):
    density = jnp.exp(z * z * -0.5) * 0.3989422804014327
    below = 0.5 + 0.5 * lax.erf(z * 0.7071067811865476)
    return z * below, below + z * density


def layer_forward(x_ref, bias_ref, wqkv, wproj, wup, wdown, small, a_ref, qkv_ref, lse_ref, o_ref,
                  h_ref, a2_ref, gp_ref, u_ref, out_ref, ot_ref, before):
    rows, width = x_ref.shape
    hidden = wup.shape[1]
    normed, _ = norm_parts(x_ref[...].astype(F32))
    a_ref[...] = (normed * small[0:1, :] + small[1:2, :]).astype(BF)
    for part in range(3):
        cols = slice(part * width, (part + 1) * width)
        mixed = mm(a_ref[...], wqkv[:, cols])
        if part == 0:
            mixed = mixed + small[2:3, :]
        if part == 2:
            mixed = mixed + small[3:4, :]
        qkv_ref[:, cols] = mixed.astype(BF)
    lane = lax.broadcasted_iota(jnp.int32, (rows, 128), 1)
    scores, raised, inverse = {}, {}, {}
    for step in range(HEADS + 2):
        if step < HEADS:
            at = step // 2 * 128
            half = (lane < 64) if step % 2 == 0 else (lane >= 64)
            k = qkv_ref[:, width + at : width + at + 128]
            k = jnp.where(half, k, jnp.zeros_like(k)) * jnp.asarray(0.125, BF)
            scores[step] = mm_nt(k, qkv_ref[:, at : at + 128])
        head = step - 1
        if 0 <= head < HEADS:
            shifted = scores.pop(head) + bias_ref[...]
            peak = jnp.max(shifted, axis=0, keepdims=True)
            grown = jnp.exp(shifted - peak)
            summed = jnp.sum(grown, axis=0, keepdims=True)
            raised[head] = grown.astype(BF)
            inverse[head] = 1.0 / summed
            lse_ref[head : head + 1, :] = peak + jnp.log(summed)
        head = step - 2
        if 0 <= head < HEADS:
            if head % 2 == 0:
                vt = qkv_ref[:, 2 * width + head * 64 : 2 * width + head * 64 + 128].T
            mixed = mm(vt[head % 2 * 64 : head % 2 * 64 + 64, :], raised.pop(head)) * inverse.pop(head)
            ot_ref[head * 64 : head * 64 + 64, :] = mixed.astype(BF)
    o_ref[...] = ot_ref[...].T
    before(1)
    h = x_ref[...].astype(F32) + (mm(o_ref[...], wproj[...]) + small[4:5, :])
    h_ref[...] = h
    normed, _ = norm_parts(h)
    a2_ref[...] = (normed * small[5:6, :] + small[6:7, :]).astype(BF)
    before(2)
    chunk = width
    z = {}
    for step in range(hidden // chunk + 1):
        cols = slice(step * chunk, (step + 1) * chunk)
        if step < hidden // chunk:
            row, start = 8 + step * chunk // width, step * chunk % width
            z[step] = mm(a2_ref[...], wup[:, cols]) + small[row : row + 1, start : start + chunk]
        part = step - 1
        if 0 <= part < hidden // chunk:
            cols = slice(part * chunk, (part + 1) * chunk)
            u, slope = gelu_parts(z.pop(part))
            u_ref[:, cols] = u.astype(BF)
            gp_ref[:, cols] = slope.astype(BF)
    before(3)
    total = mm(u_ref[...], wdown[...])
    out_ref[...] = (h_ref[...] + (total + small[7:8, :])).astype(BF)


def layer_backward(g_ref, x_ref, bias_ref, qkv_ref, lse_ref, h_ref, gp_ref, wqkv, wproj, wup, wdown,
                   small, dz_ref, f_ref, r_ref, gin_ref, sums_ref, do_ref, dh_ref, dqt_ref, before):
    rows, width = x_ref.shape
    hidden = wup.shape[1]
    carried = g_ref[...].astype(F32)
    sums_ref[7:8, :] += column_sum(carried)
    back = {}
    for step in range(hidden // width + 1):
        if step < hidden // width:
            back[step] = mm_nt(g_ref[...], wdown[step * width : (step + 1) * width, :])
        part = step - 1
        if part >= 0:
            cols = slice(part * width, (part + 1) * width)
            dz = (back.pop(part) * gp_ref[:, cols].astype(F32)).astype(BF)
            dz_ref[:, cols] = dz
            sums_ref[8 + part : 9 + part, :] += column_sum(dz.astype(F32))
    before(1)
    back = mm_nt(dz_ref[...], wup[...])
    normed, inv = norm_parts(h_ref[...])
    sums_ref[5:6, :] += column_sum(back * normed)
    sums_ref[6:7, :] += column_sum(back)
    dh = carried + norm_back(back * small[5:6, :], normed, inv)
    dh_ref[...] = dh
    f = dh.astype(BF)
    f_ref[...] = f
    sums_ref[4:5, :] += column_sum(f.astype(F32))
    before(2)
    do_ref[...] = mm_nt(f_ref[...], wproj[...]).astype(BF)
    lane = lax.broadcasted_iota(jnp.int32, (rows, 128), 1)
    scores, grads, probs, slopes, dks, dvs = {}, {}, {}, {}, {}, {}
    eighth = jnp.asarray(0.125, BF)
    for step in range(HEADS + 2):
        if step < HEADS:
            at = step // 2 * 128
            half = (lane < 64) if step % 2 == 0 else (lane >= 64)
            k = qkv_ref[:, width + at : width + at + 128]
            v = qkv_ref[:, 2 * width + at : 2 * width + at + 128]
            scores[step] = mm_nt(jnp.where(half, k, jnp.zeros_like(k)) * eighth, qkv_ref[:, at : at + 128])
            grads[step] = mm_nt(jnp.where(half, v, jnp.zeros_like(v)), do_ref[:, at : at + 128])
        head = step - 1
        if 0 <= head < HEADS:
            p = jnp.exp(scores.pop(head) + bias_ref[...] - lse_ref[head : head + 1, :])
            dp = grads.pop(head)
            inner = jnp.sum(p * dp, axis=0, keepdims=True)
            slopes[head] = (p * (dp - inner)).astype(BF)
            probs[head] = p.astype(BF)
        head = step - 2
        if 0 <= head < HEADS:
            at = head // 2 * 128
            side = head % 2
            ds = slopes.pop(head)
            dvs[side] = mm(probs.pop(head), do_ref[:, at : at + 128])
            dks[side] = mm(ds, qkv_ref[:, at : at + 128] * eighth)
            if side == 0:
                kt = (qkv_ref[:, width + at : width + at + 128] * eighth).T
            dqt_ref[head * 64 : head * 64 + 64, :] = mm(kt[side * 64 : side * 64 + 64, :], ds).astype(BF)
            if side == 1:
                r_ref[:, width + at : width + at + 128] = jnp.where(lane < 64, dks[0], dks[1]).astype(BF)
                r_ref[:, 2 * width + at : 2 * width + at + 128] = jnp.where(lane < 64, dvs[0], dvs[1]).astype(BF)
    r_ref[:, 0:width] = dqt_ref[...].T
    sums_ref[2:3, :] += column_sum(r_ref[:, 0:width].astype(F32))
    sums_ref[3:4, :] += column_sum(r_ref[:, 2 * width :].astype(F32))
    before(3)
    back = mm_nt(r_ref[...], wqkv[...])
    normed, inv = norm_parts(x_ref[...].astype(F32))
    sums_ref[0:1, :] += column_sum(back * normed)
    sums_ref[1:2, :] += column_sum(back)
    gin_ref[...] = (dh_ref[...] + norm_back(back * small[0:1, :], normed, inv)).astype(BF)


class Line:
    def __init__(self, axis, count, stride):
        self.axis, self.count, self.stride = axis, count, stride

    def stage(self):
        return lax.axis_index(self.axis) // self.stride

    def beside(self, by):
        return {self.axis: lax.axis_index(self.axis) + by * self.stride}


class Spot:
    def __init__(self, x, y, z, c):
        self.x, self.y, self.z, self.c = x, y, z, c

    @staticmethod
    def here():
        dp, section = lax.axis_index("dp"), lax.axis_index("section")
        return Spot(dp % 2, section // 2, dp // 2, section % 2)

    def dp(self):
        return self.z * 2 + self.x

    def section(self):
        return self.y * 2 + self.c

    def id(self):
        return (self.dp(), self.section())

    def flip(self, x=0, y=0, c=0):
        return Spot(1 - self.x if x else self.x, 1 - self.y if y else self.y, self.z, 1 - self.c if c else self.c)

    def ahead(self):
        return Spot(self.x, self.z % 2, self.section(), self.z // 2)

    def back(self):
        return Spot(self.x, self.z // 2, 2 * self.c + self.y, self.z % 2)

    def feeds(self, stage, core):
        return ((self.y == self.z % 2) & (self.c == core)) & (self.z >= 0)

    def fed_at(self, stage):
        return Spot(self.x, self.y, stage, self.z // 2)

    def feeder(self, core):
        return Spot(self.x, self.y, 2 * self.c + self.y, core)

    def gives_down(self):
        return self.back().z < self.z

    def takes_down(self):
        return self.z < self.section()

    def gives_near(self):
        return (self.z >= 2) & (self.back().z == self.z - 1)

    def takes_near(self):
        return (self.section() >= 2) & (self.z == self.section() - 1)

    def yields(self):
        return (self.y == 0) & (self.z >= 2) & (self.back().z == 0)

    def carries(self):
        return self.flip(y=1).yields()

    def carrier(self):
        return Spot(self.x, 1, self.section(), 0)

    def takes_carried(self):
        return (self.z == 0) & (self.section() >= 2)

    def crosses(self):
        return (self.z + self.c) % 2 == 1

    def drop(self):
        return Spot(self.x, self.y, 2 * ((self.y + self.z + self.c) % 2) + self.c, self.z // 2)

    def source(self):
        c = self.z % 2
        return Spot(self.x, self.y, 2 * self.c + (self.y + self.z // 2 + c) % 2, c)

    def part(self):
        return self.source().dp()


def same(one, other):
    return (one.dp() == other.dp()) & (one.section() == other.section())


def hail(spot):
    pl.semaphore_signal(pltpu.get_barrier_semaphore(), inc=1, device_id=spot.id(), device_id_type=MESH)


def hail_stagger(me, leading, by):
    waits = (me.z == leading) & (me.c == 1)
    tells = (me.z == leading + by) & (me.c == 0)
    pl.when(waits)(lambda: hail(Spot(me.x, me.y, me.z + by, 0)))
    pl.when(tells)(lambda: hail(Spot(me.x, me.y, me.z - by, 1)))
    return jnp.where(waits, 1, 0) + jnp.where(tells, 1, 0)


def tell_stagger(me, leading, by, token, m):
    @pl.when((me.z == leading + by) & (me.c == 0) & (m == 0))
    def _():
        pl.semaphore_signal(token, inc=1, device_id=Spot(me.x, me.y, me.z - by, 1).id(), device_id_type=MESH)


def wait_stagger(me, leading, token, m):
    @pl.when((me.z == leading) & (me.c == 1) & (m == 0))
    def _():
        pl.semaphore_wait(token, 1)


def hail_feeding(me, stage, core):
    gives = me.feeds(stage, core) & jnp.logical_not(same(me, me.fed_at(stage)))
    takes = (me.z == stage) & jnp.logical_not(same(me, me.feeder(core)))
    pl.when(gives)(lambda: hail(me.fed_at(stage)))
    pl.when(takes)(lambda: hail(me.feeder(core)))
    return jnp.where(gives, 1, 0) + jnp.where(takes, 1, 0)


def greet(line, turned, feeding=False):
    stage = line.stage()
    barrier = pltpu.get_barrier_semaphore()

    @pl.when(stage > 0)
    def _():
        pl.semaphore_signal(barrier, inc=1, device_id=line.beside(-1), device_id_type=MESH)

    @pl.when(stage < line.count - 1)
    def _():
        pl.semaphore_signal(barrier, inc=1, device_id=line.beside(1), device_id_type=MESH)

    expected = jnp.where(stage > 0, 1, 0) + jnp.where(stage < line.count - 1, 1, 0)
    if turned:
        me = Spot.here()
        alone = same(me, me.back())

        @pl.when(jnp.logical_not(alone))
        def _():
            hail(me.back())
            hail(me.ahead())

        expected = expected + jnp.where(alone, 0, 2)
        if feeding:
            expected = expected + hail_feeding(me, 0, 0) + hail_stagger(me, 0, 1)
        else:
            aside = me.yields() | me.carries()
            pl.when(aside)(lambda: hail(me.flip(y=1)))
            expected = expected + hail_stagger(me, line.count - 1, -1) + jnp.where(aside, 1, 0)
    pl.semaphore_wait(barrier, expected)


def forward_kernel(line, length, turned, x_first, x_in, words, wqkv_h, wproj_h, wup_h, wdown_h, small_in,
                   x_o, a_o, qkv_o, lse_o, o_o, h_o, a2_o, gp_o, u_o, acts_o, home_o,
                   wqkv, wproj, wup, wdown, xs, outs, a, qkv, lse, o, h, a2, gp, u, bias, ot, small,
                   w_sem, in_sem, x_sem, save_sem, act_sem, send_sem, recv_sem, home_sem, token):
    micro = xs.shape[0]
    stage = line.stage()
    loads = [
        pltpu.make_async_copy(src, dst, w_sem.at[i])
        for i, (src, dst) in enumerate(((wqkv_h, wqkv), (wproj_h, wproj), (wup_h, wup), (wdown_h, wdown)))
    ]
    loads[0].start()

    def first_in(m):
        return pltpu.make_async_copy(x_in.at[m], xs.at[m], in_sem.at[m])

    if turned:
        spread_small(small_in, small)
    else:
        small[...] = small_in[...]
    greet(line, turned, feeding=True)
    if turned:
        me = Spot.here()
        back = me.back()

        def turn_in(m):
            return pltpu.make_async_remote_copy(
                src_ref=x_in.at[m], dst_ref=xs.at[m], send_sem=in_sem.at[m], recv_sem=recv_sem.at[m],
                device_id=taker.id(), device_id_type=MESH)

        taker, feeder = me.fed_at(0), me.feeder(0)
        feeds = me.feeds(0, 0) & jnp.logical_not(same(me, taker))
        feeds_self = me.feeds(0, 0) & same(me, taker)
        homing, homed = me.gives_down(), me.takes_down()

        def home(m):
            return pltpu.make_async_remote_copy(
                src_ref=outs.at[m], dst_ref=home_o.at[m], send_sem=home_sem.at[0, m], recv_sem=home_sem.at[1, m],
                device_id=back.id(), device_id_type=MESH)

        @pl.when(stage == 0)
        def _():
            for m in range(FIRST):
                pltpu.make_async_copy(x_first.at[m], xs.at[m], in_sem.at[m]).start()

        for m in range(FIRST, micro):
            @pl.when(feeds)
            def _():
                turn_in(m).start()

            @pl.when(feeds_self)
            def _():
                first_in(m).start()
    else:
        @pl.when(stage == 0)
        def _():
            for m in range(micro):
                first_in(m).start()

    loads[0].wait()
    for load in loads[1:]:
        load.start()

    saved = ((a, a_o), (qkv, qkv_o), (lse, lse_o), (o, o_o), (h, h_o), (a2, a2_o), (gp, gp_o), (u, u_o))

    def saves(m, slot):
        return [
            pltpu.make_async_copy(here.at[slot], there.at[m], save_sem.at[slot, i])
            for i, (here, there) in enumerate(saved)
        ]

    def hop(m):
        return pltpu.make_async_remote_copy(
            src_ref=outs.at[m], dst_ref=xs.at[m], send_sem=send_sem.at[m], recv_sem=recv_sem.at[m],
            device_id=line.beside(1), device_id_type=MESH)

    def step(m, carry):
        slot = lax.rem(m, 2)

        if turned:
            here = jnp.logical_or(feeds_self, jnp.logical_and(stage == 0, m < FIRST))
        else:
            here = stage == 0

        @pl.when(here)
        def _():
            first_in(m).wait()

        @pl.when(jnp.logical_not(here))
        def _():
            hop(m).wait_recv()

        if turned:
            tell_stagger(me, 0, 1, token, m)
        pltpu.make_async_copy(xs.at[m], x_o.at[m], x_sem.at[m]).start()

        @pl.when(m >= 2)
        def _():
            for save in saves(m - 2, slot):
                save.wait()

        bias[...] = micro_bias(words, m, micro, length)

        def before(i):
            @pl.when(m == 0)
            def _():
                loads[i].wait()

        layer_forward(xs.at[m], bias, wqkv, wproj, wup, wdown, small, a.at[slot], qkv.at[slot],
                      lse.at[slot], o.at[slot], h.at[slot], a2.at[slot], gp.at[slot], u.at[slot],
                      outs.at[m], ot, before)

        if turned:
            wait_stagger(me, 0, token, m)

        @pl.when(stage < line.count - 1)
        def _():
            hop(m).start()

        for save in saves(m, slot):
            save.start()
        pltpu.make_async_copy(outs.at[m], acts_o.at[m], act_sem.at[m]).start()
        if turned:
            pl.when(homing & (m < EARLY))(lambda: home(m).start())
        return carry

    lax.fori_loop(0, micro, step, 0)

    for m in range(max(micro - 2, 0), micro):
        for save in saves(m, m % 2):
            save.wait()
    for m in range(micro):
        pltpu.make_async_copy(xs.at[m], x_o.at[m], x_sem.at[m]).wait()
        pltpu.make_async_copy(outs.at[m], acts_o.at[m], act_sem.at[m]).wait()

    @pl.when(stage < line.count - 1)
    def _():
        for m in range(micro):
            hop(m).wait_send()

    if turned:
        @pl.when(feeds)
        def _():
            for m in range(FIRST, micro):
                turn_in(m).wait_send()

        for m in range(EARLY):
            pl.when(homing)(lambda: home(m).wait_send())
            pl.when(homed)(lambda: home(m).wait_recv())


def backward_kernel(line, length, turned, acts_h, g_in, x_h, qkv_h, lse_h, h_h, gp_h, words,
                    wqkv_h, wproj_h, wup_h, wdown_h, small_in,
                    acts_o, home_o, side_o, g_o, dz_o, f_o, r_o, gin_o, sums_out,
                    wqkv, wproj, wup, wdown, gs, gins, x, qkv, lse, h, gp, dz, f, r, bias, do, dh, dqt, small, sums_o,
                    w_sem, in_sem, g_sem, load_sem, save_sem, act_sem, send_sem, recv_sem, home_sem, back_sem, side_sem, token):
    micro = gs.shape[0]
    stage = line.stage()
    loads = [
        pltpu.make_async_copy(src, dst, w_sem.at[i])
        for i, (src, dst) in enumerate(((wdown_h, wdown), (wup_h, wup), (wproj_h, wproj), (wqkv_h, wqkv)))
    ]

    def last_in(m):
        return pltpu.make_async_copy(g_in.at[m], gs.at[m], in_sem.at[m])

    @pl.when(stage == line.count - 1)
    def _():
        for m in range(micro):
            last_in(m).start()

    kept = ((gp_h, gp), (h_h, h), (qkv_h, qkv), (lse_h, lse), (x_h, x))

    def fetches(m, slot):
        return [
            pltpu.make_async_copy(there.at[m], here.at[slot], load_sem.at[slot, i])
            for i, (there, here) in enumerate(kept)
        ]

    loads[0].start()
    fetches(0, 0)[0].start()
    sums_o[...] = jnp.zeros_like(sums_o)
    if turned:
        spread_small(small_in, small)
    else:
        small[...] = small_in[...]
    greet(line, turned)
    if turned:
        me = Spot.here()
        back = me.back()
        alone = same(me, back)

        def home(m):
            return pltpu.make_async_remote_copy(
                src_ref=acts_h.at[m], dst_ref=acts_o.at[m], send_sem=home_sem.at[0, m], recv_sem=home_sem.at[1, m],
                device_id=back.id(), device_id_type=MESH)

        def stay(m):
            return pltpu.make_async_copy(acts_h.at[m], acts_o.at[m], home_sem.at[0, m])

        pairs = jnp.logical_not(alone)
        low, low_home = jnp.logical_not(me.gives_down()), jnp.logical_not(me.takes_down())

        def home_back(m):
            return pltpu.make_async_remote_copy(
                src_ref=gins.at[m], dst_ref=home_o.at[m], send_sem=back_sem.at[0, m], recv_sem=back_sem.at[1, m],
                device_id=back.id(), device_id_type=MESH)

        near, near_home = me.gives_near(), me.takes_near()

        def aside(m):
            return pltpu.make_async_remote_copy(
                src_ref=gins.at[m], dst_ref=side_o.at[m], send_sem=side_sem.at[0, m], recv_sem=side_sem.at[1, m],
                device_id=me.flip(y=1).id(), device_id_type=MESH)

        def settle_back(m):
            return pltpu.make_async_copy(gins.at[m], home_o.at[m], back_sem.at[0, m])

        for m in range(micro):
            now = low | (m >= EARLY)
            pl.when(alone & now)(lambda: stay(m).start())
            pl.when(pairs & now)(lambda: home(m).start())
    else:
        for m in range(micro):
            pltpu.make_async_copy(acts_h.at[m], acts_o.at[m], home_sem.at[0, m]).start()

    loads[0].wait()
    for load, some in zip(loads[1:], ((1,), (2, 3), (4,))):
        for i in some:
            fetches(0, 0)[i].start()
        load.start()
    saved = ((dz, dz_o), (f, f_o), (r, r_o))

    def saves(m, slot):
        return [
            pltpu.make_async_copy(here.at[slot], there.at[m], save_sem.at[slot, i])
            for i, (here, there) in enumerate(saved)
        ]

    def hop(m):
        return pltpu.make_async_remote_copy(
            src_ref=gins.at[m], dst_ref=gs.at[m], send_sem=send_sem.at[m], recv_sem=recv_sem.at[m],
            device_id=line.beside(-1), device_id_type=MESH)

    def step(m, carry):
        slot = lax.rem(m, 2)

        @pl.when(m + 1 < micro)
        def _():
            for fetch in fetches(m + 1, 1 - slot):
                fetch.start()

        def before(i):
            @pl.when(m == 0)
            def _():
                loads[i].wait()

            for at in ((), (1,), (2, 3), (4,))[i]:
                fetches(m, slot)[at].wait()

        fetches(m, slot)[0].wait()
        bias[...] = micro_bias(words, m, micro, length)

        @pl.when(m >= 2)
        def _():
            for save in saves(m - 2, slot):
                save.wait()

        @pl.when(stage == line.count - 1)
        def _():
            last_in(m).wait()

        @pl.when(stage < line.count - 1)
        def _():
            hop(m).wait_recv()

        if turned:
            tell_stagger(me, line.count - 1, -1, token, m)
        pltpu.make_async_copy(gs.at[m], g_o.at[m], g_sem.at[m]).start()
        layer_backward(gs.at[m], x.at[slot], bias, qkv.at[slot], lse.at[slot], h.at[slot], gp.at[slot],
                       wqkv, wproj, wup, wdown, small, dz.at[slot], f.at[slot], r.at[slot], gins.at[m],
                       sums_o, do, dh, dqt, before)

        if turned:
            wait_stagger(me, line.count - 1, token, m)

        @pl.when(stage > 0)
        def _():
            hop(m).start()

        for save in saves(m, slot):
            save.start()
        pltpu.make_async_copy(gins.at[m], gin_o.at[m], act_sem.at[m]).start()
        if turned:
            pl.when(pairs & low & (m < micro - 1))(lambda: home_back(m).start())
            pl.when(alone & low & (m < micro - 1))(lambda: settle_back(m).start())
            pl.when(me.yields())(lambda: aside(m).start())
        return carry

    lax.fori_loop(0, micro, step, 0)

    @pl.when(stage > 0)
    def _():
        for m in range(micro):
            hop(m).wait_send()

    if turned:
        @pl.when(near)
        def _():
            for m in range(micro):
                home_back(m).start()
    if turned:
        share_small(sums_o, sums_out)
    else:
        sums_out[...] = sums_o[...]

    for m in range(max(micro - 2, 0), micro):
        for save in saves(m, m % 2):
            save.wait()
    for m in range(micro):
        pltpu.make_async_copy(gs.at[m], g_o.at[m], g_sem.at[m]).wait()
        pltpu.make_async_copy(gins.at[m], gin_o.at[m], act_sem.at[m]).wait()

    for m in range(micro):
        if turned:
            pl.when(near)(lambda: home_back(m).wait_send())
            pl.when(near_home)(lambda: home_back(m).wait_recv())
            pl.when(me.yields())(lambda: aside(m).wait_send())
            pl.when(me.carries())(lambda: aside(m).wait_recv())
            now, then = low | (m >= EARLY), low_home | (m >= EARLY)
            pl.when(alone & now)(lambda: stay(m).wait())
            pl.when(pairs & now)(lambda: home(m).wait_send())
            pl.when(pairs & then)(lambda: home(m).wait_recv())
            if m < micro - 1:
                pl.when(pairs & low)(lambda: home_back(m).wait_send())
                pl.when(pairs & low_home)(lambda: home_back(m).wait_recv())
                pl.when(alone & low)(lambda: settle_back(m).wait())
        else:
            pltpu.make_async_copy(acts_h.at[m], acts_o.at[m], home_sem.at[0, m]).wait()


IN_VMEM = pl.BlockSpec(memory_space=pltpu.VMEM)
IN_SMEM = pl.BlockSpec(memory_space=pltpu.SMEM)
ANYWHERE = pl.BlockSpec(memory_space=pl.ANY)
DMA = pltpu.SemaphoreType.DMA


def run_forward(line, length, turned, x_first, x_in, words, weights, small):
    micro, rows, width = x_in.shape
    hidden = weights[2].shape[1]
    shape = jax.ShapeDtypeStruct
    saved = (
        ((rows, width), BF), ((rows, 3 * width), BF), ((16, rows), F32), ((rows, width), BF),
        ((rows, width), F32), ((rows, width), BF), ((rows, hidden), BF), ((rows, hidden), BF))
    many = shape((micro, rows, width), BF)
    return pl.pallas_call(
        functools.partial(forward_kernel, line, length, turned),
        out_shape=[many] + [shape((micro,) + s, t) for s, t in saved] + [many, many],
        in_specs=[ANYWHERE, ANYWHERE, IN_VMEM] + [ANYWHERE] * 4 + [IN_VMEM],
        out_specs=[ANYWHERE] * 11,
        scratch_shapes=[pltpu.VMEM(w.shape, BF) for w in weights]
        + [pltpu.VMEM((micro, rows, width), BF)] * 2
        + [pltpu.VMEM((2,) + s, t) for s, t in saved]
        + [pltpu.VMEM((rows, rows), F32), pltpu.VMEM((width, rows), BF), pltpu.VMEM((16, width), F32)]
        + [DMA((4,)), DMA((micro,)), DMA((micro,)), DMA((2, 8)), DMA((micro,)), DMA((micro,)), DMA((micro,)),
           DMA((2, micro)), pltpu.SemaphoreType.REGULAR],
        compiler_params=pltpu.CompilerParams(
            collective_id=0, has_side_effects=True, vmem_limit_bytes=VMEM_CAP),
        name="forward_line",
    )(x_first, x_in, words, *weights, small)


def run_backward(line, length, turned, acts, g_in, x, qkv, lse, h, gp, words, weights, small):
    micro, rows, width = g_in.shape
    hidden = weights[2].shape[1]
    shape = jax.ShapeDtypeStruct
    many = shape((micro, rows, width), BF)
    wqkv, wproj, wup, wdown = weights
    return pl.pallas_call(
        functools.partial(backward_kernel, line, length, turned),
        out_shape=[many, many, many, many, shape((micro, rows, hidden), BF), many, shape((micro, rows, 3 * width), BF), many,
                   shape(small.shape, F32)],
        in_specs=[ANYWHERE] * 7 + [IN_VMEM] + [ANYWHERE] * 4 + [IN_VMEM],
        out_specs=[ANYWHERE] * 8 + [IN_VMEM],
        scratch_shapes=[pltpu.VMEM(w.shape, BF) for w in weights]
        + [pltpu.VMEM((micro, rows, width), BF)] * 2
        + [pltpu.VMEM((2, rows, width), BF), pltpu.VMEM((2, rows, 3 * width), BF), pltpu.VMEM((2, 16, rows), F32),
           pltpu.VMEM((2, rows, width), F32), pltpu.VMEM((2, rows, hidden), BF),
           pltpu.VMEM((2, rows, hidden), BF), pltpu.VMEM((2, rows, width), BF), pltpu.VMEM((2, rows, 3 * width), BF),
           pltpu.VMEM((rows, rows), F32), pltpu.VMEM((rows, width), BF), pltpu.VMEM((rows, width), F32),
           pltpu.VMEM((width, rows), BF), pltpu.VMEM((16, width), F32), pltpu.VMEM((16, width), F32)]
        + [DMA((4,)), DMA((micro,)), DMA((micro,)), DMA((2, 5)), DMA((2, 3)), DMA((micro,)), DMA((micro,)),
           DMA((micro,)), DMA((2, micro)), DMA((2, micro)), DMA((2, micro)),
           pltpu.SemaphoreType.REGULAR],
        compiler_params=pltpu.CompilerParams(
            collective_id=1, has_side_effects=True, vmem_limit_bytes=VMEM_CAP),
        name="backward_line",
    )(acts, g_in, x, qkv, lse, h, gp, words, wqkv, wproj, wup, wdown, small)


GATHER_PIECES = ((0, 0, 48, "c"), (0, 48, 48, "x"), (4, 0, 16, "x"), (1, 0, 96, "c"), (2, 0, 48, "x"), (2, 48, 48, "c"),
                 (3, 0, 192, "x"), (3, 192, 192, "c"))


def gather_kernel(pieces, micro, *refs):
    count = 5
    masters, (x_in, g_in, seg_in, cls_in) = refs[:count], refs[count : count + 4]
    wholes, (x_o, x_all, g_o, seg_o) = refs[count + 4 : 2 * count + 4], refs[2 * count + 4 : 2 * count + 8]
    refs = refs[2 * count + 8 :]
    swap, wide, narrow, (x_raw, g_raw, x_pad, g_pad, words, table) = refs[:5], refs[5:9], refs[9:13], refs[13:19]
    send, recv, local, turn_send, turn_recv, load_sem = refs[19:]
    shares = narrow + (table,)
    loads = [pltpu.make_async_copy(masters[i], wide[i], load_sem.at[i]) for i in range(4)]
    loads += [pltpu.make_async_copy(x_in, x_raw, load_sem.at[4]), pltpu.make_async_copy(g_in, g_raw, load_sem.at[5])]
    for i in (0, 1, 2, 3, 4, 5):
        loads[i].start()
    me = Spot.here()
    xn, yn, cn = me.flip(x=1), me.flip(y=1), me.flip(c=1)
    target, source, ahead, back = me.drop(), me.source(), me.ahead(), me.back()
    stays, alone = same(me, target), same(me, back)
    moves, pairs = jnp.logical_not(stays), jnp.logical_not(alone)
    crosses = me.crosses()
    direct = jnp.logical_and(moves, jnp.logical_not(crosses))
    for spot in (xn, yn, cn):
        hail(spot)

    @pl.when(moves)
    def _():
        hail(target)
        hail(source)

    @pl.when(pairs)
    def _():
        hail(ahead)
        hail(back)

    fed = hail_feeding(me, 0, 0) + hail_feeding(me, 3, 1)
    expected = 3 + jnp.where(stays, 0, 2) + jnp.where(alone, 0, 2) + fed

    def rows(k, part):
        array, first, size, _ = pieces[k]
        share = shares[array].shape[0]
        return wholes[array].at[pl.ds(pl.multiple_of(part * share + first, 16), size)]

    def mine(k):
        array, first, size, _ = pieces[k]
        return shares[array].at[pl.ds(first, size)]

    def swapped(k):
        array, first, size, _ = pieces[k]
        return swap[array].at[pl.ds(first, size)]

    def remote(src, dst, kind, k, spot):
        return pltpu.make_async_remote_copy(
            src_ref=src, dst_ref=dst, send_sem=send.at[kind, k], recv_sem=recv.at[kind, k],
            device_id=spot.id(), device_id_type=MESH)

    def crossed(k):
        return remote(mine(k), swapped(k), 8, k, yn)

    def brought(k, part):
        return remote(mine(k), rows(k, part), 0, k, target)

    def brought_on(k, part):
        return remote(swapped(k), rows(k, part), 0, k, target)

    def kept(k):
        return pltpu.make_async_copy(mine(k), rows(k, me.dp()), local.at[k])

    def passed(kind, k, part, spot):
        return remote(rows(k, part), rows(k, part), kind, k, spot)

    def parts(spot):
        return [s.part() for s in (spot, spot.flip(x=1), spot.flip(y=1), spot.flip(x=1, y=1))]

    own, own_x, own_y, own_d = parts(me)
    beside = parts(cn)
    turns = [(words, seg_o)] + [(x_pad.at[m], x_o.at[m]) for m in range(FIRST)] + [(g_pad.at[m], g_o.at[m]) for m in range(micro)]
    gives = [me.z >= 0] + [me.feeds(0, 0)] * FIRST + [me.feeds(3, 1)] * micro
    takes = [me.z >= 0] + [me.z == 0] * FIRST + [me.z == 3] * micro
    takers = [ahead] + [me.fed_at(0)] * FIRST + [me.fed_at(3)] * micro
    givers = [back] + [me.feeder(0)] * FIRST + [me.feeder(1)] * micro

    def turn(i):
        return pltpu.make_async_remote_copy(
            src_ref=turns[i][0], dst_ref=turns[i][1], send_sem=turn_send.at[i], recv_sem=turn_recv.at[i],
            device_id=takers[i].id(), device_id_type=MESH)

    def turn_start(i):
        here = same(me, takers[i])
        pl.when(gives[i] & here)(lambda: pltpu.make_async_copy(*turns[i], turn_send.at[i]).start())
        pl.when(gives[i] & jnp.logical_not(here))(lambda: turn(i).start())

    def turn_end(i):
        here = same(me, takers[i])
        pl.when(gives[i] & here)(lambda: pltpu.make_async_copy(*turns[i], turn_send.at[i]).wait())
        pl.when(gives[i] & jnp.logical_not(here))(lambda: turn(i).wait_send())
        pl.when(takes[i] & jnp.logical_not(same(me, givers[i])))(lambda: turn(i).wait_recv())

    flat = masters[4][...].astype(BF).astype(F32)
    share = flat.shape[1] // 12
    table[...] = jnp.zeros_like(table)
    for i in range(8):
        table[i : i + 1, 0:share] = flat[:, i * share : (i + 1) * share]
    for i in range(share // 32):
        table[8 + i : 9 + i, :] = flat[:, 8 * share + 128 * i : 8 * share + 128 * (i + 1)]
    words[...] = jnp.full_like(words, -1)
    words[0:micro, 0 : seg_in.shape[1]] = seg_in[...]
    for m in range(micro):
        words[micro + m : micro + m + 1, :] = jnp.full((1, words.shape[1]), cls_in[m], jnp.int32)

    def pad(raw, padded):
        for m in range(micro):
            short = raw[m]
            rest = jnp.zeros((padded.shape[1] - short.shape[0], short.shape[1]), short.dtype)
            padded[m] = jnp.concatenate([short, rest], axis=0)

    ready = set()
    for k in range(len(pieces)):
        array = pieces[k][0]
        if array < 4 and array not in ready:
            ready.add(array)
            loads[array].wait()
            size = wide[array].shape[0]
            for first in range(0, size, 48):
                narrow[array][first : first + 48, :] = wide[array][first : first + 48, :].astype(BF)
        if k == 0:
            pl.semaphore_wait(pltpu.get_barrier_semaphore(), expected)
        pl.when(stays)(lambda: kept(k).start())
        pl.when(direct)(lambda: brought(k, me.dp()).start())
        pl.when(crosses)(lambda: crossed(k).start())
    turn_start(0)
    loads[4].wait()
    pad(x_raw, x_pad)
    for i in range(FIRST):
        turn_start(1 + i)
    x_save = pltpu.make_async_copy(x_pad, x_all, load_sem.at[4])
    x_save.start()
    loads[5].wait()
    pad(g_raw, g_pad)
    for k in range(len(pieces) + 3):
        if k < len(pieces):
            @pl.when(crosses)
            def _():
                crossed(k).wait_recv()
                brought_on(k, me.dp()).start()

        if k == len(pieces) - 1:
            for i in range(1 + FIRST, 1 + FIRST + micro):
                turn_start(i)
        b = k - 1
        if 0 <= b < len(pieces):
            pl.when(stays)(lambda: kept(b).wait())
            pl.when(moves)(lambda: brought(b, own).wait_recv())
            passed(1, b, own, xn).start()
            passed(2, b, own, yn).start()
            passed(4, b, own, cn).start()
        b = k - 2
        if 0 <= b < len(pieces):
            turn_x = (me.c == 0) if pieces[b][3] == "c" else (me.c < 0)
            passed(1, b, own_x, xn).wait_recv()
            pl.when(turn_x)(lambda: passed(3, b, own_x, yn).start())
            passed(5, b, own_x, cn).start()
            passed(2, b, own_y, yn).wait_recv()
            pl.when(jnp.logical_not(turn_x))(lambda: passed(3, b, own_y, xn).start())
            passed(6, b, own_y, cn).start()
        b = k - 3
        if 0 <= b < len(pieces):
            passed(3, b, own_d, yn).wait_recv()
            passed(7, b, own_d, cn).start()
    for k in range(len(pieces)):
        for kind in range(4, 8):
            passed(kind, k, beside[kind - 4], cn).wait_recv()
        pl.when(moves)(lambda: brought(k, own).wait_send())
        pl.when(crosses)(lambda: crossed(k).wait_send())
        for kind in range(1, 8):
            passed(kind, k, own, cn).wait_send()
    for i in range(len(turns)):
        turn_end(i)
    x_save.wait()


def run_gather(masters, inputs, g, segs, classes, rows):
    pieces = GATHER_PIECES
    micro, _, width = g.shape
    shape = jax.ShapeDtypeStruct
    shares = [shape(m.shape, BF) for m in masters[:4]] + [shape((16, 128), F32)]
    many = shape((micro, rows, width), BF)
    outs = [shape((s.shape[0] * 8,) + s.shape[1:], s.dtype) for s in shares]
    outs += [shape((FIRST, rows, width), BF), many, many, shape((2 * micro, rows), segs.dtype)]
    return pl.pallas_call(
        functools.partial(gather_kernel, pieces, micro),
        out_shape=outs,
        in_specs=[ANYWHERE] * 4 + [IN_VMEM] + [ANYWHERE] * 2 + [IN_VMEM, IN_SMEM],
        out_specs=[ANYWHERE] * 9,
        scratch_shapes=[pltpu.VMEM(s.shape, s.dtype) for s in shares] + [pltpu.VMEM(m.shape, F32) for m in masters[:4]]
        + [pltpu.VMEM(s.shape, BF) for s in shares[:4]] + [pltpu.VMEM(g.shape, BF)] * 2
        + [pltpu.VMEM((micro, rows, width), BF)] * 2
        + [pltpu.VMEM((2 * micro, rows), segs.dtype), pltpu.VMEM((16, 128), F32)]
        + [DMA((9, len(pieces))), DMA((9, len(pieces))), DMA((len(pieces),)), DMA((1 + FIRST + micro,)),
           DMA((1 + FIRST + micro,)), DMA((6,))],
        compiler_params=pltpu.CompilerParams(collective_id=2, has_side_effects=True, vmem_limit_bytes=VMEM_CAP),
        name="gather_layers",
    )(*masters, inputs, g, segs, classes)


SCATTER_PIECES = ((3, 0, 128, 0, 768, "x"), (3, 128, 128, 0, 768, "c"), (3, 256, 128, 0, 768, "x"),
                  (2, 0, 96, 0, 1024, "c"), (2, 0, 96, 1024, 1024, "x"), (2, 0, 96, 2048, 1024, "c"),
                  (0, 0, 96, 0, 768, "x"), (0, 0, 96, 768, 768, "c"), (0, 0, 96, 1536, 768, "x"),
                  (1, 0, 96, 0, 768, "c"), (4, 0, 16, 0, 128, "x"))


SCATTER_LAGS = (1, 3, 4, 5)


def scatter_kernel(pieces, micro, *refs):
    count = 5
    a_h, r_h, o_h, f_h, a2_h, dz_h, u_h, g_h, small_h, gin_in, side_in = refs[:11]
    outs, gin_o, norm_o = refs[11:16], refs[16], refs[17]
    at = 18
    totals, beside, diag, from_x, from_y, done, swap, home = (refs[at + i * count : at + (i + 1) * count] for i in range(8))
    (stream, fixed, flipped, sums, tallies, stream_sem, fixed_sem, send, recv, local, turn_sem, note_send, note_recv,
     out_sem) = refs[at + 8 * count :]
    me = Spot.here()
    xn, yn, cn = me.flip(x=1), me.flip(y=1), me.flip(c=1)
    target, giver, back, ahead = me.source(), me.drop(), me.back(), me.ahead()
    stays, alone = same(me, target), same(me, back)
    moves, pairs = jnp.logical_not(stays), jnp.logical_not(alone)
    crosses, target_crosses = me.crosses(), target.crosses()
    slab = [me.flip(x=i & 1, y=(i >> 1) & 1, c=i >> 2) for i in range(1, 8)]
    column = [Spot(me.x, me.y, (me.z + i) % 4, me.c) for i in range(1, 4)]
    left_right = {0: (a_h, r_h), 1: (o_h, f_h), 2: (a2_h, dz_h), 3: (u_h, g_h)}
    resting = (g_h, a2_h, a_h, o_h)
    rest_at = {3: 0, 2: 1, 0: 2, 1: 3}

    openers = {}
    for k in reversed(range(len(pieces))):
        openers[pieces[k][0]] = k
    opened = sorted((k, array) for array, k in openers.items() if array < 4)

    def streamed(k):
        array, first, size, column_at, columns, _ = pieces[k]
        slot = k % 2
        if array == 3:
            share = totals[3].shape[0] // 8
            return [pltpu.make_async_copy(u_h.at[:, pl.ds(p * share + first, size)],
                                          stream.at[slot, :, pl.ds(p * size, size)], stream_sem.at[slot, p])
                    for p in range(8)]
        if array == 4:
            return [pltpu.make_async_copy(small_h, totals[4], stream_sem.at[slot, 0])]
        return [pltpu.make_async_copy(left_right[array][1].at[:, pl.ds(column_at, columns)],
                                      stream.at[slot, :, pl.ds(0, columns)], stream_sem.at[slot, 0])]

    def rested(i):
        return pltpu.make_async_copy(resting[i], fixed.at[i], fixed_sem.at[i])

    for copy in streamed(0):
        copy.start()
    rested(rest_at[opened[0][1]]).start()
    for copy in streamed(1):
        copy.start()
    for _, array in opened[1:]:
        rested(rest_at[array]).start()
    for spot in slab + column:
        hail(spot)

    @pl.when(moves)
    def _():
        hail(target)
        hail(giver)

    @pl.when(pairs)
    def _():
        hail(back)
        hail(ahead)

    carried_to = Spot(me.x, 1, 0, me.z % 2)
    pl.when(me.carries())(lambda: hail(carried_to))
    pl.when(me.takes_carried())(lambda: hail(me.carrier()))

    def work(k):
        array, first, size, column_at, columns, _ = pieces[k]
        slot = k % 2
        for copy in streamed(k):
            copy.wait()
        if array == 4:
            pass
        elif array == 3:
            if k == openers[3]:
                rested(rest_at[3]).wait()
            share = totals[3].shape[0] // 8
            for p in range(0, 8, 2):
                both = lax.dot_general(stream[slot, :, p * size : (p + 2) * size], fixed[rest_at[3]], TN,
                                       preferred_element_type=F32).astype(BF)
                for i in range(2):
                    totals[3][(p + i) * share + first : (p + i) * share + first + size, :] = both[i * size : (i + 1) * size]
        else:
            if k == openers[array]:
                rested(rest_at[array]).wait()
                flipped[...] = fixed[rest_at[array]].T
            for c in range(0, columns, 256):
                totals[array][:, column_at + c : column_at + c + 256] = mm(flipped[...], stream[slot, :, c : c + 256]).astype(BF)
        if k + 2 < len(pieces):
            for copy in streamed(k + 2):
                copy.start()

    def parts(spot):
        return [s.part() for s in (spot, spot.flip(x=1), spot.flip(y=1), spot.flip(x=1, y=1))]

    kept, given = parts(me), parts(cn)

    def box(k):
        _, first, size, column_at, columns, _ = pieces[k]
        return pl.ds(first, size), pl.ds(column_at, columns)

    def whole(k, part):
        array, first, size, column_at, columns, _ = pieces[k]
        share = done[array].shape[0]
        return totals[array].at[pl.ds(pl.multiple_of(part * share + first, 16), size), pl.ds(column_at, columns)]

    def remote(src, dst, kind, k, spot):
        return pltpu.make_async_remote_copy(
            src_ref=src, dst_ref=dst, send_sem=send.at[kind, k], recv_sem=recv.at[kind, k],
            device_id=spot.id(), device_id_type=MESH)

    def of(refs_, k):
        return refs_[pieces[k][0]].at[box(k)]

    def crossed(k, j):
        return remote(whole(k, given[j]), beside[pieces[k][0]].at[(j,) + box(k)], j, k, cn)

    def to_diag(k, spot):
        return remote(whole(k, kept[3]), of(diag, k), 4, k, spot)

    def to_x(k):
        return remote(whole(k, kept[1]), of(from_x, k), 5, k, xn)

    def to_y(k):
        return remote(whole(k, kept[2]), of(from_y, k), 6, k, yn)

    def to_home(k):
        return remote(of(done, k), of(home, k), 7, k, target)

    def to_swap(k):
        return remote(of(done, k), of(swap, k), 7, k, target)

    def stay_home(k):
        return pltpu.make_async_copy(of(done, k), of(home, k), local.at[k])

    def over(k):
        return remote(of(swap, k), of(home, k), 8, k, yn)

    def add(k, j, extra):
        here = whole(k, kept[j])
        here[...] = (here[...].astype(F32) + extra.astype(F32)).astype(here.dtype)

    def turn(m):
        return pltpu.make_async_remote_copy(
            src_ref=gin_in.at[m], dst_ref=gin_o.at[m], send_sem=turn_sem.at[0, m], recv_sem=turn_sem.at[1, m],
            device_id=back.id(), device_id_type=MESH)

    def carry(m):
        return pltpu.make_async_remote_copy(
            src_ref=side_in.at[m], dst_ref=gin_o.at[m], send_sem=turn_sem.at[2, m], recv_sem=turn_sem.at[1, m],
            device_id=carried_to.id(), device_id_type=MESH)

    gives_now = me.gives_down() & jnp.logical_not(me.gives_near() | me.yields())
    takes_now = me.takes_down() & jnp.logical_not(me.takes_near())

    def turn_stay(m):
        return pltpu.make_async_copy(gin_in.at[m], gin_o.at[m], turn_sem.at[0, m])

    work(0)
    pl.semaphore_wait(pltpu.get_barrier_semaphore(), 10 + jnp.where(stays, 0, 2) + jnp.where(alone, 0, 2)
                      + jnp.where(me.carries(), 1, 0) + jnp.where(me.takes_carried(), 1, 0))
    for m in range(micro):
        now = gives_now | (m == micro - 1) & jnp.logical_not(me.gives_down())
        pl.when(alone & now)(lambda: turn_stay(m).start())
        pl.when(pairs & now)(lambda: turn(m).start())
        pl.when(me.carries())(lambda: carry(m).start())
    tally = jnp.zeros((8, 128), F32)
    for k in range(len(pieces) + SCATTER_LAGS[3]):
        if k < len(pieces):
            if k > 0:
                work(k)
            for j in (3, 2, 1, 0):
                crossed(k, j).start()
        b = k - SCATTER_LAGS[0]
        if 0 <= b < len(pieces):
            turn_x = (me.c == 0) if pieces[b][5] == "c" else (me.c < 0)
            for j in (3, 2, 1, 0):
                crossed(b, j).wait_recv()
                add(b, j, beside[pieces[b][0]][(j,) + box(b)])
                if j == 3:
                    pl.when(turn_x)(lambda: to_diag(b, yn).start())
                    pl.when(jnp.logical_not(turn_x))(lambda: to_diag(b, xn).start())
                if j == 2:
                    pl.when(turn_x)(lambda: to_y(b).start())
                if j == 1:
                    pl.when(jnp.logical_not(turn_x))(lambda: to_x(b).start())
        b = k - SCATTER_LAGS[1]
        if 0 <= b < len(pieces):
            to_diag(b, yn).wait_recv()
            turn_x = (me.c == 0) if pieces[b][5] == "c" else (me.c < 0)

            @pl.when(turn_x)
            def _():
                add(b, 1, of(diag, b)[...])
                to_x(b).start()

            @pl.when(jnp.logical_not(turn_x))
            def _():
                add(b, 2, of(diag, b)[...])
                to_y(b).start()
        b = k - SCATTER_LAGS[2]
        if 0 <= b < len(pieces):
            to_x(b).wait_recv()
            to_y(b).wait_recv()
            total = (whole(b, kept[0])[...].astype(F32) + of(from_x, b)[...].astype(F32) + of(from_y, b)[...].astype(F32))
            total = total.astype(done[pieces[b][0]].dtype)
            done[pieces[b][0]][box(b)] = total
            square = total.astype(F32) * total.astype(F32)
            for c in range(0, square.shape[1], 128):
                tally = tally + jnp.sum(square[:, c : c + 128].reshape(-1, 8, 128), axis=0)
            pl.when(stays)(lambda: stay_home(b).start())
            pl.when(moves & jnp.logical_not(target_crosses))(lambda: to_home(b).start())
            pl.when(target_crosses)(lambda: to_swap(b).start())
        b = k - SCATTER_LAGS[3]
        if 0 <= b < len(pieces):
            @pl.when(crosses)
            def _():
                to_swap(b).wait_recv()
                over(b).start()
    sums[0] = tally

    def note(i, src, slot, spot):
        return pltpu.make_async_remote_copy(
            src_ref=src, dst_ref=tallies.at[slot], send_sem=note_send.at[i], recv_sem=note_recv.at[slot],
            device_id=spot.id(), device_id_type=MESH)

    for i, spot in enumerate(column):
        note(i, sums.at[0], i, spot).start()
    for i, spot in enumerate(column):
        note(i, sums.at[0], i, spot).wait_recv()
        tally = tally + tallies[i]
    sums[1] = tally
    for i, spot in enumerate(slab):
        note(3 + i, sums.at[1], 3 + i, spot).start()
    for i, spot in enumerate(slab):
        note(3 + i, sums.at[1], 3 + i, spot).wait_recv()
        tally = tally + tallies[3 + i]
    whole_norm = jnp.sqrt(jnp.sum(jnp.sum(tally, axis=0, keepdims=True), axis=1, keepdims=True))
    norm_o[...] = jnp.broadcast_to(whole_norm, norm_o.shape)
    last = {}
    for k in range(len(pieces)):
        last[pieces[k][0]] = k
    for k in range(len(pieces)):
        pl.when(stays)(lambda: stay_home(k).wait())
        pl.when(moves & jnp.logical_not(crosses))(lambda: to_home(k).wait_recv())
        pl.when(crosses)(lambda: over(k).wait_recv())
        array = pieces[k][0]
        if last[array] == k:
            pltpu.make_async_copy(home[array], outs[array], out_sem.at[array]).start()
    for i, spot in enumerate(column):
        note(i, sums.at[0], i, spot).wait_send()
    for i, spot in enumerate(slab):
        note(3 + i, sums.at[1], 3 + i, spot).wait_send()
    for k in range(len(pieces)):
        for j in range(4):
            crossed(k, j).wait_send()
        to_diag(k, yn).wait_send()
        to_x(k).wait_send()
        to_y(k).wait_send()
        pl.when(moves)(lambda: to_home(k).wait_send())
        pl.when(crosses)(lambda: over(k).wait_send())
    for m in range(micro):
        last_one = m == micro - 1
        now = gives_now | last_one & jnp.logical_not(me.gives_down())
        then = takes_now | last_one & jnp.logical_not(me.takes_down())
        pl.when(me.carries())(lambda: carry(m).wait_send())
        pl.when(alone & now)(lambda: turn_stay(m).wait())
        pl.when(pairs & now)(lambda: turn(m).wait_send())
        pl.when(pairs & then)(lambda: turn(m).wait_recv())
    for array in range(count):
        pltpu.make_async_copy(home[array], outs[array], out_sem.at[array]).wait()


def run_scatter(operands, small, gin, side):
    pieces = SCATTER_PIECES
    micro = gin.shape[0]
    shape = jax.ShapeDtypeStruct
    a, r, o, f, a2, dz, u, g = operands = [v.reshape(-1, v.shape[-1]) for v in operands]
    rows = a.shape[0]
    sizes = [((left.shape[1], right.shape[1]), BF) for left, right in ((a, r), (o, f), (a2, dz), (u, g))]
    sizes.append((small.shape, F32))
    shares = [((s[0] // 8, s[1]), t) for s, t in sizes]
    one = [pltpu.VMEM(s, t) for s, t in shares]
    return pl.pallas_call(
        functools.partial(scatter_kernel, pieces, micro),
        out_shape=[shape(s, t) for s, t in shares] + [shape(gin.shape, gin.dtype), shape((8, 128), F32)],
        in_specs=[ANYWHERE] * 11,
        out_specs=[ANYWHERE] * 6 + [IN_VMEM],
        scratch_shapes=[pltpu.VMEM(s, t) for s, t in sizes] + [pltpu.VMEM((4,) + s, t) for s, t in shares] + one * 6
        + [pltpu.VMEM((2, rows, 1024), BF), pltpu.VMEM((4, rows, a.shape[1]), BF), pltpu.VMEM((a.shape[1], rows), BF),
           pltpu.VMEM((2, 8, 128), F32), pltpu.VMEM((10, 8, 128), F32), DMA((2, 8)), DMA((4,)),
           DMA((9, len(pieces))), DMA((9, len(pieces))), DMA((len(pieces),)), DMA((3, micro)), DMA((10,)), DMA((10,)),
           DMA((5,))],
        compiler_params=pltpu.CompilerParams(collective_id=3, has_side_effects=True, vmem_limit_bytes=VMEM_CAP),
        name="scatter_layers",
    )(*operands, small, gin, side)


def finish_kernel(order, micro, norm, *refs):
    table, small_state, refs = refs[0], refs[1:4], refs[4:]
    shards_h, state_h, (acts_early, acts_late, gin_early, gin_late) = refs[:4], refs[4:16], refs[16:20]
    norm_o, small_o, refs = refs[20], refs[21:25], refs[5:]
    state_o, acts_o, gin_o = refs[20:36], refs[36], refs[37]
    shards, state, (acts, gin, acts_cut, gin_cut, row) = refs[38:42], refs[42:58], refs[58:63]
    load_sem, pick_sem, out_sem = refs[63:]
    me = Spot.here()
    upper, near = me.takes_down(), me.takes_near()

    def loads(array):
        copies = [pltpu.make_async_copy(shards_h[array], shards[array], load_sem.at[array, 0])]
        for i in range(3):
            copies.append(pltpu.make_async_copy(state_h[4 * i + array], state[4 * (i + 1) + array], load_sem.at[array, 1 + i]))
        return copies

    def pick(i, m, src, dst):
        return pltpu.make_async_copy(src.at[m], dst.at[m], pick_sem.at[i, m])

    def saves(array):
        return [pltpu.make_async_copy(state[4 * i + array], state_o[4 * array + i], out_sem.at[array, i]) for i in range(4)]

    for array in order:
        for copy in loads(array):
            copy.start()
    for m in range(micro):
        from_early = (upper & (m < EARLY), jnp.logical_not(upper) & (m < micro - 1) | near)
        for i, (early, late, dst) in enumerate(((acts_early, acts_late, acts), (gin_early, gin_late, gin))):
            pl.when(from_early[i])(lambda: pick(i, m, early, dst).start())
            pl.when(jnp.logical_not(from_early[i]))(lambda: pick(i, m, late, dst).start())
    factor = 1.0 / jnp.maximum(norm[0:1, 0:1], 1.0)
    fix = 1.0 / (1.0 - 0.5**STEP)
    strip = 16
    norm_o[0] = norm[0, 0]
    share = row.shape[1] // 12
    for i in range(8):
        row[:, i * share : (i + 1) * share] = table[i : i + 1, 0:share]
    for i in range(share // 32):
        row[:, 8 * share + 128 * i : 8 * share + 128 * (i + 1)] = table[8 + i : 9 + i, :]
    grad = row[...] * factor
    first_new = 0.5 * small_state[1][...] + 0.5 * grad
    second_new = 0.5 * small_state[2][...] + 0.5 * grad * grad
    small_o[0][...] = grad
    small_o[1][...] = small_state[0][...] - small_rate * ((first_new * fix) / (jnp.sqrt(second_new * fix) + adam_eps))
    small_o[2][...] = first_new
    small_o[3][...] = second_new
    for array in order:
        for copy in loads(array):
            copy.wait()
        grads, master, first, second = state[array], state[4 + array], state[8 + array], state[12 + array]

        def update(i, carry):
            rows = pl.ds(pl.multiple_of(i * strip, strip), strip)
            grad = shards[array][rows, :].astype(F32) * factor
            first_new = 0.5 * first[rows, :] + 0.5 * grad
            second_new = 0.5 * second[rows, :] + 0.5 * grad * grad
            old = master[rows, :]
            change = (first_new * fix) / (jnp.sqrt(second_new * fix) + adam_eps) + decay_rate * old
            grads[rows, :] = grad
            first[rows, :] = first_new
            second[rows, :] = second_new
            master[rows, :] = old - learn_rate * change
            return carry

        lax.fori_loop(0, grads.shape[0] // strip, update, 0)
        for copy in saves(array):
            copy.start()
    length = acts_cut.shape[1]
    for i, (src, cut, out) in enumerate(((acts, acts_cut, acts_o), (gin, gin_cut, gin_o))):
        for m in range(micro):
            pick(i, m, gin_late, src).wait()
            cut[m] = src[m, 0:length, :]
        pltpu.make_async_copy(cut, out, out_sem.at[4, i]).start()
    for array in order:
        for copy in saves(array):
            copy.wait()
    for i, (cut, out) in enumerate(((acts_cut, acts_o), (gin_cut, gin_o))):
        pltpu.make_async_copy(cut, out, out_sem.at[4, i]).wait()


def run_finish(norm, table, small_states, shards, states, tall, length):
    micro, rows, width = tall[0].shape
    shape = jax.ShapeDtypeStruct
    return pl.pallas_call(
        functools.partial(finish_kernel, (1, 0, 2, 3), micro),
        out_shape=[shape((1,), F32)] + [shape(small_states[0].shape, F32)] * 4
        + [shape(s.shape, F32) for s in shards for _ in range(4)] + [shape((micro, length, width), BF)] * 2,
        in_specs=[IN_VMEM] * 5 + [ANYWHERE] * 20,
        out_specs=[IN_SMEM] + [IN_VMEM] * 4 + [ANYWHERE] * 18,
        scratch_shapes=[pltpu.VMEM(s.shape, BF) for s in shards]
        + [pltpu.VMEM(s.shape, F32) for _ in range(4) for s in shards]
        + [pltpu.VMEM((micro, rows, width), BF)] * 2 + [pltpu.VMEM((micro, length, width), BF)] * 2
        + [pltpu.VMEM(small_states[0].shape, F32)] + [DMA((4, 4)), DMA((2, micro)), DMA((5, 4))],
        compiler_params=pltpu.CompilerParams(vmem_limit_bytes=VMEM_CAP),
        name="finish",
    )(norm, table, *small_states, *shards, *states, *tall)


def split_small(small, width, slices):
    share = width // slices
    stacked = small.reshape(slices, small.shape[0] // slices)
    eight = stacked[:, : 8 * share].reshape(slices, 8, share).transpose(1, 0, 2).reshape(8, width)
    up = stacked[:, 8 * share :].reshape(-1, width)
    return jnp.concatenate([eight, up, jnp.zeros((16 - 8 - up.shape[0], width), small.dtype)], axis=0)


def join_small(table, total, slices):
    width = table.shape[1]
    share = width // slices
    ups = total // width - 8
    eight = table[:8].reshape(8, slices, share).transpose(1, 0, 2).reshape(slices, 8 * share)
    up = table[8 : 8 + ups].reshape(slices, -1)
    return jnp.concatenate([eight, up], axis=1).reshape(-1)


def weight_grad(left, right):
    rows = left.shape[0] * left.shape[1]
    return lax.dot_general(left.reshape(rows, -1), right.reshape(rows, -1), (((0,), (0,)), ((), ())),
                           preferred_element_type=F32)


def adam(grad, master, first, second, rate, decay):
    fix = 1.0 - 0.5**STEP
    first = 0.5 * first + 0.5 * grad
    second = 0.5 * second + 0.5 * grad * grad
    update = first / fix / (jnp.sqrt(second / fix) + adam_eps)
    if decay:
        update = update + decay * master
    return [grad, master - rate * update, first, second]


def per_device(inputs, out_grad, segment_ids, cls_index, *states):
    masters, firsts, seconds = states[0:5], states[5:10], states[10:15]
    slices = lax.axis_size("dp")
    stages = lax.axis_size("section")
    turned = slices == 8 and stages == 4
    seq_dev, length, width = inputs.shape
    rows = -(-length // 128) * 128
    share = masters[4].shape[1]
    total = share * slices

    if turned:
        line = Line("dp", 4, 2)
        *weights, small, x_first, x_in, g_in, words = run_gather(
            [m[0] for m in masters[:4]] + [masters[4]], inputs, out_grad, segment_ids, cls_index, rows)
    else:
        line = Line("section", stages, 1)
        extra = ((0, 0), (0, rows - length), (0, 0))
        x_in, g_in = jnp.pad(inputs, extra), jnp.pad(out_grad, extra)
        segs = jnp.pad(segment_ids, ((0, 0), (0, rows - length)), constant_values=-1)
        words = jnp.concatenate([segs, jnp.broadcast_to(cls_index[:, None], (seq_dev, rows))], axis=0)
        gathered = [lax.all_gather(m[0].astype(BF), "dp", axis=0, tiled=True) for m in masters]
        weights, x_first = gathered[:4], x_in[0]
        small = split_small(gathered[4].astype(F32), width, slices)

    x, a, qkv, lse, o, h, a2, gp, u, acts, acts_early = run_forward(
        line, length, turned, x_first, x_in, words, weights, small)
    acts, gin_early, side, g, dz, f, r, gin, sums = run_backward(
        line, length, turned, acts, g_in, x, qkv, lse, h, gp, words, weights, small)
    results = []
    if turned:
        matrix_states = [v[0] for group in (masters, firsts, seconds) for v in group[:4]]
        *shards, table, gin, norm = run_scatter([a, r, o, f, a2, dz, u, g], sums, gin, side)
        grad_norm, *rest = run_finish(norm, table, [masters[4], firsts[4], seconds[4]], shards, matrix_states,
                                      [acts_early, acts, gin_early, gin], length)
        acts, gin = rest[20:]
        results = [v[None] for v in rest[4:20]] + rest[:4]
    else:
        acts, gin = acts[:, :length], gin[:, :length]
        totals = [weight_grad(a, r).astype(BF), weight_grad(o, f).astype(BF), weight_grad(a2, dz).astype(BF),
                  weight_grad(u, g).astype(BF), join_small(sums, total, slices)]
        shards = [lax.psum_scatter(t[None], "dp", scatter_dimension=1, tiled=True).astype(F32) for t in totals]
        squares = jnp.sum(jnp.stack([jnp.sum(s * s) for s in shards]))
        grad_norm = jnp.sqrt(lax.psum(squares, ("dp", "section")))
        factor = 1.0 / jnp.maximum(grad_norm, 1.0)
        for kind in range(5):
            rate, decay = (learn_rate, decay_rate) if kind < 4 else (small_rate, 0.0)
            results += adam(shards[kind] * factor, masters[kind], firsts[kind], seconds[kind], rate, decay)
    return (acts[None], gin[None], grad_norm.reshape(1)) + tuple(results)


def solution(mesh):
    matrix, vector = P("section", "dp", None), P("section", "dp")
    states = (matrix,) * 4 + (vector,)
    return jax.shard_map(
        per_device,
        mesh=mesh,
        in_specs=(P("dp", None, None), P("dp", None, None), P("dp", None), P("dp")) + states * 3,
        out_specs=(P("section", "dp", None, None), P("section", "dp", None, None), P())
        + (matrix,) * 16 + (vector,) * 4,
        check_vma=False,
    )
```

```python
import functools

import jax
import jax.numpy as jnp
from jax import lax
from jax.experimental import pallas as pl
from jax.experimental.pallas import tpu as pltpu
from jax.sharding import PartitionSpec as P

HEADS = 12
STEP = 3
F32 = jnp.float32
BF = jnp.bfloat16
MESH = pl.DeviceIdType.MESH
VMEM_CAP = 60 * 1024 * 1024
EARLY = 3
FIRST = 2

norm_eps = 1e-06
masked_score = -1e30
learn_rate = 0.05
small_rate = 0.3
decay_rate = 0.05
adam_eps = 1e-08

NT = (((1,), (1,)), ((), ()))
TN = (((0,), (0,)), ((), ()))


def mm(a, b):
    return jnp.dot(a, b, preferred_element_type=F32)


def mm_nt(a, b):
    return lax.dot_general(a, b, NT, preferred_element_type=F32)


def norm_parts(values):
    center = values - jnp.mean(values, axis=-1, keepdims=True)
    spread = jnp.mean(center * center, axis=-1, keepdims=True)
    inv = lax.rsqrt(spread + norm_eps)
    return center * inv, inv


def norm_back(y, normed, inv):
    pull = jnp.mean(y * normed, axis=-1, keepdims=True)
    return (y - jnp.mean(y, axis=-1, keepdims=True) - normed * pull) * inv


def column_sum(values):
    return jnp.sum(values, axis=0, keepdims=True)


def mask_bias(seg_row, seg_col, cls_row, length):
    size = seg_col.shape[0]
    key_at = lax.broadcasted_iota(jnp.int32, (size, size), 0)
    query_at = lax.broadcasted_iota(jnp.int32, (size, size), 1)
    allowed = (seg_row == seg_col) | (key_at == cls_row) | (query_at == cls_row)
    allowed = allowed & (key_at < length)
    return jnp.where(allowed, 0.0, masked_score).astype(F32)


def micro_bias(words, m, micro, length):
    seg_row, cls_row = words[pl.ds(m, 1), :], words[pl.ds(micro + m, 1), :]
    size = seg_row.shape[1]
    on_diagonal = lax.broadcasted_iota(jnp.int32, (size, size), 0) == lax.broadcasted_iota(jnp.int32, (size, size), 1)
    seg_col = jnp.sum(jnp.where(on_diagonal, seg_row.astype(F32), 0.0), axis=1, keepdims=True)
    return mask_bias(seg_row.astype(F32), seg_col, cls_row, length)


def spread_small(table, small):
    width = small.shape[1]
    share, ups = width // 8, width // 256
    small[...] = jnp.zeros_like(small)
    for i in range(8):
        small[0:8, i * share : (i + 1) * share] = table[16 * i : 16 * i + 8, 0:share]
        for j in range(ups):
            at = i % 2 * (width // 2) + j * 128
            small[8 + i // 2 : 9 + i // 2, at : at + 128] = table[16 * i + 8 + j : 16 * i + 9 + j, :]


def share_small(sums, table):
    width = sums.shape[1]
    share, ups = width // 8, width // 256
    table[...] = jnp.zeros_like(table)
    for i in range(8):
        table[16 * i : 16 * i + 8, 0:share] = sums[0:8, i * share : (i + 1) * share]
        for j in range(ups):
            at = i % 2 * (width // 2) + j * 128
            table[16 * i + 8 + j : 16 * i + 9 + j, :] = sums[8 + i // 2 : 9 + i // 2, at : at + 128]


def gelu_parts(z):
    density = jnp.exp(z * z * -0.5) * 0.3989422804014327
    below = 0.5 + 0.5 * lax.erf(z * 0.7071067811865476)
    return z * below, below + z * density


def layer_forward(x_ref, bias_ref, wqkv, wproj, wup, wdown, small, a_ref, qkv_ref, lse_ref, o_ref,
                  h_ref, a2_ref, gp_ref, u_ref, out_ref, ot_ref, before):
    rows, width = x_ref.shape
    hidden = wup.shape[1]
    normed, _ = norm_parts(x_ref[...].astype(F32))
    a_ref[...] = (normed * small[0:1, :] + small[1:2, :]).astype(BF)
    for part in range(3):
        cols = slice(part * width, (part + 1) * width)
        mixed = mm(a_ref[...], wqkv[:, cols])
        if part == 0:
            mixed = mixed + small[2:3, :]
        if part == 2:
            mixed = mixed + small[3:4, :]
        qkv_ref[:, cols] = mixed.astype(BF)
    lane = lax.broadcasted_iota(jnp.int32, (rows, 128), 1)
    scores, raised, inverse = {}, {}, {}
    for step in range(HEADS + 2):
        if step < HEADS:
            at = step // 2 * 128
            half = (lane < 64) if step % 2 == 0 else (lane >= 64)
            k = qkv_ref[:, width + at : width + at + 128]
            k = jnp.where(half, k, jnp.zeros_like(k)) * jnp.asarray(0.125, BF)
            scores[step] = mm_nt(k, qkv_ref[:, at : at + 128])
        head = step - 1
        if 0 <= head < HEADS:
            shifted = scores.pop(head) + bias_ref[...]
            peak = jnp.max(shifted, axis=0, keepdims=True)
            grown = jnp.exp(shifted - peak)
            summed = jnp.sum(grown, axis=0, keepdims=True)
            raised[head] = grown.astype(BF)
            inverse[head] = 1.0 / summed
            lse_ref[head : head + 1, :] = peak + jnp.log(summed)
        head = step - 2
        if 0 <= head < HEADS:
            if head % 2 == 0:
                vt = qkv_ref[:, 2 * width + head * 64 : 2 * width + head * 64 + 128].T
            mixed = mm(vt[head % 2 * 64 : head % 2 * 64 + 64, :], raised.pop(head)) * inverse.pop(head)
            ot_ref[head * 64 : head * 64 + 64, :] = mixed.astype(BF)
    o_ref[...] = ot_ref[...].T
    before(1)
    h = x_ref[...].astype(F32) + (mm(o_ref[...], wproj[...]) + small[4:5, :])
    h_ref[...] = h
    normed, _ = norm_parts(h)
    a2_ref[...] = (normed * small[5:6, :] + small[6:7, :]).astype(BF)
    before(2)
    chunk = width
    z = {}
    for step in range(hidden // chunk + 1):
        cols = slice(step * chunk, (step + 1) * chunk)
        if step < hidden // chunk:
            row, start = 8 + step * chunk // width, step * chunk % width
            z[step] = mm(a2_ref[...], wup[:, cols]) + small[row : row + 1, start : start + chunk]
        part = step - 1
        if 0 <= part < hidden // chunk:
            cols = slice(part * chunk, (part + 1) * chunk)
            u, slope = gelu_parts(z.pop(part))
            u_ref[:, cols] = u.astype(BF)
            gp_ref[:, cols] = slope.astype(BF)
    before(3)
    total = mm(u_ref[...], wdown[...])
    out_ref[...] = (h_ref[...] + (total + small[7:8, :])).astype(BF)


def layer_backward(g_ref, x_ref, bias_ref, qkv_ref, lse_ref, h_ref, gp_ref, wqkv, wproj, wup, wdown,
                   small, dz_ref, f_ref, r_ref, gin_ref, sums_ref, do_ref, dh_ref, dqt_ref, before):
    rows, width = x_ref.shape
    hidden = wup.shape[1]
    carried = g_ref[...].astype(F32)
    sums_ref[7:8, :] += column_sum(carried)
    back = {}
    for step in range(hidden // width + 1):
        if step < hidden // width:
            back[step] = mm_nt(g_ref[...], wdown[step * width : (step + 1) * width, :])
        part = step - 1
        if part >= 0:
            cols = slice(part * width, (part + 1) * width)
            dz = (back.pop(part) * gp_ref[:, cols].astype(F32)).astype(BF)
            dz_ref[:, cols] = dz
            sums_ref[8 + part : 9 + part, :] += column_sum(dz.astype(F32))
    before(1)
    back = mm_nt(dz_ref[...], wup[...])
    normed, inv = norm_parts(h_ref[...])
    sums_ref[5:6, :] += column_sum(back * normed)
    sums_ref[6:7, :] += column_sum(back)
    dh = carried + norm_back(back * small[5:6, :], normed, inv)
    dh_ref[...] = dh
    f = dh.astype(BF)
    f_ref[...] = f
    sums_ref[4:5, :] += column_sum(f.astype(F32))
    before(2)
    do_ref[...] = mm_nt(f_ref[...], wproj[...]).astype(BF)
    lane = lax.broadcasted_iota(jnp.int32, (rows, 128), 1)
    scores, grads, probs, slopes, dks, dvs = {}, {}, {}, {}, {}, {}
    eighth = jnp.asarray(0.125, BF)
    for step in range(HEADS + 2):
        if step < HEADS:
            at = step // 2 * 128
            half = (lane < 64) if step % 2 == 0 else (lane >= 64)
            k = qkv_ref[:, width + at : width + at + 128]
            v = qkv_ref[:, 2 * width + at : 2 * width + at + 128]
            scores[step] = mm_nt(jnp.where(half, k, jnp.zeros_like(k)) * eighth, qkv_ref[:, at : at + 128])
            grads[step] = mm_nt(jnp.where(half, v, jnp.zeros_like(v)), do_ref[:, at : at + 128])
        head = step - 1
        if 0 <= head < HEADS:
            p = jnp.exp(scores.pop(head) + bias_ref[...] - lse_ref[head : head + 1, :])
            dp = grads.pop(head)
            inner = jnp.sum(p * dp, axis=0, keepdims=True)
            slopes[head] = (p * (dp - inner)).astype(BF)
            probs[head] = p.astype(BF)
        head = step - 2
        if 0 <= head < HEADS:
            at = head // 2 * 128
            side = head % 2
            ds = slopes.pop(head)
            dvs[side] = mm(probs.pop(head), do_ref[:, at : at + 128])
            dks[side] = mm(ds, qkv_ref[:, at : at + 128] * eighth)
            if side == 0:
                kt = (qkv_ref[:, width + at : width + at + 128] * eighth).T
            dqt_ref[head * 64 : head * 64 + 64, :] = mm(kt[side * 64 : side * 64 + 64, :], ds).astype(BF)
            if side == 1:
                r_ref[:, width + at : width + at + 128] = jnp.where(lane < 64, dks[0], dks[1]).astype(BF)
                r_ref[:, 2 * width + at : 2 * width + at + 128] = jnp.where(lane < 64, dvs[0], dvs[1]).astype(BF)
    r_ref[:, 0:width] = dqt_ref[...].T
    sums_ref[2:3, :] += column_sum(r_ref[:, 0:width].astype(F32))
    sums_ref[3:4, :] += column_sum(r_ref[:, 2 * width :].astype(F32))
    before(3)
    back = mm_nt(r_ref[...], wqkv[...])
    normed, inv = norm_parts(x_ref[...].astype(F32))
    sums_ref[0:1, :] += column_sum(back * normed)
    sums_ref[1:2, :] += column_sum(back)
    gin_ref[...] = (dh_ref[...] + norm_back(back * small[0:1, :], normed, inv)).astype(BF)


class Line:
    def __init__(self, axis, count, stride):
        self.axis, self.count, self.stride = axis, count, stride

    def stage(self):
        return lax.axis_index(self.axis) // self.stride

    def beside(self, by):
        return {self.axis: lax.axis_index(self.axis) + by * self.stride}


class Spot:
    def __init__(self, x, y, z, c):
        self.x, self.y, self.z, self.c = x, y, z, c

    @staticmethod
    def here():
        dp, section = lax.axis_index("dp"), lax.axis_index("section")
        return Spot(dp % 2, section // 2, dp // 2, section % 2)

    def dp(self):
        return self.z * 2 + self.x

    def section(self):
        return self.y * 2 + self.c

    def id(self):
        return (self.dp(), self.section())

    def flip(self, x=0, y=0, c=0):
        return Spot(1 - self.x if x else self.x, 1 - self.y if y else self.y, self.z, 1 - self.c if c else self.c)

    def ahead(self):
        return Spot(self.x, self.z % 2, self.section(), self.z // 2)

    def back(self):
        return Spot(self.x, self.z // 2, 2 * self.c + self.y, self.z % 2)

    def feeds(self, stage, core):
        return ((self.y == self.z % 2) & (self.c == core)) & (self.z >= 0)

    def fed_at(self, stage):
        return Spot(self.x, self.y, stage, self.z // 2)

    def feeder(self, core):
        return Spot(self.x, self.y, 2 * self.c + self.y, core)

    def gives_down(self):
        return self.back().z < self.z

    def takes_down(self):
        return self.z < self.section()

    def gives_near(self):
        return (self.z >= 2) & (self.back().z == self.z - 1)

    def takes_near(self):
        return (self.section() >= 2) & (self.z == self.section() - 1)

    def yields(self):
        return (self.y == 0) & (self.z >= 2) & (self.back().z == 0)

    def carries(self):
        return self.flip(y=1).yields()

    def carrier(self):
        return Spot(self.x, 1, self.section(), 0)

    def takes_carried(self):
        return (self.z == 0) & (self.section() >= 2)

    def crosses(self):
        return (self.z + self.c) % 2 == 1

    def drop(self):
        return Spot(self.x, self.y, 2 * ((self.y + self.z + self.c) % 2) + self.c, self.z // 2)

    def source(self):
        c = self.z % 2
        return Spot(self.x, self.y, 2 * self.c + (self.y + self.z // 2 + c) % 2, c)

    def part(self):
        return self.source().dp()


def same(one, other):
    return (one.dp() == other.dp()) & (one.section() == other.section())


def hail(spot):
    pl.semaphore_signal(pltpu.get_barrier_semaphore(), inc=1, device_id=spot.id(), device_id_type=MESH)


def hail_stagger(me, leading, by):
    waits = (me.z == leading) & (me.c == 1)
    tells = (me.z == leading + by) & (me.c == 0)
    pl.when(waits)(lambda: hail(Spot(me.x, me.y, me.z + by, 0)))
    pl.when(tells)(lambda: hail(Spot(me.x, me.y, me.z - by, 1)))
    return jnp.where(waits, 1, 0) + jnp.where(tells, 1, 0)


def tell_stagger(me, leading, by, token, m):
    @pl.when((me.z == leading + by) & (me.c == 0) & (m == 0))
    def _():
        pl.semaphore_signal(token, inc=1, device_id=Spot(me.x, me.y, me.z - by, 1).id(), device_id_type=MESH)


def wait_stagger(me, leading, token, m):
    @pl.when((me.z == leading) & (me.c == 1) & (m == 0))
    def _():
        pl.semaphore_wait(token, 1)


def hail_feeding(me, stage, core):
    gives = me.feeds(stage, core) & jnp.logical_not(same(me, me.fed_at(stage)))
    takes = (me.z == stage) & jnp.logical_not(same(me, me.feeder(core)))
    pl.when(gives)(lambda: hail(me.fed_at(stage)))
    pl.when(takes)(lambda: hail(me.feeder(core)))
    return jnp.where(gives, 1, 0) + jnp.where(takes, 1, 0)


def greet(line, turned, feeding=False):
    stage = line.stage()
    barrier = pltpu.get_barrier_semaphore()

    @pl.when(stage > 0)
    def _():
        pl.semaphore_signal(barrier, inc=1, device_id=line.beside(-1), device_id_type=MESH)

    @pl.when(stage < line.count - 1)
    def _():
        pl.semaphore_signal(barrier, inc=1, device_id=line.beside(1), device_id_type=MESH)

    expected = jnp.where(stage > 0, 1, 0) + jnp.where(stage < line.count - 1, 1, 0)
    if turned:
        me = Spot.here()
        alone = same(me, me.back())

        @pl.when(jnp.logical_not(alone))
        def _():
            hail(me.back())
            hail(me.ahead())

        expected = expected + jnp.where(alone, 0, 2)
        if feeding:
            expected = expected + hail_feeding(me, 0, 0) + hail_stagger(me, 0, 1)
        else:
            aside = me.yields() | me.carries()
            pl.when(aside)(lambda: hail(me.flip(y=1)))
            expected = expected + hail_stagger(me, line.count - 1, -1) + jnp.where(aside, 1, 0)
    pl.semaphore_wait(barrier, expected)


def forward_kernel(line, length, turned, x_first, x_in, words, wqkv_h, wproj_h, wup_h, wdown_h, small_in,
                   x_o, a_o, qkv_o, lse_o, o_o, h_o, a2_o, gp_o, u_o, acts_o, home_o,
                   wqkv, wproj, wup, wdown, xs, outs, a, qkv, lse, o, h, a2, gp, u, bias, ot, small,
                   w_sem, in_sem, x_sem, save_sem, act_sem, send_sem, recv_sem, home_sem, token):
    micro = xs.shape[0]
    stage = line.stage()
    loads = [
        pltpu.make_async_copy(src, dst, w_sem.at[i])
        for i, (src, dst) in enumerate(((wqkv_h, wqkv), (wproj_h, wproj), (wup_h, wup), (wdown_h, wdown)))
    ]
    loads[0].start()

    def first_in(m):
        return pltpu.make_async_copy(x_in.at[m], xs.at[m], in_sem.at[m])

    if turned:
        spread_small(small_in, small)
    else:
        small[...] = small_in[...]
    greet(line, turned, feeding=True)
    if turned:
        me = Spot.here()
        back = me.back()

        def turn_in(m):
            return pltpu.make_async_remote_copy(
                src_ref=x_in.at[m], dst_ref=xs.at[m], send_sem=in_sem.at[m], recv_sem=recv_sem.at[m],
                device_id=taker.id(), device_id_type=MESH)

        taker, feeder = me.fed_at(0), me.feeder(0)
        feeds = me.feeds(0, 0) & jnp.logical_not(same(me, taker))
        feeds_self = me.feeds(0, 0) & same(me, taker)
        homing, homed = me.gives_down(), me.takes_down()

        def home(m):
            return pltpu.make_async_remote_copy(
                src_ref=outs.at[m], dst_ref=home_o.at[m], send_sem=home_sem.at[0, m], recv_sem=home_sem.at[1, m],
                device_id=back.id(), device_id_type=MESH)

        @pl.when(stage == 0)
        def _():
            for m in range(FIRST):
                pltpu.make_async_copy(x_first.at[m], xs.at[m], in_sem.at[m]).start()

        for m in range(FIRST, micro):
            @pl.when(feeds)
            def _():
                turn_in(m).start()

            @pl.when(feeds_self)
            def _():
                first_in(m).start()
    else:
        @pl.when(stage == 0)
        def _():
            for m in range(micro):
                first_in(m).start()

    loads[0].wait()
    for load in loads[1:]:
        load.start()

    saved = ((a, a_o), (qkv, qkv_o), (lse, lse_o), (o, o_o), (h, h_o), (a2, a2_o), (gp, gp_o), (u, u_o))

    def saves(m, slot):
        return [
            pltpu.make_async_copy(here.at[slot], there.at[m], save_sem.at[slot, i])
            for i, (here, there) in enumerate(saved)
        ]

    def hop(m):
        return pltpu.make_async_remote_copy(
            src_ref=outs.at[m], dst_ref=xs.at[m], send_sem=send_sem.at[m], recv_sem=recv_sem.at[m],
            device_id=line.beside(1), device_id_type=MESH)

    def step(m, carry):
        slot = lax.rem(m, 2)

        if turned:
            here = jnp.logical_or(feeds_self, jnp.logical_and(stage == 0, m < FIRST))
        else:
            here = stage == 0

        @pl.when(here)
        def _():
            first_in(m).wait()

        @pl.when(jnp.logical_not(here))
        def _():
            hop(m).wait_recv()

        if turned:
            tell_stagger(me, 0, 1, token, m)
        pltpu.make_async_copy(xs.at[m], x_o.at[m], x_sem.at[m]).start()

        @pl.when(m >= 2)
        def _():
            for save in saves(m - 2, slot):
                save.wait()

        bias[...] = micro_bias(words, m, micro, length)

        def before(i):
            @pl.when(m == 0)
            def _():
                loads[i].wait()

        layer_forward(xs.at[m], bias, wqkv, wproj, wup, wdown, small, a.at[slot], qkv.at[slot],
                      lse.at[slot], o.at[slot], h.at[slot], a2.at[slot], gp.at[slot], u.at[slot],
                      outs.at[m], ot, before)

        if turned:
            wait_stagger(me, 0, token, m)

        @pl.when(stage < line.count - 1)
        def _():
            hop(m).start()

        for save in saves(m, slot):
            save.start()
        pltpu.make_async_copy(outs.at[m], acts_o.at[m], act_sem.at[m]).start()
        if turned:
            pl.when(homing & (m < EARLY))(lambda: home(m).start())
        return carry

    lax.fori_loop(0, micro, step, 0)

    for m in range(max(micro - 2, 0), micro):
        for save in saves(m, m % 2):
            save.wait()
    for m in range(micro):
        pltpu.make_async_copy(xs.at[m], x_o.at[m], x_sem.at[m]).wait()
        pltpu.make_async_copy(outs.at[m], acts_o.at[m], act_sem.at[m]).wait()

    @pl.when(stage < line.count - 1)
    def _():
        for m in range(micro):
            hop(m).wait_send()

    if turned:
        @pl.when(feeds)
        def _():
            for m in range(FIRST, micro):
                turn_in(m).wait_send()

        for m in range(EARLY):
            pl.when(homing)(lambda: home(m).wait_send())
            pl.when(homed)(lambda: home(m).wait_recv())


def backward_kernel(line, length, turned, acts_h, g_in, x_h, qkv_h, lse_h, h_h, gp_h, words,
                    wqkv_h, wproj_h, wup_h, wdown_h, small_in,
                    acts_o, home_o, side_o, g_o, dz_o, f_o, r_o, gin_o, sums_out,
                    wqkv, wproj, wup, wdown, gs, gins, x, qkv, lse, h, gp, dz, f, r, bias, do, dh, dqt, small, sums_o,
                    w_sem, in_sem, g_sem, load_sem, save_sem, act_sem, send_sem, recv_sem, home_sem, back_sem, side_sem, token):
    micro = gs.shape[0]
    stage = line.stage()
    loads = [
        pltpu.make_async_copy(src, dst, w_sem.at[i])
        for i, (src, dst) in enumerate(((wdown_h, wdown), (wup_h, wup), (wproj_h, wproj), (wqkv_h, wqkv)))
    ]

    def last_in(m):
        return pltpu.make_async_copy(g_in.at[m], gs.at[m], in_sem.at[m])

    @pl.when(stage == line.count - 1)
    def _():
        for m in range(micro):
            last_in(m).start()

    kept = ((gp_h, gp), (h_h, h), (qkv_h, qkv), (lse_h, lse), (x_h, x))

    def fetches(m, slot):
        return [
            pltpu.make_async_copy(there.at[m], here.at[slot], load_sem.at[slot, i])
            for i, (there, here) in enumerate(kept)
        ]

    loads[0].start()
    fetches(0, 0)[0].start()
    sums_o[...] = jnp.zeros_like(sums_o)
    if turned:
        spread_small(small_in, small)
    else:
        small[...] = small_in[...]
    greet(line, turned)
    if turned:
        me = Spot.here()
        back = me.back()
        alone = same(me, back)

        def home(m):
            return pltpu.make_async_remote_copy(
                src_ref=acts_h.at[m], dst_ref=acts_o.at[m], send_sem=home_sem.at[0, m], recv_sem=home_sem.at[1, m],
                device_id=back.id(), device_id_type=MESH)

        def stay(m):
            return pltpu.make_async_copy(acts_h.at[m], acts_o.at[m], home_sem.at[0, m])

        pairs = jnp.logical_not(alone)
        low, low_home = jnp.logical_not(me.gives_down()), jnp.logical_not(me.takes_down())

        def home_back(m):
            return pltpu.make_async_remote_copy(
                src_ref=gins.at[m], dst_ref=home_o.at[m], send_sem=back_sem.at[0, m], recv_sem=back_sem.at[1, m],
                device_id=back.id(), device_id_type=MESH)

        near, near_home = me.gives_near(), me.takes_near()

        def aside(m):
            return pltpu.make_async_remote_copy(
                src_ref=gins.at[m], dst_ref=side_o.at[m], send_sem=side_sem.at[0, m], recv_sem=side_sem.at[1, m],
                device_id=me.flip(y=1).id(), device_id_type=MESH)

        def settle_back(m):
            return pltpu.make_async_copy(gins.at[m], home_o.at[m], back_sem.at[0, m])

        for m in range(micro):
            now = low | (m >= EARLY)
            pl.when(alone & now)(lambda: stay(m).start())
            pl.when(pairs & now)(lambda: home(m).start())
    else:
        for m in range(micro):
            pltpu.make_async_copy(acts_h.at[m], acts_o.at[m], home_sem.at[0, m]).start()

    loads[0].wait()
    for load, some in zip(loads[1:], ((1,), (2, 3), (4,))):
        for i in some:
            fetches(0, 0)[i].start()
        load.start()
    saved = ((dz, dz_o), (f, f_o), (r, r_o))

    def saves(m, slot):
        return [
            pltpu.make_async_copy(here.at[slot], there.at[m], save_sem.at[slot, i])
            for i, (here, there) in enumerate(saved)
        ]

    def hop(m):
        return pltpu.make_async_remote_copy(
            src_ref=gins.at[m], dst_ref=gs.at[m], send_sem=send_sem.at[m], recv_sem=recv_sem.at[m],
            device_id=line.beside(-1), device_id_type=MESH)

    def step(m, carry):
        slot = lax.rem(m, 2)

        @pl.when(m + 1 < micro)
        def _():
            for fetch in fetches(m + 1, 1 - slot):
                fetch.start()

        def before(i):
            @pl.when(m == 0)
            def _():
                loads[i].wait()

            for at in ((), (1,), (2, 3), (4,))[i]:
                fetches(m, slot)[at].wait()

        fetches(m, slot)[0].wait()
        bias[...] = micro_bias(words, m, micro, length)

        @pl.when(m >= 2)
        def _():
            for save in saves(m - 2, slot):
                save.wait()

        @pl.when(stage == line.count - 1)
        def _():
            last_in(m).wait()

        @pl.when(stage < line.count - 1)
        def _():
            hop(m).wait_recv()

        if turned:
            tell_stagger(me, line.count - 1, -1, token, m)
        pltpu.make_async_copy(gs.at[m], g_o.at[m], g_sem.at[m]).start()
        layer_backward(gs.at[m], x.at[slot], bias, qkv.at[slot], lse.at[slot], h.at[slot], gp.at[slot],
                       wqkv, wproj, wup, wdown, small, dz.at[slot], f.at[slot], r.at[slot], gins.at[m],
                       sums_o, do, dh, dqt, before)

        if turned:
            wait_stagger(me, line.count - 1, token, m)

        @pl.when(stage > 0)
        def _():
            hop(m).start()

        for save in saves(m, slot):
            save.start()
        pltpu.make_async_copy(gins.at[m], gin_o.at[m], act_sem.at[m]).start()
        if turned:
            pl.when(pairs & low & (m < micro - 1))(lambda: home_back(m).start())
            pl.when(alone & low & (m < micro - 1))(lambda: settle_back(m).start())
            pl.when(me.yields())(lambda: aside(m).start())
        return carry

    lax.fori_loop(0, micro, step, 0)

    @pl.when(stage > 0)
    def _():
        for m in range(micro):
            hop(m).wait_send()

    if turned:
        @pl.when(near)
        def _():
            for m in range(micro):
                home_back(m).start()
    if turned:
        share_small(sums_o, sums_out)
    else:
        sums_out[...] = sums_o[...]

    for m in range(max(micro - 2, 0), micro):
        for save in saves(m, m % 2):
            save.wait()
    for m in range(micro):
        pltpu.make_async_copy(gs.at[m], g_o.at[m], g_sem.at[m]).wait()
        pltpu.make_async_copy(gins.at[m], gin_o.at[m], act_sem.at[m]).wait()

    for m in range(micro):
        if turned:
            pl.when(near)(lambda: home_back(m).wait_send())
            pl.when(near_home)(lambda: home_back(m).wait_recv())
            pl.when(me.yields())(lambda: aside(m).wait_send())
            pl.when(me.carries())(lambda: aside(m).wait_recv())
            now, then = low | (m >= EARLY), low_home | (m >= EARLY)
            pl.when(alone & now)(lambda: stay(m).wait())
            pl.when(pairs & now)(lambda: home(m).wait_send())
            pl.when(pairs & then)(lambda: home(m).wait_recv())
            if m < micro - 1:
                pl.when(pairs & low)(lambda: home_back(m).wait_send())
                pl.when(pairs & low_home)(lambda: home_back(m).wait_recv())
                pl.when(alone & low)(lambda: settle_back(m).wait())
        else:
            pltpu.make_async_copy(acts_h.at[m], acts_o.at[m], home_sem.at[0, m]).wait()


IN_VMEM = pl.BlockSpec(memory_space=pltpu.VMEM)
IN_SMEM = pl.BlockSpec(memory_space=pltpu.SMEM)
ANYWHERE = pl.BlockSpec(memory_space=pl.ANY)
DMA = pltpu.SemaphoreType.DMA


def run_forward(line, length, turned, x_first, x_in, words, weights, small):
    micro, rows, width = x_in.shape
    hidden = weights[2].shape[1]
    shape = jax.ShapeDtypeStruct
    saved = (
        ((rows, width), BF), ((rows, 3 * width), BF), ((16, rows), F32), ((rows, width), BF),
        ((rows, width), F32), ((rows, width), BF), ((rows, hidden), BF), ((rows, hidden), BF))
    many = shape((micro, rows, width), BF)
    return pl.pallas_call(
        functools.partial(forward_kernel, line, length, turned),
        out_shape=[many] + [shape((micro,) + s, t) for s, t in saved] + [many, many],
        in_specs=[ANYWHERE, ANYWHERE, IN_VMEM] + [ANYWHERE] * 4 + [IN_VMEM],
        out_specs=[ANYWHERE] * 11,
        scratch_shapes=[pltpu.VMEM(w.shape, BF) for w in weights]
        + [pltpu.VMEM((micro, rows, width), BF)] * 2
        + [pltpu.VMEM((2,) + s, t) for s, t in saved]
        + [pltpu.VMEM((rows, rows), F32), pltpu.VMEM((width, rows), BF), pltpu.VMEM((16, width), F32)]
        + [DMA((4,)), DMA((micro,)), DMA((micro,)), DMA((2, 8)), DMA((micro,)), DMA((micro,)), DMA((micro,)),
           DMA((2, micro)), pltpu.SemaphoreType.REGULAR],
        compiler_params=pltpu.CompilerParams(
            collective_id=0, has_side_effects=True, vmem_limit_bytes=VMEM_CAP),
        name="forward_line",
    )(x_first, x_in, words, *weights, small)


def run_backward(line, length, turned, acts, g_in, x, qkv, lse, h, gp, words, weights, small):
    micro, rows, width = g_in.shape
    hidden = weights[2].shape[1]
    shape = jax.ShapeDtypeStruct
    many = shape((micro, rows, width), BF)
    wqkv, wproj, wup, wdown = weights
    return pl.pallas_call(
        functools.partial(backward_kernel, line, length, turned),
        out_shape=[many, many, many, many, shape((micro, rows, hidden), BF), many, shape((micro, rows, 3 * width), BF), many,
                   shape(small.shape, F32)],
        in_specs=[ANYWHERE] * 7 + [IN_VMEM] + [ANYWHERE] * 4 + [IN_VMEM],
        out_specs=[ANYWHERE] * 8 + [IN_VMEM],
        scratch_shapes=[pltpu.VMEM(w.shape, BF) for w in weights]
        + [pltpu.VMEM((micro, rows, width), BF)] * 2
        + [pltpu.VMEM((2, rows, width), BF), pltpu.VMEM((2, rows, 3 * width), BF), pltpu.VMEM((2, 16, rows), F32),
           pltpu.VMEM((2, rows, width), F32), pltpu.VMEM((2, rows, hidden), BF),
           pltpu.VMEM((2, rows, hidden), BF), pltpu.VMEM((2, rows, width), BF), pltpu.VMEM((2, rows, 3 * width), BF),
           pltpu.VMEM((rows, rows), F32), pltpu.VMEM((rows, width), BF), pltpu.VMEM((rows, width), F32),
           pltpu.VMEM((width, rows), BF), pltpu.VMEM((16, width), F32), pltpu.VMEM((16, width), F32)]
        + [DMA((4,)), DMA((micro,)), DMA((micro,)), DMA((2, 5)), DMA((2, 3)), DMA((micro,)), DMA((micro,)),
           DMA((micro,)), DMA((2, micro)), DMA((2, micro)), DMA((2, micro)),
           pltpu.SemaphoreType.REGULAR],
        compiler_params=pltpu.CompilerParams(
            collective_id=1, has_side_effects=True, vmem_limit_bytes=VMEM_CAP),
        name="backward_line",
    )(acts, g_in, x, qkv, lse, h, gp, words, wqkv, wproj, wup, wdown, small)


GATHER_PIECES = ((0, 0, 48, "c"), (0, 48, 48, "x"), (4, 0, 16, "x"), (1, 0, 96, "c"), (2, 0, 48, "x"), (2, 48, 48, "c"),
                 (3, 0, 192, "x"), (3, 192, 192, "c"))


def gather_kernel(pieces, micro, *refs):
    count = 5
    masters, (x_in, g_in, seg_in, cls_in) = refs[:count], refs[count : count + 4]
    wholes, (x_o, x_all, g_o, seg_o) = refs[count + 4 : 2 * count + 4], refs[2 * count + 4 : 2 * count + 8]
    refs = refs[2 * count + 8 :]
    swap, wide, narrow, (x_raw, g_raw, x_pad, g_pad, words, table) = refs[:5], refs[5:9], refs[9:13], refs[13:19]
    send, recv, local, turn_send, turn_recv, load_sem = refs[19:]
    shares = narrow + (table,)
    loads = [pltpu.make_async_copy(masters[i], wide[i], load_sem.at[i]) for i in range(4)]
    loads += [pltpu.make_async_copy(x_in, x_raw, load_sem.at[4]), pltpu.make_async_copy(g_in, g_raw, load_sem.at[5])]
    for i in (0, 1, 2, 3, 4, 5):
        loads[i].start()
    me = Spot.here()
    xn, yn, cn = me.flip(x=1), me.flip(y=1), me.flip(c=1)
    target, source, ahead, back = me.drop(), me.source(), me.ahead(), me.back()
    stays, alone = same(me, target), same(me, back)
    moves, pairs = jnp.logical_not(stays), jnp.logical_not(alone)
    crosses = me.crosses()
    direct = jnp.logical_and(moves, jnp.logical_not(crosses))
    for spot in (xn, yn, cn):
        hail(spot)

    @pl.when(moves)
    def _():
        hail(target)
        hail(source)

    @pl.when(pairs)
    def _():
        hail(ahead)
        hail(back)

    fed = hail_feeding(me, 0, 0) + hail_feeding(me, 3, 1)
    expected = 3 + jnp.where(stays, 0, 2) + jnp.where(alone, 0, 2) + fed

    def rows(k, part):
        array, first, size, _ = pieces[k]
        share = shares[array].shape[0]
        return wholes[array].at[pl.ds(pl.multiple_of(part * share + first, 16), size)]

    def mine(k):
        array, first, size, _ = pieces[k]
        return shares[array].at[pl.ds(first, size)]

    def swapped(k):
        array, first, size, _ = pieces[k]
        return swap[array].at[pl.ds(first, size)]

    def remote(src, dst, kind, k, spot):
        return pltpu.make_async_remote_copy(
            src_ref=src, dst_ref=dst, send_sem=send.at[kind, k], recv_sem=recv.at[kind, k],
            device_id=spot.id(), device_id_type=MESH)

    def crossed(k):
        return remote(mine(k), swapped(k), 8, k, yn)

    def brought(k, part):
        return remote(mine(k), rows(k, part), 0, k, target)

    def brought_on(k, part):
        return remote(swapped(k), rows(k, part), 0, k, target)

    def kept(k):
        return pltpu.make_async_copy(mine(k), rows(k, me.dp()), local.at[k])

    def passed(kind, k, part, spot):
        return remote(rows(k, part), rows(k, part), kind, k, spot)

    def parts(spot):
        return [s.part() for s in (spot, spot.flip(x=1), spot.flip(y=1), spot.flip(x=1, y=1))]

    own, own_x, own_y, own_d = parts(me)
    beside = parts(cn)
    turns = [(words, seg_o)] + [(x_pad.at[m], x_o.at[m]) for m in range(FIRST)] + [(g_pad.at[m], g_o.at[m]) for m in range(micro)]
    gives = [me.z >= 0] + [me.feeds(0, 0)] * FIRST + [me.feeds(3, 1)] * micro
    takes = [me.z >= 0] + [me.z == 0] * FIRST + [me.z == 3] * micro
    takers = [ahead] + [me.fed_at(0)] * FIRST + [me.fed_at(3)] * micro
    givers = [back] + [me.feeder(0)] * FIRST + [me.feeder(1)] * micro

    def turn(i):
        return pltpu.make_async_remote_copy(
            src_ref=turns[i][0], dst_ref=turns[i][1], send_sem=turn_send.at[i], recv_sem=turn_recv.at[i],
            device_id=takers[i].id(), device_id_type=MESH)

    def turn_start(i):
        here = same(me, takers[i])
        pl.when(gives[i] & here)(lambda: pltpu.make_async_copy(*turns[i], turn_send.at[i]).start())
        pl.when(gives[i] & jnp.logical_not(here))(lambda: turn(i).start())

    def turn_end(i):
        here = same(me, takers[i])
        pl.when(gives[i] & here)(lambda: pltpu.make_async_copy(*turns[i], turn_send.at[i]).wait())
        pl.when(gives[i] & jnp.logical_not(here))(lambda: turn(i).wait_send())
        pl.when(takes[i] & jnp.logical_not(same(me, givers[i])))(lambda: turn(i).wait_recv())

    flat = masters[4][...].astype(BF).astype(F32)
    share = flat.shape[1] // 12
    table[...] = jnp.zeros_like(table)
    for i in range(8):
        table[i : i + 1, 0:share] = flat[:, i * share : (i + 1) * share]
    for i in range(share // 32):
        table[8 + i : 9 + i, :] = flat[:, 8 * share + 128 * i : 8 * share + 128 * (i + 1)]
    words[...] = jnp.full_like(words, -1)
    words[0:micro, 0 : seg_in.shape[1]] = seg_in[...]
    for m in range(micro):
        words[micro + m : micro + m + 1, :] = jnp.full((1, words.shape[1]), cls_in[m], jnp.int32)

    def pad(raw, padded):
        for m in range(micro):
            short = raw[m]
            rest = jnp.zeros((padded.shape[1] - short.shape[0], short.shape[1]), short.dtype)
            padded[m] = jnp.concatenate([short, rest], axis=0)

    ready = set()
    for k in range(len(pieces)):
        array = pieces[k][0]
        if array < 4 and array not in ready:
            ready.add(array)
            loads[array].wait()
            size = wide[array].shape[0]
            for first in range(0, size, 48):
                narrow[array][first : first + 48, :] = wide[array][first : first + 48, :].astype(BF)
        if k == 0:
            pl.semaphore_wait(pltpu.get_barrier_semaphore(), expected)
        pl.when(stays)(lambda: kept(k).start())
        pl.when(direct)(lambda: brought(k, me.dp()).start())
        pl.when(crosses)(lambda: crossed(k).start())
    turn_start(0)
    loads[4].wait()
    pad(x_raw, x_pad)
    for i in range(FIRST):
        turn_start(1 + i)
    x_save = pltpu.make_async_copy(x_pad, x_all, load_sem.at[4])
    x_save.start()
    loads[5].wait()
    pad(g_raw, g_pad)
    for k in range(len(pieces) + 3):
        if k < len(pieces):
            @pl.when(crosses)
            def _():
                crossed(k).wait_recv()
                brought_on(k, me.dp()).start()

        if k == len(pieces) - 1:
            for i in range(1 + FIRST, 1 + FIRST + micro):
                turn_start(i)
        b = k - 1
        if 0 <= b < len(pieces):
            pl.when(stays)(lambda: kept(b).wait())
            pl.when(moves)(lambda: brought(b, own).wait_recv())
            passed(1, b, own, xn).start()
            passed(2, b, own, yn).start()
            passed(4, b, own, cn).start()
        b = k - 2
        if 0 <= b < len(pieces):
            turn_x = (me.c == 0) if pieces[b][3] == "c" else (me.c < 0)
            passed(1, b, own_x, xn).wait_recv()
            pl.when(turn_x)(lambda: passed(3, b, own_x, yn).start())
            passed(5, b, own_x, cn).start()
            passed(2, b, own_y, yn).wait_recv()
            pl.when(jnp.logical_not(turn_x))(lambda: passed(3, b, own_y, xn).start())
            passed(6, b, own_y, cn).start()
        b = k - 3
        if 0 <= b < len(pieces):
            passed(3, b, own_d, yn).wait_recv()
            passed(7, b, own_d, cn).start()
    for k in range(len(pieces)):
        for kind in range(4, 8):
            passed(kind, k, beside[kind - 4], cn).wait_recv()
        pl.when(moves)(lambda: brought(k, own).wait_send())
        pl.when(crosses)(lambda: crossed(k).wait_send())
        for kind in range(1, 8):
            passed(kind, k, own, cn).wait_send()
    for i in range(len(turns)):
        turn_end(i)
    x_save.wait()


def run_gather(masters, inputs, g, segs, classes, rows):
    pieces = GATHER_PIECES
    micro, _, width = g.shape
    shape = jax.ShapeDtypeStruct
    shares = [shape(m.shape, BF) for m in masters[:4]] + [shape((16, 128), F32)]
    many = shape((micro, rows, width), BF)
    outs = [shape((s.shape[0] * 8,) + s.shape[1:], s.dtype) for s in shares]
    outs += [shape((FIRST, rows, width), BF), many, many, shape((2 * micro, rows), segs.dtype)]
    return pl.pallas_call(
        functools.partial(gather_kernel, pieces, micro),
        out_shape=outs,
        in_specs=[ANYWHERE] * 4 + [IN_VMEM] + [ANYWHERE] * 2 + [IN_VMEM, IN_SMEM],
        out_specs=[ANYWHERE] * 9,
        scratch_shapes=[pltpu.VMEM(s.shape, s.dtype) for s in shares] + [pltpu.VMEM(m.shape, F32) for m in masters[:4]]
        + [pltpu.VMEM(s.shape, BF) for s in shares[:4]] + [pltpu.VMEM(g.shape, BF)] * 2
        + [pltpu.VMEM((micro, rows, width), BF)] * 2
        + [pltpu.VMEM((2 * micro, rows), segs.dtype), pltpu.VMEM((16, 128), F32)]
        + [DMA((9, len(pieces))), DMA((9, len(pieces))), DMA((len(pieces),)), DMA((1 + FIRST + micro,)),
           DMA((1 + FIRST + micro,)), DMA((6,))],
        compiler_params=pltpu.CompilerParams(collective_id=2, has_side_effects=True, vmem_limit_bytes=VMEM_CAP),
        name="gather_layers",
    )(*masters, inputs, g, segs, classes)


SCATTER_PIECES = ((3, 0, 128, 0, 768, "x"), (3, 128, 128, 0, 768, "c"), (3, 256, 128, 0, 768, "x"),
                  (2, 0, 96, 0, 1024, "c"), (2, 0, 96, 1024, 1024, "x"), (2, 0, 96, 2048, 1024, "c"),
                  (0, 0, 96, 0, 768, "x"), (0, 0, 96, 768, 768, "c"), (0, 0, 96, 1536, 768, "x"),
                  (1, 0, 96, 0, 768, "c"), (4, 0, 16, 0, 128, "x"))


SCATTER_LAGS = (1, 3, 4, 5)


def scatter_kernel(pieces, micro, *refs):
    count = 5
    a_h, r_h, o_h, f_h, a2_h, dz_h, u_h, g_h, small_h, gin_in, side_in = refs[:11]
    outs, gin_o, norm_o = refs[11:16], refs[16], refs[17]
    at = 18
    totals, beside, diag, from_x, from_y, done, swap, home = (refs[at + i * count : at + (i + 1) * count] for i in range(8))
    (stream, fixed, flipped, sums, tallies, stream_sem, fixed_sem, send, recv, local, turn_sem, note_send, note_recv,
     out_sem) = refs[at + 8 * count :]
    me = Spot.here()
    xn, yn, cn = me.flip(x=1), me.flip(y=1), me.flip(c=1)
    target, giver, back, ahead = me.source(), me.drop(), me.back(), me.ahead()
    stays, alone = same(me, target), same(me, back)
    moves, pairs = jnp.logical_not(stays), jnp.logical_not(alone)
    crosses, target_crosses = me.crosses(), target.crosses()
    slab = [me.flip(x=i & 1, y=(i >> 1) & 1, c=i >> 2) for i in range(1, 8)]
    column = [Spot(me.x, me.y, (me.z + i) % 4, me.c) for i in range(1, 4)]
    left_right = {0: (a_h, r_h), 1: (o_h, f_h), 2: (a2_h, dz_h), 3: (u_h, g_h)}
    resting = (g_h, a2_h, a_h, o_h)
    rest_at = {3: 0, 2: 1, 0: 2, 1: 3}

    openers = {}
    for k in reversed(range(len(pieces))):
        openers[pieces[k][0]] = k
    opened = sorted((k, array) for array, k in openers.items() if array < 4)

    def streamed(k):
        array, first, size, column_at, columns, _ = pieces[k]
        slot = k % 2
        if array == 3:
            share = totals[3].shape[0] // 8
            return [pltpu.make_async_copy(u_h.at[:, pl.ds(p * share + first, size)],
                                          stream.at[slot, :, pl.ds(p * size, size)], stream_sem.at[slot, p])
                    for p in range(8)]
        if array == 4:
            return [pltpu.make_async_copy(small_h, totals[4], stream_sem.at[slot, 0])]
        return [pltpu.make_async_copy(left_right[array][1].at[:, pl.ds(column_at, columns)],
                                      stream.at[slot, :, pl.ds(0, columns)], stream_sem.at[slot, 0])]

    def rested(i):
        return pltpu.make_async_copy(resting[i], fixed.at[i], fixed_sem.at[i])

    for copy in streamed(0):
        copy.start()
    rested(rest_at[opened[0][1]]).start()
    for copy in streamed(1):
        copy.start()
    for _, array in opened[1:]:
        rested(rest_at[array]).start()
    for spot in slab + column:
        hail(spot)

    @pl.when(moves)
    def _():
        hail(target)
        hail(giver)

    @pl.when(pairs)
    def _():
        hail(back)
        hail(ahead)

    carried_to = Spot(me.x, 1, 0, me.z % 2)
    pl.when(me.carries())(lambda: hail(carried_to))
    pl.when(me.takes_carried())(lambda: hail(me.carrier()))

    def work(k):
        array, first, size, column_at, columns, _ = pieces[k]
        slot = k % 2
        for copy in streamed(k):
            copy.wait()
        if array == 4:
            pass
        elif array == 3:
            if k == openers[3]:
                rested(rest_at[3]).wait()
            share = totals[3].shape[0] // 8
            for p in range(0, 8, 2):
                both = lax.dot_general(stream[slot, :, p * size : (p + 2) * size], fixed[rest_at[3]], TN,
                                       preferred_element_type=F32).astype(BF)
                for i in range(2):
                    totals[3][(p + i) * share + first : (p + i) * share + first + size, :] = both[i * size : (i + 1) * size]
        else:
            if k == openers[array]:
                rested(rest_at[array]).wait()
                flipped[...] = fixed[rest_at[array]].T
            for c in range(0, columns, 256):
                totals[array][:, column_at + c : column_at + c + 256] = mm(flipped[...], stream[slot, :, c : c + 256]).astype(BF)
        if k + 2 < len(pieces):
            for copy in streamed(k + 2):
                copy.start()

    def parts(spot):
        return [s.part() for s in (spot, spot.flip(x=1), spot.flip(y=1), spot.flip(x=1, y=1))]

    kept, given = parts(me), parts(cn)

    def box(k):
        _, first, size, column_at, columns, _ = pieces[k]
        return pl.ds(first, size), pl.ds(column_at, columns)

    def whole(k, part):
        array, first, size, column_at, columns, _ = pieces[k]
        share = done[array].shape[0]
        return totals[array].at[pl.ds(pl.multiple_of(part * share + first, 16), size), pl.ds(column_at, columns)]

    def remote(src, dst, kind, k, spot):
        return pltpu.make_async_remote_copy(
            src_ref=src, dst_ref=dst, send_sem=send.at[kind, k], recv_sem=recv.at[kind, k],
            device_id=spot.id(), device_id_type=MESH)

    def of(refs_, k):
        return refs_[pieces[k][0]].at[box(k)]

    def crossed(k, j):
        return remote(whole(k, given[j]), beside[pieces[k][0]].at[(j,) + box(k)], j, k, cn)

    def to_diag(k, spot):
        return remote(whole(k, kept[3]), of(diag, k), 4, k, spot)

    def to_x(k):
        return remote(whole(k, kept[1]), of(from_x, k), 5, k, xn)

    def to_y(k):
        return remote(whole(k, kept[2]), of(from_y, k), 6, k, yn)

    def to_home(k):
        return remote(of(done, k), of(home, k), 7, k, target)

    def to_swap(k):
        return remote(of(done, k), of(swap, k), 7, k, target)

    def stay_home(k):
        return pltpu.make_async_copy(of(done, k), of(home, k), local.at[k])

    def over(k):
        return remote(of(swap, k), of(home, k), 8, k, yn)

    def add(k, j, extra):
        here = whole(k, kept[j])
        here[...] = (here[...].astype(F32) + extra.astype(F32)).astype(here.dtype)

    def turn(m):
        return pltpu.make_async_remote_copy(
            src_ref=gin_in.at[m], dst_ref=gin_o.at[m], send_sem=turn_sem.at[0, m], recv_sem=turn_sem.at[1, m],
            device_id=back.id(), device_id_type=MESH)

    def carry(m):
        return pltpu.make_async_remote_copy(
            src_ref=side_in.at[m], dst_ref=gin_o.at[m], send_sem=turn_sem.at[2, m], recv_sem=turn_sem.at[1, m],
            device_id=carried_to.id(), device_id_type=MESH)

    gives_now = me.gives_down() & jnp.logical_not(me.gives_near() | me.yields())
    takes_now = me.takes_down() & jnp.logical_not(me.takes_near())

    def turn_stay(m):
        return pltpu.make_async_copy(gin_in.at[m], gin_o.at[m], turn_sem.at[0, m])

    work(0)
    pl.semaphore_wait(pltpu.get_barrier_semaphore(), 10 + jnp.where(stays, 0, 2) + jnp.where(alone, 0, 2)
                      + jnp.where(me.carries(), 1, 0) + jnp.where(me.takes_carried(), 1, 0))
    for m in range(micro):
        now = gives_now | (m == micro - 1) & jnp.logical_not(me.gives_down())
        pl.when(alone & now)(lambda: turn_stay(m).start())
        pl.when(pairs & now)(lambda: turn(m).start())
        pl.when(me.carries())(lambda: carry(m).start())
    tally = jnp.zeros((8, 128), F32)
    for k in range(len(pieces) + SCATTER_LAGS[3]):
        if k < len(pieces):
            if k > 0:
                work(k)
            for j in (3, 2, 1, 0):
                crossed(k, j).start()
        b = k - SCATTER_LAGS[0]
        if 0 <= b < len(pieces):
            turn_x = (me.c == 0) if pieces[b][5] == "c" else (me.c < 0)
            for j in (3, 2, 1, 0):
                crossed(b, j).wait_recv()
                add(b, j, beside[pieces[b][0]][(j,) + box(b)])
                if j == 3:
                    pl.when(turn_x)(lambda: to_diag(b, yn).start())
                    pl.when(jnp.logical_not(turn_x))(lambda: to_diag(b, xn).start())
                if j == 2:
                    pl.when(turn_x)(lambda: to_y(b).start())
                if j == 1:
                    pl.when(jnp.logical_not(turn_x))(lambda: to_x(b).start())
        b = k - SCATTER_LAGS[1]
        if 0 <= b < len(pieces):
            to_diag(b, yn).wait_recv()
            turn_x = (me.c == 0) if pieces[b][5] == "c" else (me.c < 0)

            @pl.when(turn_x)
            def _():
                add(b, 1, of(diag, b)[...])
                to_x(b).start()

            @pl.when(jnp.logical_not(turn_x))
            def _():
                add(b, 2, of(diag, b)[...])
                to_y(b).start()
        b = k - SCATTER_LAGS[2]
        if 0 <= b < len(pieces):
            to_x(b).wait_recv()
            to_y(b).wait_recv()
            total = (whole(b, kept[0])[...].astype(F32) + of(from_x, b)[...].astype(F32) + of(from_y, b)[...].astype(F32))
            total = total.astype(done[pieces[b][0]].dtype)
            done[pieces[b][0]][box(b)] = total
            square = total.astype(F32) * total.astype(F32)
            for c in range(0, square.shape[1], 128):
                tally = tally + jnp.sum(square[:, c : c + 128].reshape(-1, 8, 128), axis=0)
            pl.when(stays)(lambda: stay_home(b).start())
            pl.when(moves & jnp.logical_not(target_crosses))(lambda: to_home(b).start())
            pl.when(target_crosses)(lambda: to_swap(b).start())
        b = k - SCATTER_LAGS[3]
        if 0 <= b < len(pieces):
            @pl.when(crosses)
            def _():
                to_swap(b).wait_recv()
                over(b).start()
    sums[0] = tally

    def note(i, src, slot, spot):
        return pltpu.make_async_remote_copy(
            src_ref=src, dst_ref=tallies.at[slot], send_sem=note_send.at[i], recv_sem=note_recv.at[slot],
            device_id=spot.id(), device_id_type=MESH)

    for i, spot in enumerate(column):
        note(i, sums.at[0], i, spot).start()
    for i, spot in enumerate(column):
        note(i, sums.at[0], i, spot).wait_recv()
        tally = tally + tallies[i]
    sums[1] = tally
    for i, spot in enumerate(slab):
        note(3 + i, sums.at[1], 3 + i, spot).start()
    for i, spot in enumerate(slab):
        note(3 + i, sums.at[1], 3 + i, spot).wait_recv()
        tally = tally + tallies[3 + i]
    whole_norm = jnp.sqrt(jnp.sum(jnp.sum(tally, axis=0, keepdims=True), axis=1, keepdims=True))
    norm_o[...] = jnp.broadcast_to(whole_norm, norm_o.shape)
    last = {}
    for k in range(len(pieces)):
        last[pieces[k][0]] = k
    for k in range(len(pieces)):
        pl.when(stays)(lambda: stay_home(k).wait())
        pl.when(moves & jnp.logical_not(crosses))(lambda: to_home(k).wait_recv())
        pl.when(crosses)(lambda: over(k).wait_recv())
        array = pieces[k][0]
        if last[array] == k:
            pltpu.make_async_copy(home[array], outs[array], out_sem.at[array]).start()
    for i, spot in enumerate(column):
        note(i, sums.at[0], i, spot).wait_send()
    for i, spot in enumerate(slab):
        note(3 + i, sums.at[1], 3 + i, spot).wait_send()
    for k in range(len(pieces)):
        for j in range(4):
            crossed(k, j).wait_send()
        to_diag(k, yn).wait_send()
        to_x(k).wait_send()
        to_y(k).wait_send()
        pl.when(moves)(lambda: to_home(k).wait_send())
        pl.when(crosses)(lambda: over(k).wait_send())
    for m in range(micro):
        last_one = m == micro - 1
        now = gives_now | last_one & jnp.logical_not(me.gives_down())
        then = takes_now | last_one & jnp.logical_not(me.takes_down())
        pl.when(me.carries())(lambda: carry(m).wait_send())
        pl.when(alone & now)(lambda: turn_stay(m).wait())
        pl.when(pairs & now)(lambda: turn(m).wait_send())
        pl.when(pairs & then)(lambda: turn(m).wait_recv())
    for array in range(count):
        pltpu.make_async_copy(home[array], outs[array], out_sem.at[array]).wait()


def run_scatter(operands, small, gin, side):
    pieces = SCATTER_PIECES
    micro = gin.shape[0]
    shape = jax.ShapeDtypeStruct
    a, r, o, f, a2, dz, u, g = operands = [v.reshape(-1, v.shape[-1]) for v in operands]
    rows = a.shape[0]
    sizes = [((left.shape[1], right.shape[1]), BF) for left, right in ((a, r), (o, f), (a2, dz), (u, g))]
    sizes.append((small.shape, F32))
    shares = [((s[0] // 8, s[1]), t) for s, t in sizes]
    one = [pltpu.VMEM(s, t) for s, t in shares]
    return pl.pallas_call(
        functools.partial(scatter_kernel, pieces, micro),
        out_shape=[shape(s, t) for s, t in shares] + [shape(gin.shape, gin.dtype), shape((8, 128), F32)],
        in_specs=[ANYWHERE] * 11,
        out_specs=[ANYWHERE] * 6 + [IN_VMEM],
        scratch_shapes=[pltpu.VMEM(s, t) for s, t in sizes] + [pltpu.VMEM((4,) + s, t) for s, t in shares] + one * 6
        + [pltpu.VMEM((2, rows, 1024), BF), pltpu.VMEM((4, rows, a.shape[1]), BF), pltpu.VMEM((a.shape[1], rows), BF),
           pltpu.VMEM((2, 8, 128), F32), pltpu.VMEM((10, 8, 128), F32), DMA((2, 8)), DMA((4,)),
           DMA((9, len(pieces))), DMA((9, len(pieces))), DMA((len(pieces),)), DMA((3, micro)), DMA((10,)), DMA((10,)),
           DMA((5,))],
        compiler_params=pltpu.CompilerParams(collective_id=3, has_side_effects=True, vmem_limit_bytes=VMEM_CAP),
        name="scatter_layers",
    )(*operands, small, gin, side)


def finish_kernel(order, micro, norm, *refs):
    table, small_state, refs = refs[0], refs[1:4], refs[4:]
    shards_h, state_h, (acts_early, acts_late, gin_early, gin_late) = refs[:4], refs[4:16], refs[16:20]
    norm_o, small_o, refs = refs[20], refs[21:25], refs[5:]
    state_o, acts_o, gin_o = refs[20:36], refs[36], refs[37]
    shards, state, (acts, gin, acts_cut, gin_cut, row) = refs[38:42], refs[42:58], refs[58:63]
    load_sem, pick_sem, out_sem = refs[63:]
    me = Spot.here()
    upper, near = me.takes_down(), me.takes_near()

    def loads(array):
        copies = [pltpu.make_async_copy(shards_h[array], shards[array], load_sem.at[array, 0])]
        for i in range(3):
            copies.append(pltpu.make_async_copy(state_h[4 * i + array], state[4 * (i + 1) + array], load_sem.at[array, 1 + i]))
        return copies

    def pick(i, m, src, dst):
        return pltpu.make_async_copy(src.at[m], dst.at[m], pick_sem.at[i, m])

    def saves(array):
        return [pltpu.make_async_copy(state[4 * i + array], state_o[4 * array + i], out_sem.at[array, i]) for i in range(4)]

    for array in order[:2]:
        for copy in loads(array):
            copy.start()

    def picks():
        for m in range(micro):
            from_early = (upper & (m < EARLY), jnp.logical_not(upper) & (m < micro - 1) | near)
            for i, (early, late, dst) in enumerate(((acts_early, acts_late, acts), (gin_early, gin_late, gin))):
                pl.when(from_early[i])(lambda: pick(i, m, early, dst).start())
                pl.when(jnp.logical_not(from_early[i]))(lambda: pick(i, m, late, dst).start())

    factor = 1.0 / jnp.maximum(norm[0:1, 0:1], 1.0)
    fix = 1.0 / (1.0 - 0.5**STEP)
    strip = 16
    norm_o[0] = norm[0, 0]
    share = row.shape[1] // 12
    for i in range(8):
        row[:, i * share : (i + 1) * share] = table[i : i + 1, 0:share]
    for i in range(share // 32):
        row[:, 8 * share + 128 * i : 8 * share + 128 * (i + 1)] = table[8 + i : 9 + i, :]
    grad = row[...] * factor
    first_new = 0.5 * small_state[1][...] + 0.5 * grad
    second_new = 0.5 * small_state[2][...] + 0.5 * grad * grad
    small_o[0][...] = grad
    small_o[1][...] = small_state[0][...] - small_rate * ((first_new * fix) / (jnp.sqrt(second_new * fix) + adam_eps))
    small_o[2][...] = first_new
    small_o[3][...] = second_new
    for at, array in enumerate(order):
        for copy in loads(array):
            copy.wait()
        if at + 2 < len(order):
            for copy in loads(order[at + 2]):
                copy.start()
        elif at + 2 == len(order):
            picks()
        grads, master, first, second = state[array], state[4 + array], state[8 + array], state[12 + array]

        def update(i, carry):
            rows = pl.ds(pl.multiple_of(i * strip, strip), strip)
            grad = shards[array][rows, :].astype(F32) * factor
            first_new = 0.5 * first[rows, :] + 0.5 * grad
            second_new = 0.5 * second[rows, :] + 0.5 * grad * grad
            old = master[rows, :]
            change = (first_new * fix) / (jnp.sqrt(second_new * fix) + adam_eps) + decay_rate * old
            grads[rows, :] = grad
            first[rows, :] = first_new
            second[rows, :] = second_new
            master[rows, :] = old - learn_rate * change
            return carry

        lax.fori_loop(0, grads.shape[0] // strip, update, 0)
        for copy in saves(array):
            copy.start()
    length = acts_cut.shape[1]
    for i, (src, cut, out) in enumerate(((acts, acts_cut, acts_o), (gin, gin_cut, gin_o))):
        for m in range(micro):
            pick(i, m, gin_late, src).wait()
            cut[m] = src[m, 0:length, :]
        pltpu.make_async_copy(cut, out, out_sem.at[4, i]).start()
    for array in order:
        for copy in saves(array):
            copy.wait()
    for i, (cut, out) in enumerate(((acts_cut, acts_o), (gin_cut, gin_o))):
        pltpu.make_async_copy(cut, out, out_sem.at[4, i]).wait()


def run_finish(norm, table, small_states, shards, states, tall, length):
    micro, rows, width = tall[0].shape
    shape = jax.ShapeDtypeStruct
    return pl.pallas_call(
        functools.partial(finish_kernel, (1, 0, 2, 3), micro),
        out_shape=[shape((1,), F32)] + [shape(small_states[0].shape, F32)] * 4
        + [shape(s.shape, F32) for s in shards for _ in range(4)] + [shape((micro, length, width), BF)] * 2,
        in_specs=[IN_VMEM] * 5 + [ANYWHERE] * 20,
        out_specs=[IN_SMEM] + [IN_VMEM] * 4 + [ANYWHERE] * 18,
        scratch_shapes=[pltpu.VMEM(s.shape, BF) for s in shards]
        + [pltpu.VMEM(s.shape, F32) for _ in range(4) for s in shards]
        + [pltpu.VMEM((micro, rows, width), BF)] * 2 + [pltpu.VMEM((micro, length, width), BF)] * 2
        + [pltpu.VMEM(small_states[0].shape, F32)] + [DMA((4, 4)), DMA((2, micro)), DMA((5, 4))],
        compiler_params=pltpu.CompilerParams(vmem_limit_bytes=VMEM_CAP),
        name="finish",
    )(norm, table, *small_states, *shards, *states, *tall)


def split_small(small, width, slices):
    share = width // slices
    stacked = small.reshape(slices, small.shape[0] // slices)
    eight = stacked[:, : 8 * share].reshape(slices, 8, share).transpose(1, 0, 2).reshape(8, width)
    up = stacked[:, 8 * share :].reshape(-1, width)
    return jnp.concatenate([eight, up, jnp.zeros((16 - 8 - up.shape[0], width), small.dtype)], axis=0)


def join_small(table, total, slices):
    width = table.shape[1]
    share = width // slices
    ups = total // width - 8
    eight = table[:8].reshape(8, slices, share).transpose(1, 0, 2).reshape(slices, 8 * share)
    up = table[8 : 8 + ups].reshape(slices, -1)
    return jnp.concatenate([eight, up], axis=1).reshape(-1)


def weight_grad(left, right):
    rows = left.shape[0] * left.shape[1]
    return lax.dot_general(left.reshape(rows, -1), right.reshape(rows, -1), (((0,), (0,)), ((), ())),
                           preferred_element_type=F32)


def adam(grad, master, first, second, rate, decay):
    fix = 1.0 - 0.5**STEP
    first = 0.5 * first + 0.5 * grad
    second = 0.5 * second + 0.5 * grad * grad
    update = first / fix / (jnp.sqrt(second / fix) + adam_eps)
    if decay:
        update = update + decay * master
    return [grad, master - rate * update, first, second]


def per_device(inputs, out_grad, segment_ids, cls_index, *states):
    masters, firsts, seconds = states[0:5], states[5:10], states[10:15]
    slices = lax.axis_size("dp")
    stages = lax.axis_size("section")
    turned = slices == 8 and stages == 4
    seq_dev, length, width = inputs.shape
    rows = -(-length // 128) * 128
    share = masters[4].shape[1]
    total = share * slices

    if turned:
        line = Line("dp", 4, 2)
        *weights, small, x_first, x_in, g_in, words = run_gather(
            [m[0] for m in masters[:4]] + [masters[4]], inputs, out_grad, segment_ids, cls_index, rows)
    else:
        line = Line("section", stages, 1)
        extra = ((0, 0), (0, rows - length), (0, 0))
        x_in, g_in = jnp.pad(inputs, extra), jnp.pad(out_grad, extra)
        segs = jnp.pad(segment_ids, ((0, 0), (0, rows - length)), constant_values=-1)
        words = jnp.concatenate([segs, jnp.broadcast_to(cls_index[:, None], (seq_dev, rows))], axis=0)
        gathered = [lax.all_gather(m[0].astype(BF), "dp", axis=0, tiled=True) for m in masters]
        weights, x_first = gathered[:4], x_in[0]
        small = split_small(gathered[4].astype(F32), width, slices)

    x, a, qkv, lse, o, h, a2, gp, u, acts, acts_early = run_forward(
        line, length, turned, x_first, x_in, words, weights, small)
    acts, gin_early, side, g, dz, f, r, gin, sums = run_backward(
        line, length, turned, acts, g_in, x, qkv, lse, h, gp, words, weights, small)
    results = []
    if turned:
        matrix_states = [v[0] for group in (masters, firsts, seconds) for v in group[:4]]
        *shards, table, gin, norm = run_scatter([a, r, o, f, a2, dz, u, g], sums, gin, side)
        grad_norm, *rest = run_finish(norm, table, [masters[4], firsts[4], seconds[4]], shards, matrix_states,
                                      [acts_early, acts, gin_early, gin], length)
        acts, gin = rest[20:]
        results = [v[None] for v in rest[4:20]] + rest[:4]
    else:
        acts, gin = acts[:, :length], gin[:, :length]
        totals = [weight_grad(a, r).astype(BF), weight_grad(o, f).astype(BF), weight_grad(a2, dz).astype(BF),
                  weight_grad(u, g).astype(BF), join_small(sums, total, slices)]
        shards = [lax.psum_scatter(t[None], "dp", scatter_dimension=1, tiled=True).astype(F32) for t in totals]
        squares = jnp.sum(jnp.stack([jnp.sum(s * s) for s in shards]))
        grad_norm = jnp.sqrt(lax.psum(squares, ("dp", "section")))
        factor = 1.0 / jnp.maximum(grad_norm, 1.0)
        for kind in range(5):
            rate, decay = (learn_rate, decay_rate) if kind < 4 else (small_rate, 0.0)
            results += adam(shards[kind] * factor, masters[kind], firsts[kind], seconds[kind], rate, decay)
    return (acts[None], gin[None], grad_norm.reshape(1)) + tuple(results)


def solution(mesh):
    matrix, vector = P("section", "dp", None), P("section", "dp")
    states = (matrix,) * 4 + (vector,)
    return jax.shard_map(
        per_device,
        mesh=mesh,
        in_specs=(P("dp", None, None), P("dp", None, None), P("dp", None), P("dp")) + states * 3,
        out_specs=(P("section", "dp", None, None), P("section", "dp", None, None), P())
        + (matrix,) * 16 + (vector,) * 4,
        check_vma=False,
    )
```
